128 devices in a mesh: row: 8 (over z, core), col: 16 (over y, x).
Axes of the slice: x: 4, y: 4, z: 4, core: 2. Of those that a mesh axis runs over, the one named last changes fastest.
Arguments:
- ancestor_inverse: bfloat16 [16384, 16384], P('col', 'row'), may hold values from -6 to 6
- level_one_panels: bfloat16 [2048, 16384], P('col', 'row'), may hold values from -0.046875 to 0.046875
- level_one_pattern: int32 [16, 128], P('col', 'row'), may hold values 0 or 1
- level_one_diag: float32 [2048, 128], replicated, may hold values from -6 to 6
- level_two_panels: bfloat16 [2048, 16384], P('col', 'row'), may hold values from -0.046875 to 0.046875
- level_two_pattern: int32 [16, 128], P('col', 'row'), may hold values 0 or 1
- parent_lead: bfloat16 [2048, 128], P('col'), may hold values from -0.5 to 0.5
- level_two_diag: float32 [2048, 128], P('col'), may hold values from -6 to 6
- parents: int32 [16], P('col'), may hold values from 0 to 15
Outputs:
- level_one_rows: bfloat16 [2048, 16384], P('col', 'row')
- level_one_inv: float32 [2048, 128], P('col')
- level_two_rows: bfloat16 [2048, 16384], P('col', 'row')
- level_two_lead: float32 [2048, 128], P('col')
- level_two_inv: float32 [2048, 128], P('col')
The draws below stay inside these ranges and needn't reach their ends.
Inputs may be any that keep to these rules, and one draw needn't show every extreme that they name: `parents`: each entry names a first-level supernode, 0 to 15.
All inputs are finite; a program needn't handle non-finite values. No bound on the sum of `level_one_pattern` or of `level_two_pattern` on one device may be relied on, other than what follows from the above.
Results may differ from the reference program's by a relative error of at most 0.008.
Values may be sent and summed in bfloat16 or wider, within the bound.
No kernel may reach another device: no remote copies, remote signals or barrier semaphores. Data moves between devices by JAX's collectives and lax.ppermute only.
A program may use at most 192 MiB of HBM per device.

```python
import jax
import jax.numpy as jnp
from jax import lax

B = 128
NA = 128
NK = 16
NM = 16


def set_ends(drawn, rng, low, top_value):
    index_at = [jax.random.randint(jax.random.fold_in(rng, axis), (), 0, length) for axis, length in enumerate(drawn.shape)]
    longest = drawn.shape.index(max(drawn.shape))
    neighbour = index_at[:longest] + [(index_at[longest] + 1) % drawn.shape[longest]] + index_at[longest + 1:]
    return drawn.at[tuple(index_at)].set(low).at[tuple(neighbour)].set(top_value)


def block_scale(stream_key, shape, cuts, least, top_value):
    factor_of = 1.0
    for position, parts in cuts:
        steps = jax.random.uniform(jax.random.fold_in(jax.random.fold_in(stream_key, 6), position), (parts,), jnp.float32, least / len(cuts), top_value / len(cuts))
        factor_of = factor_of * jnp.repeat(jnp.exp(steps), shape[position] // parts).reshape((-1,) + (1,) * (len(shape) - 1 - position))
    return factor_of


def normal_values(key, shape, scale, limit, pieces=(), kind=jnp.bfloat16):
    gain = block_scale(key, shape, pieces, -0.22, 0.18) if pieces else 1.0
    values = jax.random.normal(key, shape, jnp.float32) * scale * gain
    return jnp.minimum(jnp.maximum(values, -limit), limit).astype(kind)


def setup_inputs(seed: int = 0) -> dict:
    key_of = jax.random.split(jax.random.key(seed), 10)
    ancestor_inverse = normal_values(key_of[0], (NA * B, NA * B), 1.0, 6.0, ((0, 16), (1, 8)))
    level_one_panels = normal_values(key_of[1], (NK * B, NA * B), (NA * B) ** -0.5, 0.046875, ((0, 16), (1, 8)))
    level_one_pattern = set_ends((jax.random.randint(key_of[2], (NK, NA), 0, 2) < 1).astype(jnp.int32), jax.random.fold_in(key_of[2], 1), 0, 1)
    level_one_diag = normal_values(key_of[3], (NK * B, B), 1.0, 6.0, (), jnp.float32)
    level_two_panels = normal_values(key_of[4], (NM * B, NA * B), (NA * B) ** -0.5, 0.046875, ((0, 16), (1, 8)))
    level_two_pattern = set_ends((jax.random.randint(key_of[5], (NM, NA), 0, 2) < 1).astype(jnp.int32), jax.random.fold_in(key_of[5], 1), 0, 1)
    parent_lead = normal_values(key_of[6], (NM * B, B), B ** -0.5, 0.5, ((0, 16),))
    level_two_diag = normal_values(key_of[7], (NM * B, B), 1.0, 6.0, ((0, 16),), jnp.float32)
    parents = set_ends(jax.random.randint(key_of[8], (NM,), 0, NK), jax.random.fold_in(key_of[8], 1), 0, NK - 1).astype(jnp.int32)
    return {"ancestor_inverse": ancestor_inverse, "level_one_panels": level_one_panels, "level_one_pattern": level_one_pattern, "level_one_diag": level_one_diag, "level_two_panels": level_two_panels, "level_two_pattern": level_two_pattern, "parent_lead": parent_lead, "level_two_diag": level_two_diag, "parents": parents}


def apply_pattern(panels, pattern, block):
    count, blocks = pattern.shape
    shaped = panels.reshape(count, block, blocks, block)
    return (shaped * pattern.astype(panels.dtype)[:, None, :, None]).reshape(panels.shape)


def reference(ancestor_inverse, level_one_panels, level_one_pattern, level_one_diag, level_two_panels, level_two_pattern, parent_lead, level_two_diag, parents):
    block = level_one_diag.shape[1]
    one_count = level_one_pattern.shape[0]
    two_count = level_two_pattern.shape[0]
    width = ancestor_inverse.shape[0]
    masked_one = apply_pattern(level_one_panels, level_one_pattern, block)
    masked_two = apply_pattern(level_two_panels, level_two_pattern, block)
    first = jnp.dot(masked_one, ancestor_inverse, preferred_element_type=jnp.float32)
    second = jnp.dot(masked_two, ancestor_inverse, preferred_element_type=jnp.float32)
    level_one_rows = (-apply_pattern(first, level_one_pattern, block)).astype(jnp.bfloat16)
    one_blocks = masked_one.astype(jnp.float32).reshape(one_count, block, width)
    one_inverse = level_one_rows.astype(jnp.float32).reshape(one_count, block, width)
    own_sum = jnp.einsum('kai,kbi->kab', one_blocks, one_inverse)
    level_one_inv = level_one_diag.reshape(one_count, block, block) - own_sum
    chosen_rows = jnp.take(one_inverse, parents.astype(jnp.int32), axis=0)
    lead_blocks = parent_lead.astype(jnp.float32).reshape(two_count, block, block)
    carried = jnp.einsum('mab,mbi->mai', lead_blocks, chosen_rows).reshape(two_count * block, width)
    level_two_rows = (-apply_pattern(second + carried, level_two_pattern, block)).astype(jnp.bfloat16)
    two_blocks = masked_two.astype(jnp.float32).reshape(two_count, block, width)
    cross_sum = jnp.einsum('mai,mbi->mab', two_blocks, chosen_rows)
    parent_inv = jnp.take(level_one_inv, parents.astype(jnp.int32), axis=0)
    level_two_lead = -(cross_sum + jnp.einsum('mab,mbc->mac', lead_blocks, parent_inv, precision=lax.Precision.HIGHEST))
    self_sum = jnp.einsum('mai,mbi->mab', two_blocks, level_two_rows.astype(jnp.float32).reshape(two_count, block, width))
    level_two_inv = level_two_diag.reshape(two_count, block, block) - self_sum - jnp.einsum('mab,mcb->mac', lead_blocks, level_two_lead, precision=lax.Precision.HIGHEST)
    return (level_one_rows, level_one_inv.reshape(one_count * block, block), level_two_rows, level_two_lead.reshape(two_count * block, block), level_two_inv.reshape(two_count * block, block))
```

```python
import jax
import jax.numpy as jnp
from jax import lax
from jax.sharding import PartitionSpec as P

SIDE = 4
CORES = 2
F32 = jnp.float32


def x_step(d):
    return [(y * SIDE + x, y * SIDE + (x + d) % SIDE) for y in range(SIDE) for x in range(SIDE)]


def y_step(d):
    return [(y * SIDE + x, (y + d) % SIDE * SIDE + x) for y in range(SIDE) for x in range(SIDE)]


def z_step(d):
    return [(z * CORES + e, (z + d) % SIDE * CORES + e) for z in range(SIDE) for e in range(CORES)]


CORE_SWAP = [(i, i ^ 1) for i in range(SIDE * CORES)]


def turn(k):
    cols, rows = SIDE * SIDE, SIDE * CORES
    return [
        (r * cols + c, c // 2 * cols + 2 * r + (c + k) % 2) for r in range(rows) for c in range(cols)
    ]


def apply_pattern(panels, pattern, block):
    count, blocks = pattern.shape
    shaped = panels.reshape(count, block, blocks, block)
    return (shaped * pattern.astype(panels.dtype)[:, None, :, None]).reshape(panels.shape)


def gather_panels(masked, block):
    col, row = lax.axis_index("col"), lax.axis_index("row")
    z, core = row // CORES, row % CORES
    half = masked.shape[1] // 2
    pieces = []
    for k in range(2):
        part = lax.dynamic_slice_in_dim(masked, (col + k) % 2 * half, half, 1)
        pieces.append(lax.ppermute(part, ("row", "col"), turn(k)))
    own = jnp.stack(pieces)
    below = lax.ppermute(own, "row", z_step(1))
    above = lax.ppermute(own, "row", z_step(-1))
    far = jnp.stack(
        [lax.ppermute(below[0], "row", z_step(1)), lax.ppermute(above[1], "row", z_step(-1))]
    )
    found = []
    for shift, held in ((0, own), (-1, below), (1, above), (2, far)):
        other = lax.ppermute(held, "row", CORE_SWAP)
        for e, values in ((core, held), (1 - core, other)):
            source = (z + shift) % SIDE * CORES + e
            for k in range(2):
                found.append((2 * source + (col + k) % 2, values[k]))
    return found


def place(found, position):
    total = jnp.zeros((len(found),) + found[0][1].shape, found[0][1].dtype)
    for supernode, panel in found:
        total = lax.dynamic_update_index_in_dim(total, panel, position(supernode), 0)
    return total


def scatter_sum(product, halves, join, pick, first, second):
    def send(value, step):
        return lax.ppermute(value.astype(jnp.bfloat16), "col", step)

    ahead, behind = halves(product(2))
    from_behind = send(ahead, first(1)).astype(F32)
    from_ahead = send(behind, first(-1)).astype(F32)
    near, rest = halves(product(1))
    to_ahead = join(near + from_behind, rest)
    rest, near = halves(product(3))
    to_behind = join(rest, near + from_ahead)
    one = send(to_ahead, first(1)).astype(F32)
    two = send(to_behind, first(-1)).astype(F32)
    total = product(0) + one + two

    ahead, behind = halves(pick(total, 2))
    from_behind = send(ahead, second(1)).astype(F32)
    from_ahead = send(behind, second(-1)).astype(F32)
    near, rest = halves(pick(total, 1))
    to_ahead = join(near + from_behind, rest)
    rest, near = halves(pick(total, 3))
    to_behind = join(rest, near + from_ahead)
    one = send(to_ahead, second(1)).astype(F32)
    two = send(to_behind, second(-1)).astype(F32)
    return pick(total, 0) + one + two


def row_sum(values):
    z = lax.axis_index("row") // CORES
    values = values + lax.ppermute(values, "row", CORE_SWAP)
    parts = [values] + [lax.ppermute(values, "row", z_step(-d)) for d in range(1, SIDE)]
    parts = jnp.stack(parts)
    ordered = [
        lax.dynamic_index_in_dim(parts, (i - z) % SIDE, 0, keepdims=False) for i in range(SIDE)
    ]
    return (ordered[0] + ordered[1]) + (ordered[2] + ordered[3])


def per_device(
    ancestor_inverse,
    level_one_panels,
    level_one_pattern,
    level_one_diag,
    level_two_panels,
    level_two_pattern,
    parent_lead,
    level_two_diag,
    parents,
):
    block = level_one_diag.shape[1]
    bf16 = jnp.bfloat16
    col = lax.axis_index("col")
    x, y = col % SIDE, col // SIDE
    count = SIDE * SIDE
    span, width = ancestor_inverse.shape
    masked_one = apply_pattern(level_one_panels, level_one_pattern, block)
    masked_two = apply_pattern(level_two_panels, level_two_pattern, block)

    found_one = gather_panels(masked_one, block)
    found_two = gather_panels(masked_two, block)

    facts = jnp.concatenate(
        [
            jnp.broadcast_to(level_one_pattern.reshape(count, 1, 1), (count, 8, block)),
            jnp.broadcast_to(parents.reshape(1, 1, 1), (count, 8, block)),
        ],
        1,
    ).astype(bf16)
    cut = jnp.swapaxes(masked_one.reshape(block, count, block), 0, 1)
    cut = lax.all_to_all(jnp.concatenate([cut, facts], 1), "col", 0, 0, tiled=True)
    cut_pattern = cut[:, block, 0].astype(F32)
    readers = cut[:, block + 8, 0].astype(jnp.int32)
    parent_panels = lax.all_to_all(
        jnp.take(cut[:, :block], readers, axis=0), "col", 0, 0, tiled=True
    )
    parent_panels = jnp.swapaxes(parent_panels, 0, 1).reshape(block, width)

    stacked_one = place(found_one, lambda k: k).reshape(count * block, span)
    blocks = ancestor_inverse.reshape(span, SIDE, SIDE, block)
    turned = jnp.roll(blocks, (-y, -x), (1, 2))
    by_x = jnp.swapaxes(turned, 1, 2).reshape(span, SIDE, SIDE * block)
    by_y = turned.reshape(span, SIDE, SIDE * block)

    def one_part(rows, columns, first, second):
        middle = rows.shape[0] // 2
        return scatter_sum(
            lambda d: jnp.dot(rows, columns[:, d], preferred_element_type=F32),
            lambda v: (v[:middle], v[middle:]),
            lambda a, b: jnp.concatenate([a, b], 0),
            lambda v, d: v[:, d * block : (d + 1) * block],
            first,
            second,
        )

    middle = count * block // 2
    first_sum = jnp.concatenate(
        [
            one_part(stacked_one[:middle], by_x, x_step, y_step),
            one_part(stacked_one[middle:], by_y, y_step, x_step),
        ],
        0,
    ).reshape(count, block, block)
    one_cut = (-(first_sum * cut_pattern[:, None, None])).astype(bf16)
    back = jnp.stack([one_cut, jnp.take(one_cut, readers, axis=0)], 1)
    back = lax.all_to_all(back, "col", 0, 0, tiled=True)
    back = jnp.transpose(back, (1, 2, 0, 3)).reshape(2, block, width)
    level_one_rows, chosen_rows = back[0], back[1]

    def over(a, b):
        return lax.dot_general(a, b, (((1,), (1,)), ((), ())), preferred_element_type=F32)

    own_sum, cross_sum, parent_sum = row_sum(
        jnp.stack(
            [
                over(masked_one, level_one_rows),
                over(masked_two, chosen_rows),
                over(parent_panels, chosen_rows),
            ]
        )
    )

    def two_part(position, columns, first, second):
        rows = place(found_two, position).reshape(SIDE, SIDE * block, span)
        middle = columns.shape[1] // 2
        return scatter_sum(
            lambda d: jnp.dot(rows[d], columns, preferred_element_type=F32),
            lambda v: (v[:, :middle], v[:, middle:]),
            lambda a, b: jnp.concatenate([a, b], 1),
            lambda v, d: v[d * block : (d + 1) * block],
            first,
            second,
        )

    def x_major(m):
        return (m % SIDE - x) % SIDE * SIDE + (m // SIDE - y) % SIDE

    def y_major(m):
        return (m // SIDE - y) % SIDE * SIDE + (m % SIDE - x) % SIDE

    second_sum = jnp.concatenate(
        [
            two_part(x_major, ancestor_inverse[:, : width // 2], x_step, y_step),
            two_part(y_major, ancestor_inverse[:, width // 2 :], y_step, x_step),
        ],
        1,
    )
    carried = jnp.dot(parent_lead, chosen_rows, preferred_element_type=F32)
    level_two_rows = (-apply_pattern(second_sum + carried, level_two_pattern, block)).astype(bf16)
    self_sum = row_sum(over(masked_two, level_two_rows))

    diag_blocks = level_one_diag.reshape(count, block, block)
    level_one_inv = lax.dynamic_index_in_dim(diag_blocks, col, 0, keepdims=False) - own_sum
    parent_inv = lax.dynamic_index_in_dim(diag_blocks, parents[0], 0, keepdims=False) - parent_sum
    lead_wide = parent_lead.astype(F32)
    level_two_lead = -(
        cross_sum + jnp.dot(lead_wide, parent_inv, precision=lax.Precision.HIGHEST)
    )
    level_two_inv = (
        level_two_diag
        - self_sum
        - lax.dot_general(
            lead_wide, level_two_lead, (((1,), (1,)), ((), ())), precision=lax.Precision.HIGHEST
        )
    )
    return level_one_rows, level_one_inv, level_two_rows, level_two_lead, level_two_inv


def solution(mesh):
    in_specs = (
        P("col", "row"),
        P("col", "row"),
        P("col", "row"),
        P(),
        P("col", "row"),
        P("col", "row"),
        P("col", None),
        P("col", None),
        P("col"),
    )
    out_specs = (P("col", "row"), P("col", None), P("col", "row"), P("col", None), P("col", None))
    return jax.shard_map(
        per_device, mesh=mesh, in_specs=in_specs, out_specs=out_specs, check_vma=False
    )
```

```python
import jax
import jax.numpy as jnp
from jax import lax
from jax.experimental import pallas as pl
from jax.experimental.pallas import tpu as pltpu
from jax.sharding import PartitionSpec as P

SIDE = 4
CORES = 2
F32 = jnp.float32


def x_step(d):
    return [(y * SIDE + x, y * SIDE + (x + d) % SIDE) for y in range(SIDE) for x in range(SIDE)]


def y_step(d):
    return [(y * SIDE + x, (y + d) % SIDE * SIDE + x) for y in range(SIDE) for x in range(SIDE)]


def z_step(d):
    return [(z * CORES + e, (z + d) % SIDE * CORES + e) for z in range(SIDE) for e in range(CORES)]


CORE_SWAP = [(i, i ^ 1) for i in range(SIDE * CORES)]


def turn(k):
    cols, rows = SIDE * SIDE, SIDE * CORES
    return [
        (r * cols + c, c // 2 * cols + 2 * r + (c + k) % 2) for r in range(rows) for c in range(cols)
    ]


def apply_pattern(panels, pattern, block):
    count, blocks = pattern.shape
    shaped = panels.reshape(count, block, blocks, block)
    return (shaped * pattern.astype(panels.dtype)[:, None, :, None]).reshape(panels.shape)


def gather_panels(masked):
    col = lax.axis_index("col")
    half = masked.shape[1] // 2
    pieces = []
    for k in range(2):
        part = lax.dynamic_slice_in_dim(masked, (col + k) % 2 * half, half, 1)
        pieces.append(lax.ppermute(part, ("row", "col"), turn(k)))
    even = col % 2 == 0
    own = jnp.stack(
        [jnp.where(even, pieces[0], pieces[1]), jnp.where(even, pieces[1], pieces[0])]
    )
    below = lax.ppermute(own, "row", z_step(1))
    above = lax.ppermute(own, "row", z_step(-1))
    far = jnp.stack(
        [lax.ppermute(below[0], "row", z_step(1)), lax.ppermute(above[1], "row", z_step(-1))]
    )
    return own, [
        jnp.concatenate([held, lax.ppermute(held, "row", CORE_SWAP)], 0)
        for held in (own, below, above, far)
    ]


def arrival(supernode):
    row = lax.axis_index("row")
    z, core = row // CORES, row % CORES
    source = supernode // 2
    slot = jnp.array([0, 2, 3, 1], jnp.int32)[(source // CORES - z) % SIDE]
    return slot * 4 + (source + core) % CORES * 2 + supernode % 2


def by_column(order, rows, matrix, block):
    count, depth = rows.shape
    width = matrix.shape[1]
    blocks = width // block
    tile = count // 4

    def kernel(order_ref, rows_ref, matrix_ref, out_ref, total):
        total[...] = jnp.dot(rows_ref[...], matrix_ref[...], preferred_element_type=F32)
        for j in range(blocks):
            start = pl.multiple_of(order_ref[j] * block, block)
            out_ref[j] = total[:, pl.ds(start, block)].astype(out_ref.dtype)

    return pl.pallas_call(
        kernel,
        out_shape=jax.ShapeDtypeStruct((blocks, count, block), rows.dtype),
        grid_spec=pltpu.PrefetchScalarGridSpec(
            num_scalar_prefetch=1,
            grid=(4,),
            in_specs=[
                pl.BlockSpec((tile, depth), lambda i, order_ref: (i, 0)),
                pl.BlockSpec((depth, width), lambda i, order_ref: (0, 0)),
            ],
            out_specs=pl.BlockSpec((blocks, tile, block), lambda i, order_ref: (0, i, 0)),
            scratch_shapes=[pltpu.VMEM((tile, width), F32)],
        ),
        compiler_params=pltpu.CompilerParams(vmem_limit_bytes=24 * 2**20),
        cost_estimate=pl.CostEstimate(
            flops=2 * count * depth * width,
            bytes_accessed=2 * (count * depth + depth * width + count * width),
            transcendentals=0,
        ),
    )(order, rows, matrix)


def by_supernode(order, rows, matrix, part):
    blocks, block, depth = rows.shape
    width = matrix.shape[1] // 2

    def kernel(order_ref, a_ref, b_ref, c_ref, d_ref, matrix_ref, out_ref):
        held = jnp.concatenate([a_ref[0], b_ref[0], c_ref[0], d_ref[0]], 0)
        total = jnp.dot(held, matrix_ref[...], preferred_element_type=F32)
        out_ref[...] = total.reshape(SIDE, block, width).astype(out_ref.dtype)

    def pick(j):
        return pl.BlockSpec((1, block, depth), lambda i, order_ref: (order_ref[SIDE * i + j], 0, 0))

    return pl.pallas_call(
        kernel,
        out_shape=jax.ShapeDtypeStruct((blocks, block, width), rows.dtype),
        grid_spec=pltpu.PrefetchScalarGridSpec(
            num_scalar_prefetch=1,
            grid=(SIDE,),
            in_specs=[pick(j) for j in range(SIDE)]
            + [pl.BlockSpec((depth, width), lambda i, order_ref: (0, part))],
            out_specs=pl.BlockSpec((SIDE, block, width), lambda i, order_ref: (i, 0, 0)),
        ),
        compiler_params=pltpu.CompilerParams(vmem_limit_bytes=24 * 2**20),
        cost_estimate=pl.CostEstimate(
            flops=2 * blocks * block * depth * width,
            bytes_accessed=2 * (blocks * block * (depth + width) + depth * width),
            transcendentals=0,
        ),
    )(order, rows, rows, rows, rows, matrix)


def scatter_sum(product, first, second):
    def send(value, step):
        return lax.ppermute(value.astype(jnp.bfloat16), "col", step).astype(F32)

    def ring(parts, axis, step):
        middle = parts[0].shape[axis] // 2
        cut = lambda v: (
            lax.slice_in_dim(v, 0, middle, axis=axis),
            lax.slice_in_dim(v, middle, 2 * middle, axis=axis),
        )
        ahead, behind = cut(parts[2])
        from_behind, from_ahead = send(ahead, step(1)), send(behind, step(-1))
        near, rest = cut(parts[1])
        to_ahead = jnp.concatenate([near + from_behind, rest], axis)
        rest, near = cut(parts[3])
        to_behind = jnp.concatenate([rest, near + from_ahead], axis)
        return parts[0] + send(to_ahead, step(1)) + send(to_behind, step(-1))

    wide = product.reshape((SIDE, SIDE) + product.shape[1:]).astype(F32)
    total = ring([wide[d] for d in range(SIDE)], 1, first)
    return ring([total[d] for d in range(SIDE)], 0, second)


def row_sum(values):
    z = lax.axis_index("row") // CORES
    values = values + lax.ppermute(values, "row", CORE_SWAP)
    parts = [values] + [lax.ppermute(values, "row", z_step(-d)) for d in range(1, SIDE)]
    parts = jnp.stack(parts)
    ordered = [
        lax.dynamic_index_in_dim(parts, (i - z) % SIDE, 0, keepdims=False) for i in range(SIDE)
    ]
    return (ordered[0] + ordered[1]) + (ordered[2] + ordered[3])


def per_device(
    ancestor_inverse,
    level_one_panels,
    level_one_pattern,
    level_one_diag,
    level_two_panels,
    level_two_pattern,
    parent_lead,
    level_two_diag,
    parents,
):
    block = level_one_diag.shape[1]
    bf16 = jnp.bfloat16
    col = lax.axis_index("col")
    x, y = col % SIDE, col // SIDE
    count = SIDE * SIDE
    span, width = ancestor_inverse.shape
    masked_one = apply_pattern(level_one_panels, level_one_pattern, block)
    masked_two = apply_pattern(level_two_panels, level_two_pattern, block)

    own_one, found_one = gather_panels(masked_one)
    masked_later, cut_one, _ = lax.optimization_barrier((masked_two, masked_one, own_one))
    own_two, found_two = gather_panels(masked_later)

    facts = jnp.concatenate(
        [
            jnp.broadcast_to(level_one_pattern.reshape(count, 1, 1), (count, 8, block)),
            jnp.broadcast_to(parents.reshape(1, 1, 1), (count, 8, block)),
        ],
        1,
    ).astype(bf16)
    cut = jnp.swapaxes(cut_one.reshape(block, count, block), 0, 1)
    cut = lax.all_to_all(jnp.concatenate([cut, facts], 1), "col", 0, 0, tiled=True)
    cut_pattern = cut[:, block, 0].astype(F32)
    readers = cut[:, block + 8, 0].astype(jnp.int32)
    parent_panels = lax.all_to_all(
        jnp.take(cut[:, :block], readers, axis=0), "col", 0, 0, tiled=True
    )
    parent_panels = jnp.swapaxes(parent_panels, 0, 1).reshape(block, width)

    steps = jnp.arange(count, dtype=jnp.int32)
    outer, inner = steps // SIDE, steps % SIDE
    x_major = (y + inner) % SIDE * SIDE + (x + outer) % SIDE
    y_major = (y + outer) % SIDE * SIDE + (x + inner) % SIDE

    def one_part(held, order, first, second):
        rows = jnp.concatenate(held, 0).reshape(-1, span)
        return scatter_sum(by_column(order, rows, ancestor_inverse, block), first, second)

    place = arrival(steps)
    first_sum = jnp.concatenate(
        [
            one_part(found_one[:2], x_major, x_step, y_step),
            one_part(found_one[2:], y_major, y_step, x_step),
        ],
        0,
    ).reshape(count, block, block)
    first_sum = jnp.take(first_sum, place, axis=0)
    one_cut = (-(first_sum * cut_pattern[:, None, None])).astype(bf16)
    back = jnp.stack([one_cut, jnp.take(one_cut, readers, axis=0)], 1)
    back = lax.all_to_all(back, "col", 0, 0, tiled=True)
    back = jnp.transpose(back, (1, 2, 0, 3)).reshape(2, block, width)
    level_one_rows, chosen_rows = back[0], back[1]

    def over(a, b):
        return lax.dot_general(a, b, (((1,), (1,)), ((), ())), preferred_element_type=F32)

    own_sum, cross_sum, parent_sum = row_sum(
        jnp.stack(
            [
                over(masked_one, level_one_rows),
                over(masked_two, chosen_rows),
                over(parent_panels, chosen_rows),
            ]
        )
    )

    rows_two = jnp.concatenate(found_two, 0)

    def two_part(part, order, first, second):
        return scatter_sum(
            by_supernode(jnp.take(place, order), rows_two, ancestor_inverse, part), first, second
        )

    second_sum = jnp.concatenate(
        [two_part(0, x_major, x_step, y_step), two_part(1, y_major, y_step, x_step)], 1
    )
    carried = jnp.dot(parent_lead, chosen_rows, preferred_element_type=F32)
    level_two_rows = (-apply_pattern(second_sum + carried, level_two_pattern, block)).astype(bf16)
    self_sum = row_sum(over(masked_two, level_two_rows))

    diag_blocks = level_one_diag.reshape(count, block, block)
    level_one_inv = lax.dynamic_index_in_dim(diag_blocks, col, 0, keepdims=False) - own_sum
    parent_inv = lax.dynamic_index_in_dim(diag_blocks, parents[0], 0, keepdims=False) - parent_sum
    lead_wide = parent_lead.astype(F32)
    level_two_lead = -(
        cross_sum + jnp.dot(lead_wide, parent_inv, precision=lax.Precision.HIGHEST)
    )
    level_two_inv = (
        level_two_diag
        - self_sum
        - lax.dot_general(
            lead_wide, level_two_lead, (((1,), (1,)), ((), ())), precision=lax.Precision.HIGHEST
        )
    )
    return level_one_rows, level_one_inv, level_two_rows, level_two_lead, level_two_inv


def solution(mesh):
    in_specs = (
        P("col", "row"),
        P("col", "row"),
        P("col", "row"),
        P(),
        P("col", "row"),
        P("col", "row"),
        P("col", None),
        P("col", None),
        P("col"),
    )
    out_specs = (P("col", "row"), P("col", None), P("col", "row"), P("col", None), P("col", None))
    return jax.shard_map(
        per_device, mesh=mesh, in_specs=in_specs, out_specs=out_specs, check_vma=False
    )
```

```python
import jax
import jax.numpy as jnp
from jax import lax
from jax.experimental import pallas as pl
from jax.experimental.pallas import tpu as pltpu
from jax.sharding import PartitionSpec as P

SIDE = 4
CORES = 2
F32 = jnp.float32


def x_step(d):
    return [(y * SIDE + x, y * SIDE + (x + d) % SIDE) for y in range(SIDE) for x in range(SIDE)]


def y_step(d):
    return [(y * SIDE + x, (y + d) % SIDE * SIDE + x) for y in range(SIDE) for x in range(SIDE)]


def z_step(d):
    return [(z * CORES + e, (z + d) % SIDE * CORES + e) for z in range(SIDE) for e in range(CORES)]


CORE_SWAP = [(i, i ^ 1) for i in range(SIDE * CORES)]


def turn(k):
    cols, rows = SIDE * SIDE, SIDE * CORES
    return [
        (r * cols + c, c // 2 * cols + 2 * r + (c + k) % 2) for r in range(rows) for c in range(cols)
    ]


def apply_pattern(panels, pattern, block):
    count, blocks = pattern.shape
    shaped = panels.reshape(count, block, blocks, block)
    return (shaped * pattern.astype(panels.dtype)[:, None, :, None]).reshape(panels.shape)


def gather_panels(masked):
    col = lax.axis_index("col")
    half = masked.shape[1] // 2
    pieces = []
    for k in range(2):
        part = lax.dynamic_slice_in_dim(masked, (col + k) % 2 * half, half, 1)
        pieces.append(lax.ppermute(part, ("row", "col"), turn(k)))
    even = col % 2 == 0
    own = jnp.stack(
        [jnp.where(even, pieces[0], pieces[1]), jnp.where(even, pieces[1], pieces[0])]
    )
    below = lax.ppermute(own, "row", z_step(1))
    above = lax.ppermute(own, "row", z_step(-1))
    far = jnp.stack(
        [lax.ppermute(below[0], "row", z_step(1)), lax.ppermute(above[1], "row", z_step(-1))]
    )
    return own, [
        jnp.concatenate([held, lax.ppermute(held, "row", CORE_SWAP)], 0)
        for held in (own, below, above, far)
    ]


def arrival(supernode):
    row = lax.axis_index("row")
    z, core = row // CORES, row % CORES
    source = supernode // 2
    slot = jnp.array([0, 2, 3, 1], jnp.int32)[(source // CORES - z) % SIDE]
    return slot * 4 + (source + core) % CORES * 2 + supernode % 2


def by_column(order, rows, matrix, block):
    count, depth = rows.shape
    width = matrix.shape[1]
    blocks = width // block
    tile = count // 4

    def kernel(order_ref, rows_ref, matrix_ref, out_ref, total):
        total[...] = jnp.dot(rows_ref[...], matrix_ref[...], preferred_element_type=F32)
        for j in range(blocks):
            start = pl.multiple_of(order_ref[j] * block, block)
            out_ref[j] = total[:, pl.ds(start, block)].astype(out_ref.dtype)

    return pl.pallas_call(
        kernel,
        out_shape=jax.ShapeDtypeStruct((blocks, count, block), rows.dtype),
        grid_spec=pltpu.PrefetchScalarGridSpec(
            num_scalar_prefetch=1,
            grid=(4,),
            in_specs=[
                pl.BlockSpec((tile, depth), lambda i, order_ref: (i, 0)),
                pl.BlockSpec((depth, width), lambda i, order_ref: (0, 0)),
            ],
            out_specs=pl.BlockSpec((blocks, tile, block), lambda i, order_ref: (0, i, 0)),
            scratch_shapes=[pltpu.VMEM((tile, width), F32)],
        ),
        compiler_params=pltpu.CompilerParams(vmem_limit_bytes=24 * 2**20),
        cost_estimate=pl.CostEstimate(
            flops=2 * count * depth * width,
            bytes_accessed=2 * (count * depth + depth * width + count * width),
            transcendentals=0,
        ),
    )(order, rows, matrix)


def by_supernode(order, rows, matrix):
    blocks, block, depth = rows.shape
    width = matrix.shape[1]

    def kernel(order_ref, a_ref, b_ref, c_ref, d_ref, matrix_ref, out_ref):
        held = jnp.concatenate([a_ref[0], b_ref[0], c_ref[0], d_ref[0]], 0)
        total = jnp.dot(held, matrix_ref[...], preferred_element_type=F32)
        out_ref[...] = total.reshape(SIDE, block, width).astype(out_ref.dtype)

    def pick(j):
        return pl.BlockSpec((1, block, depth), lambda i, order_ref: (order_ref[SIDE * i + j], 0, 0))

    return pl.pallas_call(
        kernel,
        out_shape=jax.ShapeDtypeStruct((blocks, block, width), rows.dtype),
        grid_spec=pltpu.PrefetchScalarGridSpec(
            num_scalar_prefetch=1,
            grid=(blocks // SIDE,),
            in_specs=[pick(j) for j in range(SIDE)]
            + [pl.BlockSpec((depth, width), lambda i, order_ref: (0, 0))],
            out_specs=pl.BlockSpec((SIDE, block, width), lambda i, order_ref: (i, 0, 0)),
        ),
        compiler_params=pltpu.CompilerParams(vmem_limit_bytes=32 * 2**20),
        cost_estimate=pl.CostEstimate(
            flops=2 * blocks * block * depth * width,
            bytes_accessed=2 * (blocks * block * (depth + width) + depth * width),
            transcendentals=0,
        ),
    )(order, rows, rows, rows, rows, matrix)


def scatter_sum(product, first, second):
    def send(value, step):
        return lax.ppermute(value.astype(jnp.bfloat16), "col", step).astype(F32)

    def ring(parts, axis, step):
        middle = parts[0].shape[axis] // 2
        low = lambda v: lax.slice_in_dim(v, 0, middle, axis=axis)
        high = lambda v: lax.slice_in_dim(v, middle, 2 * middle, axis=axis)
        from_behind, from_ahead = send(low(parts[2]), step(1)), send(high(parts[2]), step(-1))
        to_ahead = jnp.concatenate(
            [low(parts[1]).astype(F32) + from_behind, high(parts[1]).astype(F32)], axis
        )
        to_behind = jnp.concatenate(
            [low(parts[3]).astype(F32), high(parts[3]).astype(F32) + from_ahead], axis
        )
        one, two = send(to_ahead, step(1)), send(to_behind, step(-1))
        return [parts[0], one, two]

    wide = product.reshape((SIDE, SIDE) + product.shape[1:])
    terms = ring([wide[d] for d in range(SIDE)], 1, first)
    parts = [terms[0][d].astype(F32) + terms[1][d] + terms[2][d] for d in range(SIDE)]
    terms = ring(parts, 0, second)
    return terms[0] + terms[1] + terms[2]


def row_parts(values):
    values = values + lax.ppermute(values, "row", CORE_SWAP)
    values = values.astype(jnp.bfloat16)
    return [values] + [lax.ppermute(values, "row", z_step(-d)) for d in range(1, SIDE)]


def whole(space=None):
    return pl.BlockSpec(memory_space=space or pltpu.VMEM)


def small_call(kernel, shapes, scalars, arrays, scratch=()):
    return pl.pallas_call(
        kernel,
        out_shape=[jax.ShapeDtypeStruct(shape, kind) for shape, kind in shapes],
        in_specs=[whole(pltpu.SMEM)] * len(scalars) + [whole()] * len(arrays),
        out_specs=[whole()] * len(shapes),
        scratch_shapes=list(scratch),
        compiler_params=pltpu.CompilerParams(vmem_limit_bytes=24 * 2**20),
    )(*scalars, *arrays)


def outgoing(place, readers, pattern, total):
    count, block = total.shape[:2]

    def kernel(place_ref, readers_ref, pattern_ref, total_ref, out_ref):
        for d in range(count):
            for j, k in enumerate((d, readers_ref[d])):
                value = total_ref[place_ref[k]] * pattern_ref[k].astype(F32)
                out_ref[d, j] = (-value).astype(out_ref.dtype)

    return small_call(
        kernel,
        [((count, 2, block, block), jnp.bfloat16)],
        [place, readers, pattern],
        [total],
    )[0]


def finish_rows(pattern, back, parent_panels, masked_one, masked_two, second, lead):
    count, _, block, _ = back.shape
    width = count * block
    kind = back.dtype

    def over(a, b):
        return lax.dot_general(a, b, (((1,), (1,)), ((), ())), preferred_element_type=F32)

    def kernel(
        pattern_ref, back_ref, panels_ref, one_ref, two_ref, second_ref, lead_ref,
        rows_one_ref, rows_two_ref, sums_ref, chosen, panels,
    ):
        for i in range(count):
            part = pl.ds(i * block, block)
            rows_one_ref[:, part] = back_ref[i, 0]
            chosen[:, part] = back_ref[i, 1]
            panels[:, part] = panels_ref[i]
        for i in range(count):
            part = pl.ds(i * block, block)
            total = second_ref[:, part].astype(F32) + jnp.dot(
                lead_ref[...], chosen[:, part], preferred_element_type=F32
            )
            rows_two_ref[:, part] = (-(total * pattern_ref[0, i].astype(F32))).astype(kind)
        sums_ref[0] = over(one_ref[...], rows_one_ref[...])
        sums_ref[1] = over(two_ref[...], chosen[...])
        sums_ref[2] = over(panels[...], chosen[...])
        sums_ref[3] = over(two_ref[...], rows_two_ref[...])

    return small_call(
        kernel,
        [((block, width), kind), ((block, width), kind), ((4, block, block), F32)],
        [pattern],
        [back, parent_panels, masked_one, masked_two, second, lead],
        [pltpu.VMEM((block, width), kind), pltpu.VMEM((block, width), kind)],
    )


def finish_blocks(z, parts, own_diag, parent_diag, two_diag, lead):
    block = lead.shape[0]

    def kernel(z_ref, a, b, c, d, own_ref, parent_ref, two_ref, lead_ref, one_out, lead_out, two_out, sums):
        held = (a, b, c, d)
        for k in range(SIDE):

            @pl.when(z_ref[0] == k)
            def _():
                w = [held[(i - k) % SIDE][...].astype(F32) for i in range(SIDE)]
                sums[...] = (w[0] + w[1]) + (w[2] + w[3])

        one_out[...] = own_ref[...] - sums[0]
        lead_wide = lead_ref[...].astype(F32)
        found = -(
            sums[1]
            + jnp.dot(
                lead_wide,
                parent_ref[...] - sums[2],
                precision=lax.Precision.HIGHEST,
                preferred_element_type=F32,
            )
        )
        lead_out[...] = found
        two_out[...] = (
            two_ref[...]
            - sums[3]
            - lax.dot_general(
                lead_wide,
                found,
                (((1,), (1,)), ((), ())),
                precision=lax.Precision.HIGHEST,
                preferred_element_type=F32,
            )
        )

    return small_call(
        kernel,
        [((block, block), F32)] * 3,
        [z],
        [*parts, own_diag, parent_diag, two_diag, lead],
        [pltpu.VMEM((4, block, block), F32)],
    )


def per_device(
    ancestor_inverse,
    level_one_panels,
    level_one_pattern,
    level_one_diag,
    level_two_panels,
    level_two_pattern,
    parent_lead,
    level_two_diag,
    parents,
):
    block = level_one_diag.shape[1]
    bf16 = jnp.bfloat16
    col = lax.axis_index("col")
    x, y = col % SIDE, col // SIDE
    count = SIDE * SIDE
    span, width = ancestor_inverse.shape
    masked_one = apply_pattern(level_one_panels, level_one_pattern, block)
    masked_two = apply_pattern(level_two_panels, level_two_pattern, block)

    place = arrival(jnp.arange(count, dtype=jnp.int32))
    own_two, found_two = gather_panels(masked_two)
    masked_later, _ = lax.optimization_barrier((masked_one, own_two))
    own_one, found_one = gather_panels(masked_later)
    product_two = by_supernode(place, jnp.concatenate(found_two, 0), ancestor_inverse)
    second_sum = lax.psum_scatter(
        product_two.reshape(count * block, width), "col", scatter_dimension=0, tiled=True
    )

    cut_one, _ = lax.optimization_barrier((masked_one, own_one))
    facts = jnp.concatenate(
        [
            jnp.broadcast_to(level_one_pattern.reshape(count, 1, 1), (count, 8, block)),
            jnp.broadcast_to(parents.reshape(1, 1, 1), (count, 8, block)),
        ],
        1,
    ).astype(bf16)
    cut = jnp.swapaxes(cut_one.reshape(block, count, block), 0, 1)
    cut = lax.all_to_all(jnp.concatenate([cut, facts], 1), "col", 0, 0, tiled=True)
    cut_pattern = cut[:, block, 0].astype(jnp.int32)
    readers = cut[:, block + 8, 0].astype(jnp.int32)
    parent_panels = lax.all_to_all(
        jnp.take(cut[:, :block], readers, axis=0), "col", 0, 0, tiled=True
    )

    steps = jnp.arange(count, dtype=jnp.int32)
    outer, inner = steps // SIDE, steps % SIDE
    x_major = (y + inner) % SIDE * SIDE + (x + outer) % SIDE
    y_major = (y + outer) % SIDE * SIDE + (x + inner) % SIDE

    def one_part(held, order, first, second):
        rows = jnp.concatenate(held, 0).reshape(-1, span)
        return scatter_sum(by_column(order, rows, ancestor_inverse, block), first, second)

    first_sum = jnp.concatenate(
        [
            one_part(found_one[:2], x_major, x_step, y_step),
            one_part(found_one[2:], y_major, y_step, x_step),
        ],
        0,
    ).reshape(count, block, block)
    back = lax.all_to_all(
        outgoing(place, readers, cut_pattern, first_sum), "col", 0, 0, tiled=True
    )
    level_one_rows, level_two_rows, sums = finish_rows(
        level_two_pattern, back, parent_panels, masked_one, masked_two, second_sum, parent_lead
    )

    diag_blocks = level_one_diag.reshape(count, block, block)
    level_one_inv, level_two_lead, level_two_inv = finish_blocks(
        (lax.axis_index("row") // CORES).reshape(1),
        row_parts(sums),
        lax.dynamic_index_in_dim(diag_blocks, col, 0, keepdims=False),
        lax.dynamic_index_in_dim(diag_blocks, parents[0], 0, keepdims=False),
        level_two_diag,
        parent_lead,
    )
    return level_one_rows, level_one_inv, level_two_rows, level_two_lead, level_two_inv


def solution(mesh):
    in_specs = (
        P("col", "row"),
        P("col", "row"),
        P("col", "row"),
        P(),
        P("col", "row"),
        P("col", "row"),
        P("col", None),
        P("col", None),
        P("col"),
    )
    out_specs = (P("col", "row"), P("col", None), P("col", "row"), P("col", None), P("col", None))
    return jax.shard_map(
        per_device, mesh=mesh, in_specs=in_specs, out_specs=out_specs, check_vma=False
    )
```

```python
import jax
import jax.numpy as jnp
from jax import lax
from jax.experimental import pallas as pl
from jax.experimental.pallas import tpu as pltpu
from jax.sharding import PartitionSpec as P

SIDE = 4
CORES = 2
F32 = jnp.float32


def x_step(d):
    return [(y * SIDE + x, y * SIDE + (x + d) % SIDE) for y in range(SIDE) for x in range(SIDE)]


def y_step(d):
    return [(y * SIDE + x, (y + d) % SIDE * SIDE + x) for y in range(SIDE) for x in range(SIDE)]


def z_step(d):
    return [(z * CORES + e, (z + d) % SIDE * CORES + e) for z in range(SIDE) for e in range(CORES)]


CORE_SWAP = [(i, i ^ 1) for i in range(SIDE * CORES)]


def turn(k):
    cols, rows = SIDE * SIDE, SIDE * CORES
    return [
        (r * cols + c, c // 2 * cols + 2 * r + (c + k) % 2) for r in range(rows) for c in range(cols)
    ]


def apply_pattern(panels, pattern, block):
    count, blocks = pattern.shape
    shaped = panels.reshape(count, block, blocks, block)
    return (shaped * pattern.astype(panels.dtype)[:, None, :, None]).reshape(panels.shape)


def gather_panels(masked):
    col = lax.axis_index("col")
    half = masked.shape[1] // 2
    pieces = []
    for k in range(2):
        part = lax.dynamic_slice_in_dim(masked, (col + k) % 2 * half, half, 1)
        pieces.append(lax.ppermute(part, ("row", "col"), turn(k)))
    even = col % 2 == 0
    own = jnp.stack(
        [jnp.where(even, pieces[0], pieces[1]), jnp.where(even, pieces[1], pieces[0])]
    )
    below = lax.ppermute(own, "row", z_step(1))
    above = lax.ppermute(own, "row", z_step(-1))
    far = jnp.stack(
        [lax.ppermute(below[0], "row", z_step(1)), lax.ppermute(above[1], "row", z_step(-1))]
    )
    found = []
    for held in (own, below, above, far):
        found += [held, lax.ppermute(held, "row", CORE_SWAP)]
    return own, found


def arrival(supernode):
    row = lax.axis_index("row")
    z, core = row // CORES, row % CORES
    source = supernode // 2
    slot = jnp.array([0, 2, 3, 1], jnp.int32)[(source // CORES - z) % SIDE]
    return slot * 4 + (source + core) % CORES * 2 + supernode % 2


def ring_kernel(order, dots, operands, adds, last, shape):
    rows, columns = shape
    half = rows // 2
    kind = jnp.bfloat16
    split = not adds
    if last:
        outs = [((half, columns), kind)] * 2 + [((SIDE - 1, rows, columns), F32)]
    elif split:
        outs = [((SIDE, half, columns), kind)] * 2
    else:
        outs = [((SIDE, rows, columns), kind)]

    def kernel(order_ref, *refs):
        given = refs[: len(operands)]
        sums = refs[len(operands) : len(operands) + len(adds)]
        out = refs[len(operands) + len(adds) :]
        for j, start, term in dots(order_ref, *given):
            size = term.shape[0]
            for lo in range(start, start + size, min(size, half)):
                n = min(size, half)
                value = term[lo - start : lo - start + n]
                for ref, (_, first) in zip(sums, adds, strict=True):
                    if first <= lo < first + ref.shape[1]:
                        value = value + ref[j, lo - first : lo - first + n].astype(F32)
                side, at = lo // half, lo % half
                if last and j == 2:
                    out[side][at : at + n] = value.astype(kind)
                elif last:
                    out[2][min(j, 2), lo : lo + n] = value
                elif split:
                    out[side][j, at : at + n] = value.astype(kind)
                else:
                    out[0][j, lo : lo + n] = value.astype(kind)

    depth = operands[0].shape[-1]
    return pl.pallas_call(
        kernel,
        out_shape=[jax.ShapeDtypeStruct(*o) for o in outs],
        in_specs=[whole(pltpu.SMEM)] + [whole()] * (len(operands) + len(adds)),
        out_specs=[whole()] * len(outs),
        compiler_params=pltpu.CompilerParams(vmem_limit_bytes=32 * 2**20),
        cost_estimate=pl.CostEstimate(
            flops=2 * SIDE * rows * columns * depth,
            bytes_accessed=2 * SIDE * rows * columns,
            transcendentals=0,
        ),
    )(order, *operands, *[v for v, _ in adds])


def by_column(pieces, matrix, block):
    rows = sum(v.shape[0] * v.shape[1] for v in pieces)

    def dots(order_ref, *refs):
        right = jnp.concatenate(
            [
                refs[-1][:, pl.ds(pl.multiple_of(order_ref[j] * block, block), block)]
                for j in range(SIDE)
            ],
            1,
        )
        start = 0
        for ref in refs[:-1]:
            left = ref[...].reshape(-1, ref.shape[2])
            total = jnp.dot(left, right, preferred_element_type=F32)
            for j in range(SIDE):
                yield j, start, total[:, j * block : (j + 1) * block]
            start += left.shape[0]

    return lambda order, adds, last: ring_kernel(
        order, dots, [*pieces, matrix], adds, last, (rows, block)
    )


def by_supernode(rows, matrix, part):
    block = rows.shape[1]
    width = matrix.shape[1] // 2

    def dots(order_ref, rows_ref, matrix_ref):
        left = jnp.concatenate([rows_ref[order_ref[j]] for j in range(SIDE)], 0)
        total = jnp.dot(
            left, matrix_ref[:, part * width : (part + 1) * width], preferred_element_type=F32
        )
        for j in range(SIDE):
            yield j, 0, total[j * block : (j + 1) * block]

    return lambda order, adds, last: ring_kernel(
        order, dots, [rows, matrix], adds, last, (block, width)
    )


def scatter_sum(step_of, orders, first, second):
    def send(value, step):
        return lax.ppermute(value.astype(jnp.bfloat16), "col", step)

    low, high = step_of(orders[2], [], False)
    half = low.shape[1]
    from_behind, from_ahead = send(low, first(1)), send(high, first(-1))
    (to_ahead,) = step_of(orders[1], [(from_behind, 0)], False)
    (to_behind,) = step_of(orders[3], [(from_ahead, half)], False)
    one, two = send(to_ahead, first(1)), send(to_behind, first(-1))
    low, high, rest = step_of(orders[0], [(one, 0), (two, 0)], True)

    from_behind, from_ahead = send(low, second(1)).astype(F32), send(high, second(-1)).astype(F32)
    to_ahead = jnp.concatenate([rest[1, :half] + from_behind, rest[1, half:]], 0)
    to_behind = jnp.concatenate([rest[2, :half], rest[2, half:] + from_ahead], 0)
    one, two = send(to_ahead, second(1)), send(to_behind, second(-1))
    return rest[0] + one.astype(F32) + two.astype(F32)


def row_parts(values):
    values = values + lax.ppermute(values, "row", CORE_SWAP)
    values = values.astype(jnp.bfloat16)
    return [values] + [lax.ppermute(values, "row", z_step(-d)) for d in range(1, SIDE)]


def whole(space=None):
    return pl.BlockSpec(memory_space=space or pltpu.VMEM)


def small_call(kernel, shapes, scalars, arrays, scratch=()):
    return pl.pallas_call(
        kernel,
        out_shape=[jax.ShapeDtypeStruct(shape, kind) for shape, kind in shapes],
        in_specs=[whole(pltpu.SMEM)] * len(scalars) + [whole()] * len(arrays),
        out_specs=[whole()] * len(shapes),
        scratch_shapes=list(scratch),
        compiler_params=pltpu.CompilerParams(vmem_limit_bytes=24 * 2**20),
    )(*scalars, *arrays)


def outgoing(place, readers, pattern, total, cut):
    count, block = total.shape[:2]

    def kernel(place_ref, readers_ref, pattern_ref, total_ref, cut_ref, out_ref):
        for d in range(count):
            for j, k in enumerate((d, readers_ref[d])):
                value = total_ref[place_ref[k]] * pattern_ref[k].astype(F32)
                out_ref[d, j] = (-value).astype(out_ref.dtype)
            out_ref[d, 2] = cut_ref[readers_ref[d], :block]

    return small_call(
        kernel,
        [((count, 3, block, block), jnp.bfloat16)],
        [place, readers, pattern],
        [total, cut],
    )[0]


def finish_rows(pattern, back, masked_one, masked_two, second, lead):
    count, _, block, _ = back.shape
    width = count * block
    kind = back.dtype

    def over(a, b):
        return lax.dot_general(a, b, (((1,), (1,)), ((), ())), preferred_element_type=F32)

    def kernel(
        pattern_ref, back_ref, one_ref, two_ref, second_ref, lead_ref,
        rows_one_ref, rows_two_ref, sums_ref, chosen, panels,
    ):
        for i in range(count):
            part = pl.ds(i * block, block)
            rows_one_ref[:, part] = back_ref[i, 0]
            chosen[:, part] = back_ref[i, 1]
            panels[:, part] = back_ref[i, 2]
        for i in range(count):
            part = pl.ds(i * block, block)
            total = second_ref[:, part].astype(F32) + jnp.dot(
                lead_ref[...], chosen[:, part], preferred_element_type=F32
            )
            rows_two_ref[:, part] = (-(total * pattern_ref[0, i].astype(F32))).astype(kind)
        sums_ref[0] = over(one_ref[...], rows_one_ref[...])
        sums_ref[1] = over(two_ref[...], chosen[...])
        sums_ref[2] = over(panels[...], chosen[...])
        sums_ref[3] = over(two_ref[...], rows_two_ref[...])

    return small_call(
        kernel,
        [((block, width), kind), ((block, width), kind), ((4, block, block), F32)],
        [pattern],
        [back, masked_one, masked_two, second, lead],
        [pltpu.VMEM((block, width), kind), pltpu.VMEM((block, width), kind)],
    )


def finish_blocks(z, parts, own_diag, parent_diag, two_diag, lead):
    block = lead.shape[0]

    def kernel(z_ref, a, b, c, d, own_ref, parent_ref, two_ref, lead_ref, one_out, lead_out, two_out, sums):
        held = (a, b, c, d)
        for k in range(SIDE):

            @pl.when(z_ref[0] == k)
            def _():
                w = [held[(i - k) % SIDE][...].astype(F32) for i in range(SIDE)]
                sums[...] = (w[0] + w[1]) + (w[2] + w[3])

        one_out[...] = own_ref[...] - sums[0]
        lead_wide = lead_ref[...].astype(F32)
        found = -(
            sums[1]
            + jnp.dot(
                lead_wide,
                parent_ref[...] - sums[2],
                precision=lax.Precision.HIGHEST,
                preferred_element_type=F32,
            )
        )
        lead_out[...] = found
        two_out[...] = (
            two_ref[...]
            - sums[3]
            - lax.dot_general(
                lead_wide,
                found,
                (((1,), (1,)), ((), ())),
                precision=lax.Precision.HIGHEST,
                preferred_element_type=F32,
            )
        )

    return small_call(
        kernel,
        [((block, block), F32)] * 3,
        [z],
        [*parts, own_diag, parent_diag, two_diag, lead],
        [pltpu.VMEM((4, block, block), F32)],
    )


def per_device(
    ancestor_inverse,
    level_one_panels,
    level_one_pattern,
    level_one_diag,
    level_two_panels,
    level_two_pattern,
    parent_lead,
    level_two_diag,
    parents,
):
    block = level_one_diag.shape[1]
    bf16 = jnp.bfloat16
    col = lax.axis_index("col")
    x, y = col % SIDE, col // SIDE
    count = SIDE * SIDE
    span, width = ancestor_inverse.shape
    masked_one = apply_pattern(level_one_panels, level_one_pattern, block)
    masked_two = apply_pattern(level_two_panels, level_two_pattern, block)

    own_one, found_one = gather_panels(masked_one)
    masked_later, cut_one, _ = lax.optimization_barrier((masked_two, masked_one, own_one))
    own_two, found_two = gather_panels(masked_later)

    facts = jnp.concatenate(
        [
            jnp.broadcast_to(level_one_pattern.reshape(count, 1, 1), (count, 8, block)),
            jnp.broadcast_to(parents.reshape(1, 1, 1), (count, 8, block)),
        ],
        1,
    ).astype(bf16)
    cut = jnp.swapaxes(cut_one.reshape(block, count, block), 0, 1)
    cut = lax.all_to_all(jnp.concatenate([cut, facts], 1), "col", 0, 0, tiled=True)
    cut_pattern = cut[:, block, 0].astype(jnp.int32)
    readers = cut[:, block + 8, 0].astype(jnp.int32)

    steps = jnp.arange(count, dtype=jnp.int32)
    place = arrival(steps)
    outer, inner = steps // SIDE, steps % SIDE
    x_major = (y + inner) % SIDE * SIDE + (x + outer) % SIDE
    y_major = (y + outer) % SIDE * SIDE + (x + inner) % SIDE

    def one_part(pieces, order, first, second):
        return scatter_sum(
            by_column(pieces, ancestor_inverse, block), order.reshape(SIDE, SIDE), first, second
        )

    first_sum = jnp.concatenate(
        [
            one_part(found_one[:4], x_major, x_step, y_step),
            one_part(found_one[4:], y_major, y_step, x_step),
        ],
        0,
    ).reshape(count, block, block)
    back = lax.all_to_all(
        outgoing(place, readers, cut_pattern, first_sum, cut), "col", 0, 0, tiled=True
    )

    rows_two = jnp.concatenate(found_two, 0)

    def two_part(part, order, first, second):
        return scatter_sum(
            by_supernode(rows_two, ancestor_inverse, part),
            place[order].reshape(SIDE, SIDE),
            first,
            second,
        )

    second_sum = jnp.concatenate(
        [two_part(0, x_major, x_step, y_step), two_part(1, y_major, y_step, x_step)], 1
    )
    level_one_rows, level_two_rows, sums = finish_rows(
        level_two_pattern, back, masked_one, masked_two, second_sum, parent_lead
    )

    diag_blocks = level_one_diag.reshape(count, block, block)
    level_one_inv, level_two_lead, level_two_inv = finish_blocks(
        (lax.axis_index("row") // CORES).reshape(1),
        row_parts(sums),
        lax.dynamic_index_in_dim(diag_blocks, col, 0, keepdims=False),
        lax.dynamic_index_in_dim(diag_blocks, parents[0], 0, keepdims=False),
        level_two_diag,
        parent_lead,
    )
    return level_one_rows, level_one_inv, level_two_rows, level_two_lead, level_two_inv


def solution(mesh):
    in_specs = (
        P("col", "row"),
        P("col", "row"),
        P("col", "row"),
        P(),
        P("col", "row"),
        P("col", "row"),
        P("col", None),
        P("col", None),
        P("col"),
    )
    out_specs = (P("col", "row"), P("col", None), P("col", "row"), P("col", None), P("col", None))
    return jax.shard_map(
        per_device, mesh=mesh, in_specs=in_specs, out_specs=out_specs, check_vma=False
    )
```

```python
import jax
import jax.numpy as jnp
from jax import lax
from jax.experimental import pallas as pl
from jax.experimental.pallas import tpu as pltpu
from jax.sharding import PartitionSpec as P

SIDE = 4
CORES = 2
F32 = jnp.float32


def x_step(d):
    return [(y * SIDE + x, y * SIDE + (x + d) % SIDE) for y in range(SIDE) for x in range(SIDE)]


def y_step(d):
    return [(y * SIDE + x, (y + d) % SIDE * SIDE + x) for y in range(SIDE) for x in range(SIDE)]


def z_step(d):
    return [(z * CORES + e, (z + d) % SIDE * CORES + e) for z in range(SIDE) for e in range(CORES)]


CORE_SWAP = [(i, i ^ 1) for i in range(SIDE * CORES)]


def turn(k):
    cols, rows = SIDE * SIDE, SIDE * CORES
    return [
        (r * cols + c, c // 2 * cols + 2 * r + (c + k) % 2) for r in range(rows) for c in range(cols)
    ]


def apply_pattern(panels, pattern, block):
    count, blocks = pattern.shape
    shaped = panels.reshape(count, block, blocks, block)
    return (shaped * pattern.astype(panels.dtype)[:, None, :, None]).reshape(panels.shape)


def own_panels(masked):
    col = lax.axis_index("col")
    half = masked.shape[1] // 2
    pieces = []
    for k in range(2):
        part = lax.dynamic_slice_in_dim(masked, (col + k) % 2 * half, half, 1)
        pieces.append(lax.ppermute(part, ("row", "col"), turn(k)))
    even = col % 2 == 0
    return jnp.stack(
        [jnp.where(even, pieces[0], pieces[1]), jnp.where(even, pieces[1], pieces[0])]
    )


def all_panels(own):
    below = lax.ppermute(own, "row", z_step(1))
    above = lax.ppermute(own, "row", z_step(-1))
    far = jnp.stack(
        [lax.ppermute(below[0], "row", z_step(1)), lax.ppermute(above[1], "row", z_step(-1))]
    )
    found = []
    for held in (own, below, above, far):
        found += [held, lax.ppermute(held, "row", CORE_SWAP)]
    return found


def arrival(supernode):
    row = lax.axis_index("row")
    z, core = row // CORES, row % CORES
    source = supernode // 2
    slot = jnp.array([0, 2, 3, 1], jnp.int32)[(source // CORES - z) % SIDE]
    return slot * 4 + (source + core) % CORES * 2 + supernode % 2


def ring_kernel(order, dots, operands, adds, last, shape):
    rows, columns = shape
    half = rows // 2
    kind = jnp.bfloat16
    split = not adds
    if last:
        outs = [((half, columns), kind)] * 2 + [((SIDE - 1, rows, columns), F32)]
    elif split:
        outs = [((SIDE, half, columns), kind)] * 2
    else:
        outs = [((SIDE, rows, columns), kind)]

    def kernel(order_ref, *refs):
        given = refs[: len(operands)]
        sums = refs[len(operands) : len(operands) + len(adds)]
        out = refs[len(operands) + len(adds) :]
        for j, start, term in dots(order_ref, *given):
            size = term.shape[0]
            for lo in range(start, start + size, min(size, half)):
                n = min(size, half)
                value = term[lo - start : lo - start + n]
                for ref, (_, first) in zip(sums, adds, strict=True):
                    if first <= lo < first + ref.shape[1]:
                        value = value + ref[j, lo - first : lo - first + n].astype(F32)
                side, at = lo // half, lo % half
                if last and j == 2:
                    out[side][at : at + n] = value.astype(kind)
                elif last:
                    out[2][min(j, 2), lo : lo + n] = value
                elif split:
                    out[side][j, at : at + n] = value.astype(kind)
                else:
                    out[0][j, lo : lo + n] = value.astype(kind)

    depth = operands[0].shape[-1]
    return pl.pallas_call(
        kernel,
        out_shape=[jax.ShapeDtypeStruct(*o) for o in outs],
        in_specs=[whole(pltpu.SMEM)] + [whole()] * (len(operands) + len(adds)),
        out_specs=[whole()] * len(outs),
        compiler_params=pltpu.CompilerParams(vmem_limit_bytes=32 * 2**20),
        cost_estimate=pl.CostEstimate(
            flops=2 * SIDE * rows * columns * depth,
            bytes_accessed=2 * SIDE * rows * columns,
            transcendentals=0,
        ),
    )(order, *operands, *[v for v, _ in adds])


def by_column(pieces, matrix, block):
    rows, depth = pieces[0].shape[0] * pieces[0].shape[1], pieces[0].shape[2]
    width = matrix.shape[1]
    steps = len(pieces)

    def kernel(*refs):
        matrix_ref, out_ref, held = refs[steps:]
        for i in range(steps):

            @pl.when(pl.program_id(0) == i)
            def _():
                held[...] = refs[i][...].reshape(rows, depth)

        total = jnp.dot(held[...], matrix_ref[...], preferred_element_type=F32)
        for d in range(width // block):
            out_ref[d] = total[:, d * block : (d + 1) * block].astype(out_ref.dtype)

    return pl.pallas_call(
        kernel,
        out_shape=jax.ShapeDtypeStruct((width // block, steps * rows, block), matrix.dtype),
        grid=(steps,),
        in_specs=[pl.BlockSpec(v.shape, lambda i: (0, 0, 0)) for v in pieces]
        + [pl.BlockSpec((depth, width), lambda i: (0, 0))],
        out_specs=pl.BlockSpec((width // block, rows, block), lambda i: (0, i, 0)),
        scratch_shapes=[pltpu.VMEM((rows, depth), matrix.dtype)],
        compiler_params=pltpu.CompilerParams(vmem_limit_bytes=52 * 2**20),
        cost_estimate=pl.CostEstimate(
            flops=2 * steps * rows * depth * width,
            bytes_accessed=2 * (steps * rows * (depth + width) + depth * width),
            transcendentals=0,
        ),
    )(*pieces, matrix)


def by_supernode(rows, matrix, part):
    block = rows.shape[1]
    width = matrix.shape[1] // 2

    def dots(order_ref, rows_ref, matrix_ref):
        left = jnp.concatenate([rows_ref[order_ref[j]] for j in range(SIDE)], 0)
        total = jnp.dot(
            left, matrix_ref[:, part * width : (part + 1) * width], preferred_element_type=F32
        )
        for j in range(SIDE):
            yield j, 0, total[j * block : (j + 1) * block]

    return lambda order, adds, last: ring_kernel(
        order, dots, [rows, matrix], adds, last, (block, width)
    )


def scatter_sum(step_of, orders, first, second):
    def send(value, step):
        return lax.ppermute(value.astype(jnp.bfloat16), "col", step)

    low, high = step_of(orders[2], [], False)
    half = low.shape[1]
    from_behind, from_ahead = send(low, first(1)), send(high, first(-1))
    (to_ahead,) = step_of(orders[1], [(from_behind, 0)], False)
    (to_behind,) = step_of(orders[3], [(from_ahead, half)], False)
    one, two = send(to_ahead, first(1)), send(to_behind, first(-1))
    low, high, rest = step_of(orders[0], [(one, 0), (two, 0)], True)

    far = jnp.concatenate([low, high], 0)
    terms = [send(rest[1], second(1)), send(rest[2], second(-1)), send(far, second(2))]
    return rest[0] + sum(v.astype(F32) for v in terms)


def row_parts(values):
    values = values + lax.ppermute(values, "row", CORE_SWAP)
    values = values.astype(jnp.bfloat16)
    return [values] + [lax.ppermute(values, "row", z_step(-d)) for d in range(1, SIDE)]


def whole(space=None):
    return pl.BlockSpec(memory_space=space or pltpu.VMEM)


def small_call(kernel, shapes, scalars, arrays, scratch=()):
    return pl.pallas_call(
        kernel,
        out_shape=[jax.ShapeDtypeStruct(shape, kind) for shape, kind in shapes],
        in_specs=[whole(pltpu.SMEM)] * len(scalars) + [whole()] * len(arrays),
        out_specs=[whole()] * len(shapes),
        scratch_shapes=list(scratch),
        compiler_params=pltpu.CompilerParams(vmem_limit_bytes=24 * 2**20),
    )(*scalars, *arrays)


def outgoing(place, readers, pattern, total):
    count, block = total.shape[:2]

    def kernel(place_ref, readers_ref, pattern_ref, total_ref, out_ref):
        for d in range(count):
            for j, k in enumerate((d, readers_ref[d])):
                value = total_ref[place_ref[k]].astype(F32) * pattern_ref[k].astype(F32)
                out_ref[d, j] = (-value).astype(out_ref.dtype)

    return small_call(
        kernel,
        [((count, 2, block, block), jnp.bfloat16)],
        [place, readers, pattern],
        [total],
    )[0]


def finish_rows(pattern, back, parent_panels, masked_one, masked_two, second, lead):
    count, _, block, _ = back.shape
    width = count * block
    kind = back.dtype

    def over(a, b):
        return lax.dot_general(a, b, (((1,), (1,)), ((), ())), preferred_element_type=F32)

    def kernel(
        pattern_ref, back_ref, panels_ref, one_ref, two_ref, second_ref, lead_ref,
        rows_one_ref, rows_two_ref, sums_ref, chosen, panels,
    ):
        for i in range(count):
            part = pl.ds(i * block, block)
            rows_one_ref[:, part] = back_ref[i, 0]
            chosen[:, part] = back_ref[i, 1]
            panels[:, part] = panels_ref[i]
        for i in range(count):
            part = pl.ds(i * block, block)
            total = second_ref[:, part].astype(F32) + jnp.dot(
                lead_ref[...], chosen[:, part], preferred_element_type=F32
            )
            rows_two_ref[:, part] = (-(total * pattern_ref[0, i].astype(F32))).astype(kind)
        sums_ref[0] = over(one_ref[...], rows_one_ref[...])
        sums_ref[1] = over(two_ref[...], chosen[...])
        sums_ref[2] = over(panels[...], chosen[...])
        sums_ref[3] = over(two_ref[...], rows_two_ref[...])

    return small_call(
        kernel,
        [((block, width), kind), ((block, width), kind), ((4, block, block), F32)],
        [pattern],
        [back, parent_panels, masked_one, masked_two, second, lead],
        [pltpu.VMEM((block, width), kind), pltpu.VMEM((block, width), kind)],
    )


def finish_blocks(z, parts, own_diag, parent_diag, two_diag, lead):
    block = lead.shape[0]

    def kernel(z_ref, a, b, c, d, own_ref, parent_ref, two_ref, lead_ref, one_out, lead_out, two_out, sums):
        held = (a, b, c, d)
        for k in range(SIDE):

            @pl.when(z_ref[0] == k)
            def _():
                w = [held[(i - k) % SIDE][...].astype(F32) for i in range(SIDE)]
                sums[...] = (w[0] + w[1]) + (w[2] + w[3])

        one_out[...] = own_ref[...] - sums[0]
        lead_wide = lead_ref[...].astype(F32)
        found = -(
            sums[1]
            + jnp.dot(
                lead_wide,
                parent_ref[...] - sums[2],
                precision=lax.Precision.HIGHEST,
                preferred_element_type=F32,
            )
        )
        lead_out[...] = found
        two_out[...] = (
            two_ref[...]
            - sums[3]
            - lax.dot_general(
                lead_wide,
                found,
                (((1,), (1,)), ((), ())),
                precision=lax.Precision.HIGHEST,
                preferred_element_type=F32,
            )
        )

    return small_call(
        kernel,
        [((block, block), F32)] * 3,
        [z],
        [*parts, own_diag, parent_diag, two_diag, lead],
        [pltpu.VMEM((4, block, block), F32)],
    )


def per_device(
    ancestor_inverse,
    level_one_panels,
    level_one_pattern,
    level_one_diag,
    level_two_panels,
    level_two_pattern,
    parent_lead,
    level_two_diag,
    parents,
):
    block = level_one_diag.shape[1]
    bf16 = jnp.bfloat16
    col = lax.axis_index("col")
    x, y = col % SIDE, col // SIDE
    count = SIDE * SIDE
    span, width = ancestor_inverse.shape
    masked_one = apply_pattern(level_one_panels, level_one_pattern, block)
    masked_two = apply_pattern(level_two_panels, level_two_pattern, block)

    own_one = own_panels(masked_one)
    later_two, _ = lax.optimization_barrier((masked_two, own_one))
    own_two = own_panels(later_two)
    found_one = all_panels(own_one)
    own_two, found_one = lax.optimization_barrier((own_two, found_one))
    found_two = all_panels(own_two)
    product_one = by_column(found_one, ancestor_inverse, block)
    later_one, product_one = lax.optimization_barrier((masked_one, product_one))
    first_sum = lax.psum_scatter(
        product_one.reshape(count * count * block, block), "col", scatter_dimension=0, tiled=True
    ).reshape(count, block, block)

    facts = jnp.concatenate(
        [
            jnp.broadcast_to(level_one_pattern.reshape(count, 1, 1), (count, 8, block)),
            jnp.broadcast_to(parents.reshape(1, 1, 1), (count, 8, block)),
        ],
        1,
    ).astype(bf16)
    cut = jnp.swapaxes(later_one.reshape(block, count, block), 0, 1)
    cut = lax.all_to_all(jnp.concatenate([cut, facts], 1), "col", 0, 0, tiled=True)
    cut_pattern = cut[:, block, 0].astype(jnp.int32)
    readers = cut[:, block + 8, 0].astype(jnp.int32)
    parent_panels = lax.all_to_all(
        jnp.take(cut[:, :block], readers, axis=0), "col", 0, 0, tiled=True
    )

    steps = jnp.arange(count, dtype=jnp.int32)
    place = arrival(steps)
    outer, inner = steps // SIDE, steps % SIDE
    x_major = (y + inner) % SIDE * SIDE + (x + outer) % SIDE
    y_major = (y + outer) % SIDE * SIDE + (x + inner) % SIDE

    rows_two = jnp.concatenate(found_two, 0)

    def two_part(part, order, first, second):
        return scatter_sum(
            by_supernode(rows_two, ancestor_inverse, part),
            place[order].reshape(SIDE, SIDE),
            first,
            second,
        )

    second_sum = jnp.concatenate(
        [two_part(0, x_major, x_step, y_step), two_part(1, y_major, y_step, x_step)], 1
    )
    back = lax.all_to_all(
        outgoing(place, readers, cut_pattern, first_sum), "col", 0, 0, tiled=True
    )
    level_one_rows, level_two_rows, sums = finish_rows(
        level_two_pattern, back, parent_panels, masked_one, masked_two, second_sum, parent_lead
    )

    diag_blocks = level_one_diag.reshape(count, block, block)
    level_one_inv, level_two_lead, level_two_inv = finish_blocks(
        (lax.axis_index("row") // CORES).reshape(1),
        row_parts(sums),
        lax.dynamic_index_in_dim(diag_blocks, col, 0, keepdims=False),
        lax.dynamic_index_in_dim(diag_blocks, parents[0], 0, keepdims=False),
        level_two_diag,
        parent_lead,
    )
    return level_one_rows, level_one_inv, level_two_rows, level_two_lead, level_two_inv


def solution(mesh):
    in_specs = (
        P("col", "row"),
        P("col", "row"),
        P("col", "row"),
        P(),
        P("col", "row"),
        P("col", "row"),
        P("col", None),
        P("col", None),
        P("col"),
    )
    out_specs = (P("col", "row"), P("col", None), P("col", "row"), P("col", None), P("col", None))
    return jax.shard_map(
        per_device, mesh=mesh, in_specs=in_specs, out_specs=out_specs, check_vma=False
    )
```

```python
import jax
import jax.numpy as jnp
from jax import lax
from jax.experimental import pallas as pl
from jax.experimental.pallas import tpu as pltpu
from jax.sharding import PartitionSpec as P

SIDE = 4
CORES = 2
F32 = jnp.float32
RING_VMEM = 18 * 2**20


def x_step(d):
    return [(y * SIDE + x, y * SIDE + (x + d) % SIDE) for y in range(SIDE) for x in range(SIDE)]


def y_step(d):
    return [(y * SIDE + x, (y + d) % SIDE * SIDE + x) for y in range(SIDE) for x in range(SIDE)]


def z_step(d):
    return [(z * CORES + e, (z + d) % SIDE * CORES + e) for z in range(SIDE) for e in range(CORES)]


CORE_SWAP = [(i, i ^ 1) for i in range(SIDE * CORES)]


def turn(k):
    cols, rows = SIDE * SIDE, SIDE * CORES
    return [
        (r * cols + c, c // 2 * cols + 2 * r + (c + k) % 2) for r in range(rows) for c in range(cols)
    ]


def apply_pattern(panels, pattern, block):
    count, blocks = pattern.shape
    shaped = panels.reshape(count, block, blocks, block)
    return (shaped * pattern.astype(panels.dtype)[:, None, :, None]).reshape(panels.shape)


def own_panels(masked):
    col = lax.axis_index("col")
    half = masked.shape[1] // 2
    pieces = []
    for k in range(2):
        part = lax.dynamic_slice_in_dim(masked, (col + k) % 2 * half, half, 1)
        pieces.append(lax.ppermute(part, ("row", "col"), turn(k)))
    even = col % 2 == 0
    return jnp.stack(
        [jnp.where(even, pieces[0], pieces[1]), jnp.where(even, pieces[1], pieces[0])]
    )


def all_panels(own):
    below = lax.ppermute(own, "row", z_step(1))
    above = lax.ppermute(own, "row", z_step(-1))
    far = jnp.stack(
        [lax.ppermute(below[0], "row", z_step(1)), lax.ppermute(above[1], "row", z_step(-1))]
    )
    found = []
    for held in (own, below, above, far):
        found += [held, lax.ppermute(held, "row", CORE_SWAP)]
    return found


def arrival(supernode):
    row = lax.axis_index("row")
    z, core = row // CORES, row % CORES
    source = supernode // 2
    slot = jnp.array([0, 2, 3, 1], jnp.int32)[(source // CORES - z) % SIDE]
    return slot * 4 + (source + core) % CORES * 2 + supernode % 2


def ring_kernel(order, dots, operands, adds, last, shape):
    rows, columns = shape
    half = rows // 2
    kind = jnp.bfloat16
    split = not adds
    if last:
        outs = [((half, columns), kind)] * 2 + [((SIDE - 1, rows, columns), F32)]
    elif split:
        outs = [((SIDE, half, columns), kind)] * 2
    else:
        outs = [((SIDE, rows, columns), kind)]

    def kernel(order_ref, *refs):
        given = refs[: len(operands)]
        sums = refs[len(operands) : len(operands) + len(adds)]
        out = refs[len(operands) + len(adds) :]
        for j, start, term in dots(order_ref, *given):
            size = term.shape[0]
            for lo in range(start, start + size, min(size, half)):
                n = min(size, half)
                value = term[lo - start : lo - start + n]
                for ref, (_, first) in zip(sums, adds, strict=True):
                    if first <= lo < first + ref.shape[1]:
                        value = value + ref[j, lo - first : lo - first + n].astype(F32)
                side, at = lo // half, lo % half
                if last and j == 2:
                    out[side][at : at + n] = value.astype(kind)
                elif last:
                    out[2][min(j, 2), lo : lo + n] = value
                elif split:
                    out[side][j, at : at + n] = value.astype(kind)
                else:
                    out[0][j, lo : lo + n] = value.astype(kind)

    depth = operands[0].shape[-1]
    return pl.pallas_call(
        kernel,
        out_shape=[jax.ShapeDtypeStruct(*o) for o in outs],
        in_specs=[whole(pltpu.SMEM)] + [whole()] * (len(operands) + len(adds)),
        out_specs=[whole()] * len(outs),
        compiler_params=pltpu.CompilerParams(vmem_limit_bytes=RING_VMEM),
        cost_estimate=pl.CostEstimate(
            flops=2 * SIDE * rows * columns * depth,
            bytes_accessed=2 * SIDE * rows * columns,
            transcendentals=0,
        ),
    )(order, *operands, *[v for v, _ in adds])


def by_column(pieces, matrix, block):
    rows, depth = pieces[0].shape[0] * pieces[0].shape[1], pieces[0].shape[2]
    width = matrix.shape[1]
    steps = len(pieces)

    def kernel(*refs):
        matrix_ref, out_ref, held = refs[steps:]
        for i in range(steps):

            @pl.when(pl.program_id(0) == i)
            def _():
                held[...] = refs[i][...].reshape(rows, depth)

        total = jnp.dot(held[...], matrix_ref[...], preferred_element_type=F32)
        for d in range(width // block):
            out_ref[d] = total[:, d * block : (d + 1) * block].astype(out_ref.dtype)

    return pl.pallas_call(
        kernel,
        out_shape=jax.ShapeDtypeStruct((width // block, steps * rows, block), matrix.dtype),
        grid=(steps,),
        in_specs=[pl.BlockSpec(v.shape, lambda i: (0, 0, 0)) for v in pieces]
        + [pl.BlockSpec((depth, width), lambda i: (0, 0))],
        out_specs=pl.BlockSpec((width // block, rows, block), lambda i: (0, i, 0)),
        scratch_shapes=[pltpu.VMEM((rows, depth), matrix.dtype)],
        compiler_params=pltpu.CompilerParams(vmem_limit_bytes=52 * 2**20),
        cost_estimate=pl.CostEstimate(
            flops=2 * steps * rows * depth * width,
            bytes_accessed=2 * (steps * rows * (depth + width) + depth * width),
            transcendentals=0,
        ),
    )(*pieces, matrix)


def by_supernode(rows, matrix, part):
    block = rows.shape[1]
    width = matrix.shape[1] // 2

    def dots(order_ref, rows_ref, matrix_ref):
        left = jnp.concatenate([rows_ref[order_ref[j]] for j in range(SIDE)], 0)
        total = jnp.dot(
            left, matrix_ref[:, part * width : (part + 1) * width], preferred_element_type=F32
        )
        for j in range(SIDE):
            yield j, 0, total[j * block : (j + 1) * block]

    return lambda order, adds, last: ring_kernel(
        order, dots, [rows, matrix], adds, last, (block, width)
    )


def scatter_sum(step_of, orders, first, second):
    def send(value, step):
        return lax.ppermute(value.astype(jnp.bfloat16), "col", step)

    low, high = step_of(orders[2], [], False)
    half = low.shape[1]
    from_behind, from_ahead = send(low, first(1)), send(high, first(-1))
    (to_ahead,) = step_of(orders[1], [(from_behind, 0)], False)
    (to_behind,) = step_of(orders[3], [(from_ahead, half)], False)
    one, two = send(to_ahead, first(1)), send(to_behind, first(-1))

    def finish(one, two):
        low, high, rest = step_of(orders[0], [(one, 0), (two, 0)], True)
        far = jnp.concatenate([low, high], 0)
        terms = [send(rest[1], second(1)), send(rest[2], second(-1)), send(far, second(2))]
        return rest[0] + sum(v.astype(F32) for v in terms)

    return one, two, finish


def row_parts(values):
    values = values + lax.ppermute(values, "row", CORE_SWAP)
    values = values.astype(jnp.bfloat16)
    return [values] + [lax.ppermute(values, "row", z_step(-d)) for d in range(1, SIDE)]


def whole(space=None):
    return pl.BlockSpec(memory_space=space or pltpu.VMEM)


def small_call(kernel, shapes, scalars, arrays, scratch=()):
    return pl.pallas_call(
        kernel,
        out_shape=[jax.ShapeDtypeStruct(shape, kind) for shape, kind in shapes],
        in_specs=[whole(pltpu.SMEM)] * len(scalars) + [whole()] * len(arrays),
        out_specs=[whole()] * len(shapes),
        scratch_shapes=list(scratch),
        compiler_params=pltpu.CompilerParams(vmem_limit_bytes=24 * 2**20),
    )(*scalars, *arrays)


def outgoing(place, readers, pattern, total):
    count, block = total.shape[:2]

    def kernel(place_ref, readers_ref, pattern_ref, total_ref, out_ref):
        for d in range(count):
            for j, k in enumerate((d, readers_ref[d])):
                value = total_ref[place_ref[k]].astype(F32) * pattern_ref[k].astype(F32)
                out_ref[d, j] = (-value).astype(out_ref.dtype)

    return small_call(
        kernel,
        [((count, 2, block, block), jnp.bfloat16)],
        [place, readers, pattern],
        [total],
    )[0]


def finish_rows(pattern, back, parent_panels, masked_one, masked_two, second, lead):
    count, _, block, _ = back.shape
    width = count * block
    kind = back.dtype

    def over(a, b):
        return lax.dot_general(a, b, (((1,), (1,)), ((), ())), preferred_element_type=F32)

    def kernel(
        pattern_ref, back_ref, panels_ref, one_ref, two_ref, second_ref, lead_ref,
        rows_one_ref, rows_two_ref, sums_ref, chosen, panels,
    ):
        for i in range(count):
            part = pl.ds(i * block, block)
            rows_one_ref[:, part] = back_ref[i, 0]
            chosen[:, part] = back_ref[i, 1]
            panels[:, part] = panels_ref[i]
        for i in range(count):
            part = pl.ds(i * block, block)
            total = second_ref[:, part].astype(F32) + jnp.dot(
                lead_ref[...], chosen[:, part], preferred_element_type=F32
            )
            rows_two_ref[:, part] = (-(total * pattern_ref[0, i].astype(F32))).astype(kind)
        sums_ref[0] = over(one_ref[...], rows_one_ref[...])
        sums_ref[1] = over(two_ref[...], chosen[...])
        sums_ref[2] = over(panels[...], chosen[...])
        sums_ref[3] = over(two_ref[...], rows_two_ref[...])

    return small_call(
        kernel,
        [((block, width), kind), ((block, width), kind), ((4, block, block), F32)],
        [pattern],
        [back, parent_panels, masked_one, masked_two, second, lead],
        [pltpu.VMEM((block, width), kind), pltpu.VMEM((block, width), kind)],
    )


def finish_blocks(z, parts, own_diag, parent_diag, two_diag, lead):
    block = lead.shape[0]

    def kernel(z_ref, a, b, c, d, own_ref, parent_ref, two_ref, lead_ref, one_out, lead_out, two_out, sums):
        held = (a, b, c, d)
        for k in range(SIDE):

            @pl.when(z_ref[0] == k)
            def _():
                w = [held[(i - k) % SIDE][...].astype(F32) for i in range(SIDE)]
                sums[...] = (w[0] + w[1]) + (w[2] + w[3])

        one_out[...] = own_ref[...] - sums[0]
        lead_wide = lead_ref[...].astype(F32)
        found = -(
            sums[1]
            + jnp.dot(
                lead_wide,
                parent_ref[...] - sums[2],
                precision=lax.Precision.HIGHEST,
                preferred_element_type=F32,
            )
        )
        lead_out[...] = found
        two_out[...] = (
            two_ref[...]
            - sums[3]
            - lax.dot_general(
                lead_wide,
                found,
                (((1,), (1,)), ((), ())),
                precision=lax.Precision.HIGHEST,
                preferred_element_type=F32,
            )
        )

    return small_call(
        kernel,
        [((block, block), F32)] * 3,
        [z],
        [*parts, own_diag, parent_diag, two_diag, lead],
        [pltpu.VMEM((4, block, block), F32)],
    )


def per_device(
    ancestor_inverse,
    level_one_panels,
    level_one_pattern,
    level_one_diag,
    level_two_panels,
    level_two_pattern,
    parent_lead,
    level_two_diag,
    parents,
):
    block = level_one_diag.shape[1]
    bf16 = jnp.bfloat16
    col = lax.axis_index("col")
    x, y = col % SIDE, col // SIDE
    count = SIDE * SIDE
    span, width = ancestor_inverse.shape
    masked_one = apply_pattern(level_one_panels, level_one_pattern, block)
    masked_two = apply_pattern(level_two_panels, level_two_pattern, block)

    found_one = all_panels(own_panels(masked_one))
    later_two, found_one = lax.optimization_barrier((masked_two, found_one))
    own_two = own_panels(later_two)
    product_one = by_column(found_one, ancestor_inverse, block)
    later_one, product_one = lax.optimization_barrier((masked_one, product_one))
    first_sum = lax.psum_scatter(
        product_one.reshape(count * count * block, block), "col", scatter_dimension=0, tiled=True
    ).reshape(count, block, block)

    facts = jnp.concatenate(
        [
            jnp.broadcast_to(level_one_pattern.reshape(count, 1, 1), (count, 8, block)),
            jnp.broadcast_to(parents.reshape(1, 1, 1), (count, 8, block)),
        ],
        1,
    ).astype(bf16)
    cut = jnp.swapaxes(later_one.reshape(block, count, block), 0, 1)
    cut = lax.all_to_all(jnp.concatenate([cut, facts], 1), "col", 0, 0, tiled=True)
    own_two, cut = lax.optimization_barrier((own_two, cut))
    cut_pattern = cut[:, block, 0].astype(jnp.int32)
    readers = cut[:, block + 8, 0].astype(jnp.int32)
    parent_panels = lax.all_to_all(
        jnp.take(cut[:, :block], readers, axis=0), "col", 0, 0, tiled=True
    )
    found_two, parent_panels = lax.optimization_barrier((all_panels(own_two), parent_panels))

    steps = jnp.arange(count, dtype=jnp.int32)
    place = arrival(steps)
    outer, inner = steps // SIDE, steps % SIDE
    x_major = (y + inner) % SIDE * SIDE + (x + outer) % SIDE
    y_major = (y + outer) % SIDE * SIDE + (x + inner) % SIDE

    rows_two = jnp.concatenate(found_two, 0)

    def two_part(part, order, first, second):
        return scatter_sum(
            by_supernode(rows_two, ancestor_inverse, part),
            place[order].reshape(SIDE, SIDE),
            first,
            second,
        )

    one_a, two_a, finish_a = two_part(0, x_major, x_step, y_step)
    one_b, two_b, finish_b = two_part(1, y_major, y_step, x_step)
    going = outgoing(place, readers, cut_pattern, first_sum)
    back = lax.all_to_all(going, "col", 0, 0, tiled=True)
    one_a, two_a, one_b, two_b, _ = lax.optimization_barrier((one_a, two_a, one_b, two_b, going))
    second_sum = jnp.concatenate([finish_a(one_a, two_a), finish_b(one_b, two_b)], 1)
    level_one_rows, level_two_rows, sums = finish_rows(
        level_two_pattern, back, parent_panels, masked_one, masked_two, second_sum, parent_lead
    )

    diag_blocks = level_one_diag.reshape(count, block, block)
    level_one_inv, level_two_lead, level_two_inv = finish_blocks(
        (lax.axis_index("row") // CORES).reshape(1),
        row_parts(sums),
        lax.dynamic_index_in_dim(diag_blocks, col, 0, keepdims=False),
        lax.dynamic_index_in_dim(diag_blocks, parents[0], 0, keepdims=False),
        level_two_diag,
        parent_lead,
    )
    return level_one_rows, level_one_inv, level_two_rows, level_two_lead, level_two_inv


def solution(mesh):
    in_specs = (
        P("col", "row"),
        P("col", "row"),
        P("col", "row"),
        P(),
        P("col", "row"),
        P("col", "row"),
        P("col", None),
        P("col", None),
        P("col"),
    )
    out_specs = (P("col", "row"), P("col", None), P("col", "row"), P("col", None), P("col", None))
    return jax.shard_map(
        per_device, mesh=mesh, in_specs=in_specs, out_specs=out_specs, check_vma=False
    )
```

```python
import jax
import jax.numpy as jnp
from jax import lax
from jax.experimental import pallas as pl
from jax.experimental.pallas import tpu as pltpu
from jax.sharding import PartitionSpec as P

SIDE = 4
CORES = 2
F32 = jnp.float32
RING_VMEM = 18 * 2**20


def x_step(d):
    return [(y * SIDE + x, y * SIDE + (x + d) % SIDE) for y in range(SIDE) for x in range(SIDE)]


def y_step(d):
    return [(y * SIDE + x, (y + d) % SIDE * SIDE + x) for y in range(SIDE) for x in range(SIDE)]


def z_step(d):
    return [(z * CORES + e, (z + d) % SIDE * CORES + e) for z in range(SIDE) for e in range(CORES)]


CORE_SWAP = [(i, i ^ 1) for i in range(SIDE * CORES)]


def turn(k):
    cols, rows = SIDE * SIDE, SIDE * CORES
    return [
        (r * cols + c, c // 2 * cols + 2 * r + (c + k) % 2) for r in range(rows) for c in range(cols)
    ]


def apply_pattern(panels, pattern, block):
    count, blocks = pattern.shape
    shaped = panels.reshape(count, block, blocks, block)
    return (shaped * pattern.astype(panels.dtype)[:, None, :, None]).reshape(panels.shape)


def own_panels(masked):
    col = lax.axis_index("col")
    half = masked.shape[1] // 2
    pieces = []
    for k in range(2):
        part = lax.dynamic_slice_in_dim(masked, (col + k) % 2 * half, half, 1)
        pieces.append(lax.ppermute(part, ("row", "col"), turn(k)))
    even = col % 2 == 0
    return jnp.stack(
        [jnp.where(even, pieces[0], pieces[1]), jnp.where(even, pieces[1], pieces[0])]
    )


def all_panels(own):
    below = lax.ppermute(own, "row", z_step(1))
    above = lax.ppermute(own, "row", z_step(-1))
    far = jnp.stack(
        [lax.ppermute(below[0], "row", z_step(1)), lax.ppermute(above[1], "row", z_step(-1))]
    )
    found = []
    for held in (own, below, above, far):
        found += [held, lax.ppermute(held, "row", CORE_SWAP)]
    return found


def arrival(supernode):
    row = lax.axis_index("row")
    z, core = row // CORES, row % CORES
    source = supernode // 2
    slot = jnp.array([0, 2, 3, 1], jnp.int32)[(source // CORES - z) % SIDE]
    return slot * 4 + (source + core) % CORES * 2 + supernode % 2


def by_column(pieces, matrix, block):
    rows, depth = pieces[0].shape[0] * pieces[0].shape[1], pieces[0].shape[2]
    width = matrix.shape[1]
    steps = len(pieces)

    def kernel(*refs):
        matrix_ref, out_ref, held = refs[steps:]
        for i in range(steps):

            @pl.when(pl.program_id(0) == i)
            def _():
                held[...] = refs[i][...].reshape(rows, depth)

        total = jnp.dot(held[...], matrix_ref[...], preferred_element_type=F32)
        for d in range(width // block):
            out_ref[d] = total[:, d * block : (d + 1) * block].astype(out_ref.dtype)

    return pl.pallas_call(
        kernel,
        out_shape=jax.ShapeDtypeStruct((width // block, steps * rows, block), matrix.dtype),
        grid=(steps,),
        in_specs=[pl.BlockSpec(v.shape, lambda i: (0, 0, 0)) for v in pieces]
        + [pl.BlockSpec((depth, width), lambda i: (0, 0))],
        out_specs=pl.BlockSpec((width // block, rows, block), lambda i: (0, i, 0)),
        scratch_shapes=[pltpu.VMEM((rows, depth), matrix.dtype)],
        compiler_params=pltpu.CompilerParams(vmem_limit_bytes=52 * 2**20),
        cost_estimate=pl.CostEstimate(
            flops=2 * steps * rows * depth * width,
            bytes_accessed=2 * (steps * rows * (depth + width) + depth * width),
            transcendentals=0,
        ),
    )(*pieces, matrix)


def by_supernode(order, rows, matrix, part):
    block, depth = rows.shape[1:]
    width = matrix.shape[1] // 2
    groups = order.shape[0] // SIDE

    def kernel(order_ref, rows_ref, matrix_ref, out_ref):
        right = matrix_ref[:, part * width : (part + 1) * width]
        for g in range(groups):
            left = jnp.concatenate([rows_ref[order_ref[SIDE * g + j]] for j in range(SIDE)], 0)
            total = jnp.dot(left, right, preferred_element_type=F32)
            out_ref[g] = total.reshape(SIDE, block, width).astype(out_ref.dtype)

    return pl.pallas_call(
        kernel,
        out_shape=jax.ShapeDtypeStruct((groups, SIDE, block, width), rows.dtype),
        in_specs=[whole(pltpu.SMEM), whole(), whole()],
        out_specs=whole(),
        compiler_params=pltpu.CompilerParams(vmem_limit_bytes=RING_VMEM),
        cost_estimate=pl.CostEstimate(
            flops=2 * groups * SIDE * block * depth * width,
            bytes_accessed=2 * groups * SIDE * block * (depth + width),
            transcendentals=0,
        ),
    )(order, rows, matrix)


def send(value, step):
    return lax.ppermute(value.astype(jnp.bfloat16), "col", step)


def first_sends(product, order, step):
    far = product(order[2])[0]
    half = far.shape[1] // 2
    arriving = send(far[:, :half], step(1)), send(far[:, half:], step(-1))
    near = product(jnp.concatenate([order[1], order[3], order[0]]))
    return arriving, near


def second_sends(arriving, near, step):
    from_behind, from_ahead = [v.astype(F32) for v in arriving]
    half = from_behind.shape[1]
    wide = near.astype(F32)
    to_ahead = jnp.concatenate([wide[0, :, :half] + from_behind, wide[0, :, half:]], 1)
    to_behind = jnp.concatenate([wide[1, :, :half], wide[1, :, half:] + from_ahead], 1)
    return send(to_ahead, step(1)), send(to_behind, step(-1))


def third_sends(arriving, near, step):
    total = near[2].astype(F32) + arriving[0].astype(F32) + arriving[1].astype(F32)
    terms = [send(total[d], step(d)) for d in range(1, SIDE)]
    return total[0] + sum(v.astype(F32) for v in terms)


def row_parts(values):
    values = values + lax.ppermute(values, "row", CORE_SWAP)
    values = values.astype(jnp.bfloat16)
    return [values] + [lax.ppermute(values, "row", z_step(-d)) for d in range(1, SIDE)]


def whole(space=None):
    return pl.BlockSpec(memory_space=space or pltpu.VMEM)


def small_call(kernel, shapes, scalars, arrays, scratch=()):
    return pl.pallas_call(
        kernel,
        out_shape=[jax.ShapeDtypeStruct(shape, kind) for shape, kind in shapes],
        in_specs=[whole(pltpu.SMEM)] * len(scalars) + [whole()] * len(arrays),
        out_specs=[whole()] * len(shapes),
        scratch_shapes=list(scratch),
        compiler_params=pltpu.CompilerParams(vmem_limit_bytes=24 * 2**20),
    )(*scalars, *arrays)


def outgoing(place, readers, pattern, total):
    count, block = total.shape[:2]

    def kernel(place_ref, readers_ref, pattern_ref, total_ref, out_ref):
        for d in range(count):
            for j, k in enumerate((d, readers_ref[d])):
                value = total_ref[place_ref[k]].astype(F32) * pattern_ref[k].astype(F32)
                out_ref[d, j] = (-value).astype(out_ref.dtype)

    return small_call(
        kernel,
        [((count, 2, block, block), jnp.bfloat16)],
        [place, readers, pattern],
        [total],
    )[0]


def finish_rows(pattern, back, parent_panels, masked_one, masked_two, second, lead):
    count, _, block, _ = back.shape
    width = count * block
    kind = back.dtype

    def over(a, b):
        return lax.dot_general(a, b, (((1,), (1,)), ((), ())), preferred_element_type=F32)

    def kernel(
        pattern_ref, back_ref, panels_ref, one_ref, two_ref, second_ref, lead_ref,
        rows_one_ref, rows_two_ref, sums_ref, chosen, panels,
    ):
        for i in range(count):
            part = pl.ds(i * block, block)
            rows_one_ref[:, part] = back_ref[i, 0]
            chosen[:, part] = back_ref[i, 1]
            panels[:, part] = panels_ref[i]
        for i in range(count):
            part = pl.ds(i * block, block)
            total = second_ref[:, part].astype(F32) + jnp.dot(
                lead_ref[...], chosen[:, part], preferred_element_type=F32
            )
            rows_two_ref[:, part] = (-(total * pattern_ref[0, i].astype(F32))).astype(kind)
        sums_ref[0] = over(one_ref[...], rows_one_ref[...])
        sums_ref[1] = over(two_ref[...], chosen[...])
        sums_ref[2] = over(panels[...], chosen[...])
        sums_ref[3] = over(two_ref[...], rows_two_ref[...])

    return small_call(
        kernel,
        [((block, width), kind), ((block, width), kind), ((4, block, block), F32)],
        [pattern],
        [back, parent_panels, masked_one, masked_two, second, lead],
        [pltpu.VMEM((block, width), kind), pltpu.VMEM((block, width), kind)],
    )


def finish_blocks(z, parts, own_diag, parent_diag, two_diag, lead):
    block = lead.shape[0]

    def kernel(z_ref, a, b, c, d, own_ref, parent_ref, two_ref, lead_ref, one_out, lead_out, two_out, sums):
        held = (a, b, c, d)
        for k in range(SIDE):

            @pl.when(z_ref[0] == k)
            def _():
                w = [held[(i - k) % SIDE][...].astype(F32) for i in range(SIDE)]
                sums[...] = (w[0] + w[1]) + (w[2] + w[3])

        one_out[...] = own_ref[...] - sums[0]
        lead_wide = lead_ref[...].astype(F32)
        found = -(
            sums[1]
            + jnp.dot(
                lead_wide,
                parent_ref[...] - sums[2],
                precision=lax.Precision.HIGHEST,
                preferred_element_type=F32,
            )
        )
        lead_out[...] = found
        two_out[...] = (
            two_ref[...]
            - sums[3]
            - lax.dot_general(
                lead_wide,
                found,
                (((1,), (1,)), ((), ())),
                precision=lax.Precision.HIGHEST,
                preferred_element_type=F32,
            )
        )

    return small_call(
        kernel,
        [((block, block), F32)] * 3,
        [z],
        [*parts, own_diag, parent_diag, two_diag, lead],
        [pltpu.VMEM((4, block, block), F32)],
    )


def per_device(
    ancestor_inverse,
    level_one_panels,
    level_one_pattern,
    level_one_diag,
    level_two_panels,
    level_two_pattern,
    parent_lead,
    level_two_diag,
    parents,
):
    block = level_one_diag.shape[1]
    bf16 = jnp.bfloat16
    col = lax.axis_index("col")
    x, y = col % SIDE, col // SIDE
    count = SIDE * SIDE
    span, width = ancestor_inverse.shape
    masked_one = apply_pattern(level_one_panels, level_one_pattern, block)
    masked_two = apply_pattern(level_two_panels, level_two_pattern, block)

    found_one = all_panels(own_panels(masked_one))
    later_two, found_one = lax.optimization_barrier((masked_two, found_one))
    own_two = own_panels(later_two)
    later_one, own_two = lax.optimization_barrier((masked_one, own_two))
    product_one = by_column(found_one, ancestor_inverse, block)
    first_sum = lax.psum_scatter(
        product_one.reshape(count * count * block, block), "col", scatter_dimension=0, tiled=True
    ).reshape(count, block, block)

    facts = jnp.concatenate(
        [
            jnp.broadcast_to(level_one_pattern.reshape(count, 1, 1), (count, 8, block)),
            jnp.broadcast_to(parents.reshape(1, 1, 1), (count, 8, block)),
        ],
        1,
    ).astype(bf16)
    cut = jnp.swapaxes(later_one.reshape(block, count, block), 0, 1)
    cut = lax.all_to_all(jnp.concatenate([cut, facts], 1), "col", 0, 0, tiled=True)
    cut_pattern = cut[:, block, 0].astype(jnp.int32)
    readers = cut[:, block + 8, 0].astype(jnp.int32)
    parent_panels = lax.all_to_all(
        jnp.take(cut[:, :block], readers, axis=0), "col", 0, 0, tiled=True
    )
    found_two = all_panels(own_two)

    steps = jnp.arange(count, dtype=jnp.int32)
    place = arrival(steps)
    outer, inner = steps // SIDE, steps % SIDE
    x_major = (y + inner) % SIDE * SIDE + (x + outer) % SIDE
    y_major = (y + outer) % SIDE * SIDE + (x + inner) % SIDE

    rows_two = jnp.concatenate(found_two, 0)

    def product(part):
        return lambda order: by_supernode(order, rows_two, ancestor_inverse, part)

    first_a, near_a = first_sends(product(0), place[x_major].reshape(SIDE, SIDE), x_step)
    first_b, near_b = first_sends(product(1), place[y_major].reshape(SIDE, SIDE), y_step)
    first_a, first_b, parent_panels = lax.optimization_barrier((first_a, first_b, parent_panels))
    second_a = second_sends(first_a, near_a, x_step)
    second_b = second_sends(first_b, near_b, y_step)
    going = outgoing(place, readers, cut_pattern, first_sum)
    back = lax.all_to_all(going, "col", 0, 0, tiled=True)
    second_a, second_b, _ = lax.optimization_barrier((second_a, second_b, going))
    second_sum = jnp.concatenate(
        [third_sends(second_a, near_a, y_step), third_sends(second_b, near_b, x_step)], 1
    )
    level_one_rows, level_two_rows, sums = finish_rows(
        level_two_pattern, back, parent_panels, masked_one, masked_two, second_sum, parent_lead
    )

    diag_blocks = level_one_diag.reshape(count, block, block)
    level_one_inv, level_two_lead, level_two_inv = finish_blocks(
        (lax.axis_index("row") // CORES).reshape(1),
        row_parts(sums),
        lax.dynamic_index_in_dim(diag_blocks, col, 0, keepdims=False),
        lax.dynamic_index_in_dim(diag_blocks, parents[0], 0, keepdims=False),
        level_two_diag,
        parent_lead,
    )
    return level_one_rows, level_one_inv, level_two_rows, level_two_lead, level_two_inv


def solution(mesh):
    in_specs = (
        P("col", "row"),
        P("col", "row"),
        P("col", "row"),
        P(),
        P("col", "row"),
        P("col", "row"),
        P("col", None),
        P("col", None),
        P("col"),
    )
    out_specs = (P("col", "row"), P("col", None), P("col", "row"), P("col", None), P("col", None))
    return jax.shard_map(
        per_device, mesh=mesh, in_specs=in_specs, out_specs=out_specs, check_vma=False
    )
```

```python
import jax
import jax.numpy as jnp
from jax import lax
from jax.experimental import pallas as pl
from jax.experimental.pallas import tpu as pltpu
from jax.sharding import PartitionSpec as P

SIDE = 4
CORES = 2
F32 = jnp.float32
RING_VMEM = 28 * 2**20


def x_step(d):
    return [(y * SIDE + x, y * SIDE + (x + d) % SIDE) for y in range(SIDE) for x in range(SIDE)]


def y_step(d):
    return [(y * SIDE + x, (y + d) % SIDE * SIDE + x) for y in range(SIDE) for x in range(SIDE)]


def z_step(d):
    return [(z * CORES + e, (z + d) % SIDE * CORES + e) for z in range(SIDE) for e in range(CORES)]


CORE_SWAP = [(i, i ^ 1) for i in range(SIDE * CORES)]


def turn(k):
    cols, rows = SIDE * SIDE, SIDE * CORES
    return [
        (r * cols + c, c // 2 * cols + 2 * r + (c + k) % 2) for r in range(rows) for c in range(cols)
    ]


def apply_pattern(panels, pattern, block):
    count, blocks = pattern.shape
    shaped = panels.reshape(count, block, blocks, block)
    return (shaped * pattern.astype(panels.dtype)[:, None, :, None]).reshape(panels.shape)


def turned_panels(masked, k):
    col = lax.axis_index("col")
    half = masked.shape[1] // 2
    part = lax.dynamic_slice_in_dim(masked, (col + k) % 2 * half, half, 1)
    return lax.ppermute(part, ("row", "col"), turn(k))


def in_order(pieces):
    even = lax.axis_index("col") % 2 == 0
    return jnp.stack(
        [jnp.where(even, pieces[0], pieces[1]), jnp.where(even, pieces[1], pieces[0])]
    )


def all_panels(own):
    below = lax.ppermute(own, "row", z_step(1))
    above = lax.ppermute(own, "row", z_step(-1))
    far = jnp.stack(
        [lax.ppermute(below[0], "row", z_step(1)), lax.ppermute(above[1], "row", z_step(-1))]
    )
    found = []
    for held in (own, below, above, far):
        found += [held, lax.ppermute(held, "row", CORE_SWAP)]
    return found


def arrival(supernode):
    row = lax.axis_index("row")
    z, core = row // CORES, row % CORES
    source = supernode // 2
    slot = jnp.array([0, 2, 3, 1], jnp.int32)[(source // CORES - z) % SIDE]
    return slot * 4 + (source + core) % CORES * 2 + supernode % 2


def by_column(pieces, matrix, block):
    rows, depth = pieces[0].shape[0] * pieces[0].shape[1], pieces[0].shape[2]
    width = matrix.shape[1]
    steps = len(pieces)

    def kernel(*refs):
        matrix_ref, out_ref, held = refs[steps:]
        for i in range(steps):

            @pl.when(pl.program_id(0) == i)
            def _():
                held[...] = refs[i][...].reshape(rows, depth)

        total = jnp.dot(held[...], matrix_ref[...], preferred_element_type=F32)
        for d in range(width // block):
            out_ref[d] = total[:, d * block : (d + 1) * block].astype(out_ref.dtype)

    return pl.pallas_call(
        kernel,
        out_shape=jax.ShapeDtypeStruct((width // block, steps * rows, block), matrix.dtype),
        grid=(steps,),
        in_specs=[pl.BlockSpec(v.shape, lambda i: (0, 0, 0)) for v in pieces]
        + [pl.BlockSpec((depth, width), lambda i: (0, 0))],
        out_specs=pl.BlockSpec((width // block, rows, block), lambda i: (0, i, 0)),
        scratch_shapes=[pltpu.VMEM((rows, depth), matrix.dtype)],
        compiler_params=pltpu.CompilerParams(vmem_limit_bytes=52 * 2**20),
        cost_estimate=pl.CostEstimate(
            flops=2 * steps * rows * depth * width,
            bytes_accessed=2 * (steps * rows * (depth + width) + depth * width),
            transcendentals=0,
        ),
    )(*pieces, matrix)


def grouped_dot(rows_ref, order_ref, first, matrix_ref, part):
    width = matrix_ref.shape[1] // 2
    left = jnp.concatenate([rows_ref[order_ref[part, first + j]] for j in range(SIDE)], 0)
    total = jnp.dot(
        left, matrix_ref[:, part * width : (part + 1) * width], preferred_element_type=F32
    )
    return total.reshape(SIDE, -1, width)


def ring_call(kernel, shapes, scalars, arrays, flops=0):
    return pl.pallas_call(
        kernel,
        out_shape=[jax.ShapeDtypeStruct(shape, kind) for shape, kind in shapes],
        in_specs=[whole(pltpu.SMEM)] * len(scalars) + [whole()] * len(arrays),
        out_specs=[whole()] * len(shapes),
        compiler_params=pltpu.CompilerParams(vmem_limit_bytes=RING_VMEM),
        cost_estimate=pl.CostEstimate(flops=flops, bytes_accessed=2**22, transcendentals=0),
    )(*scalars, *arrays)


def ring_far(order, rows, matrix):
    block, depth = rows.shape[1:]
    half, width = block // 2, matrix.shape[1] // 2

    def kernel(order_ref, rows_ref, matrix_ref, *out):
        for part in range(2):
            total = grouped_dot(rows_ref, order_ref, 2 * SIDE, matrix_ref, part)
            out[2 * part][...] = total[:, :half].astype(rows.dtype)
            out[2 * part + 1][...] = total[:, half:].astype(rows.dtype)

    shape = ((SIDE, half, width), rows.dtype)
    flops = 4 * SIDE * block * depth * width
    return ring_call(kernel, [shape] * 4, [order], [rows, matrix], flops)


def ring_near(order, rows, matrix):
    block, depth = rows.shape[1:]
    width = matrix.shape[1] // 2

    def kernel(order_ref, rows_ref, matrix_ref, *out):
        for part in range(2):
            for g, d in enumerate((1, 3, 0)):
                total = grouped_dot(rows_ref, order_ref, d * SIDE, matrix_ref, part)
                out[3 * part + g][...] = total.astype(rows.dtype)

    shape = ((SIDE, block, width), rows.dtype)
    flops = 12 * SIDE * block * depth * width
    return ring_call(kernel, [shape] * 6, [order], [rows, matrix], flops)


def send(value, step):
    return lax.ppermute(value, "col", step)


def second_sends(arriving, near, step):
    half = arriving[0].shape[1]

    def kernel(low_ref, high_ref, ahead_ref, behind_ref, ahead_out, behind_out):
        kind = ahead_out.dtype
        ahead_out[:, :half] = (ahead_ref[:, :half].astype(F32) + low_ref[...].astype(F32)).astype(kind)
        ahead_out[:, half:] = ahead_ref[:, half:]
        behind_out[:, :half] = behind_ref[:, :half]
        behind_out[:, half:] = (behind_ref[:, half:].astype(F32) + high_ref[...].astype(F32)).astype(kind)

    shape = (near[0].shape, near[0].dtype)
    ahead, behind = ring_call(kernel, [shape] * 2, [], [*arriving, near[0], near[1]])
    return send(ahead, step(1)), send(behind, step(-1))


def third_sends(arriving, near, step):
    _, block, width = near[2].shape
    kind = near[2].dtype

    def kernel(one_ref, two_ref, own_ref, own_out, *out):
        for d in range(SIDE):
            total = own_ref[d].astype(F32) + one_ref[d].astype(F32) + two_ref[d].astype(F32)
            if d:
                out[d - 1][...] = total.astype(kind)
            else:
                own_out[...] = total

    shape = (block, width)
    own, *others = ring_call(
        kernel, [(shape, F32)] + [(shape, kind)] * 3, [], [*arriving, near[2]]
    )
    return [own] + [send(v, step(d + 1)) for d, v in enumerate(others)]


def row_parts(values):
    values = values + lax.ppermute(values, "row", CORE_SWAP)
    values = values.astype(jnp.bfloat16)
    return [values] + [lax.ppermute(values, "row", z_step(-d)) for d in range(1, SIDE)]


def whole(space=None):
    return pl.BlockSpec(memory_space=space or pltpu.VMEM)


def small_call(kernel, shapes, scalars, arrays, scratch=()):
    return pl.pallas_call(
        kernel,
        out_shape=[jax.ShapeDtypeStruct(shape, kind) for shape, kind in shapes],
        in_specs=[whole(pltpu.SMEM)] * len(scalars) + [whole()] * len(arrays),
        out_specs=[whole()] * len(shapes),
        scratch_shapes=list(scratch),
        compiler_params=pltpu.CompilerParams(vmem_limit_bytes=24 * 2**20),
    )(*scalars, *arrays)


def outgoing(place, readers, pattern, total):
    count, block = total.shape[:2]

    def kernel(place_ref, readers_ref, pattern_ref, total_ref, out_ref):
        for d in range(count):
            for j, k in enumerate((d, readers_ref[d])):
                value = total_ref[place_ref[k]].astype(F32) * pattern_ref[k].astype(F32)
                out_ref[d, j] = (-value).astype(out_ref.dtype)

    return small_call(
        kernel,
        [((count, 2, block, block), jnp.bfloat16)],
        [place, readers, pattern],
        [total],
    )[0]


def finish_rows(pattern, back, parent_panels, masked_one, masked_two, lead, second):
    count, _, block, _ = back.shape
    width = count * block
    kind = back.dtype

    def over(a, b):
        return lax.dot_general(a, b, (((1,), (1,)), ((), ())), preferred_element_type=F32)

    def kernel(
        pattern_ref, back_ref, panels_ref, one_ref, two_ref, lead_ref, *refs
    ):
        terms = [refs[: len(second) // 2], refs[len(second) // 2 : len(second)]]
        rows_one_ref, rows_two_ref, sums_ref, chosen, panels = refs[len(second) :]
        for i in range(count):
            part = pl.ds(i * block, block)
            rows_one_ref[:, part] = back_ref[i, 0]
            chosen[:, part] = back_ref[i, 1]
            panels[:, part] = panels_ref[i]
        for i in range(count):
            part = pl.ds(i * block, block)
            side, first = i * 2 // count, i % (count // 2) * block
            total = jnp.dot(lead_ref[...], chosen[:, part], preferred_element_type=F32)
            for ref in terms[side]:
                total = total + ref[:, first : first + block].astype(F32)
            rows_two_ref[:, part] = (-(total * pattern_ref[0, i].astype(F32))).astype(kind)
        sums_ref[0] = over(one_ref[...], rows_one_ref[...])
        sums_ref[1] = over(two_ref[...], chosen[...])
        sums_ref[2] = over(panels[...], chosen[...])
        sums_ref[3] = over(two_ref[...], rows_two_ref[...])

    return small_call(
        kernel,
        [((block, width), kind), ((block, width), kind), ((4, block, block), F32)],
        [pattern],
        [back, parent_panels, masked_one, masked_two, lead, *second],
        [pltpu.VMEM((block, width), kind), pltpu.VMEM((block, width), kind)],
    )


def finish_blocks(z, parts, own_diag, parent_diag, two_diag, lead):
    block = lead.shape[0]

    def kernel(z_ref, a, b, c, d, own_ref, parent_ref, two_ref, lead_ref, one_out, lead_out, two_out, sums):
        held = (a, b, c, d)
        for k in range(SIDE):

            @pl.when(z_ref[0] == k)
            def _():
                w = [held[(i - k) % SIDE][...].astype(F32) for i in range(SIDE)]
                sums[...] = (w[0] + w[1]) + (w[2] + w[3])

        one_out[...] = own_ref[...] - sums[0]
        lead_wide = lead_ref[...].astype(F32)
        found = -(
            sums[1]
            + jnp.dot(
                lead_wide,
                parent_ref[...] - sums[2],
                precision=lax.Precision.HIGHEST,
                preferred_element_type=F32,
            )
        )
        lead_out[...] = found
        two_out[...] = (
            two_ref[...]
            - sums[3]
            - lax.dot_general(
                lead_wide,
                found,
                (((1,), (1,)), ((), ())),
                precision=lax.Precision.HIGHEST,
                preferred_element_type=F32,
            )
        )

    return small_call(
        kernel,
        [((block, block), F32)] * 3,
        [z],
        [*parts, own_diag, parent_diag, two_diag, lead],
        [pltpu.VMEM((4, block, block), F32)],
    )


def per_device(
    ancestor_inverse,
    level_one_panels,
    level_one_pattern,
    level_one_diag,
    level_two_panels,
    level_two_pattern,
    parent_lead,
    level_two_diag,
    parents,
):
    block = level_one_diag.shape[1]
    bf16 = jnp.bfloat16
    col = lax.axis_index("col")
    x, y = col % SIDE, col // SIDE
    count = SIDE * SIDE
    span, width = ancestor_inverse.shape
    masked_one = apply_pattern(level_one_panels, level_one_pattern, block)
    masked_two = apply_pattern(level_two_panels, level_two_pattern, block)

    found_one = all_panels(in_order([turned_panels(masked_one, k) for k in range(2)]))
    later_two, _ = lax.optimization_barrier((masked_two, found_one[2:6:2]))
    early_two = turned_panels(later_two, 0)
    early_two, found_one = lax.optimization_barrier((early_two, found_one))
    product_one = by_column(found_one, ancestor_inverse, block)
    later_two, product_one = lax.optimization_barrier((masked_two, product_one))
    own_two = in_order([early_two, turned_panels(later_two, 1)])
    later_one, own_two = lax.optimization_barrier((masked_one, own_two))
    first_sum = lax.psum_scatter(
        product_one.reshape(count * count * block, block), "col", scatter_dimension=0, tiled=True
    ).reshape(count, block, block)

    facts = jnp.concatenate(
        [
            jnp.broadcast_to(level_one_pattern.reshape(count, 1, 1), (count, 8, block)),
            jnp.broadcast_to(parents.reshape(1, 1, 1), (count, 8, block)),
        ],
        1,
    ).astype(bf16)
    cut = jnp.swapaxes(later_one.reshape(block, count, block), 0, 1)
    cut = lax.all_to_all(jnp.concatenate([cut, facts], 1), "col", 0, 0, tiled=True)
    cut_pattern = cut[:, block, 0].astype(jnp.int32)
    readers = cut[:, block + 8, 0].astype(jnp.int32)
    parent_panels = lax.all_to_all(
        jnp.take(cut[:, :block], readers, axis=0), "col", 0, 0, tiled=True
    )
    rows_two = lax.all_gather(own_two, "row", axis=0, tiled=True)

    steps = jnp.arange(count, dtype=jnp.int32)
    place = arrival(steps)
    outer, inner = steps // SIDE, steps % SIDE
    x_major = (y + inner) % SIDE * SIDE + (x + outer) % SIDE
    y_major = (y + outer) % SIDE * SIDE + (x + inner) % SIDE

    order = jnp.stack([x_major, y_major])
    low_a, high_a, low_b, high_b = ring_far(order, rows_two, ancestor_inverse)
    first_a = send(low_a, x_step(1)), send(high_a, x_step(-1))
    first_b = send(low_b, y_step(1)), send(high_b, y_step(-1))
    near = ring_near(order, rows_two, ancestor_inverse)
    first_a, first_b, parent_panels = lax.optimization_barrier((first_a, first_b, parent_panels))
    second_a = second_sends(first_a, near[:3], x_step)
    second_b = second_sends(first_b, near[3:], y_step)
    going = outgoing(place, readers, cut_pattern, first_sum)
    back = lax.all_to_all(going, "col", 0, 0, tiled=True)
    second_a, second_b, _ = lax.optimization_barrier((second_a, second_b, going))
    second_sum = third_sends(second_a, near[:3], y_step) + third_sends(second_b, near[3:], x_step)
    level_one_rows, level_two_rows, sums = finish_rows(
        level_two_pattern, back, parent_panels, masked_one, masked_two, parent_lead, second_sum
    )

    diag_blocks = level_one_diag.reshape(count, block, block)
    level_one_inv, level_two_lead, level_two_inv = finish_blocks(
        (lax.axis_index("row") // CORES).reshape(1),
        row_parts(sums),
        lax.dynamic_index_in_dim(diag_blocks, col, 0, keepdims=False),
        lax.dynamic_index_in_dim(diag_blocks, parents[0], 0, keepdims=False),
        level_two_diag,
        parent_lead,
    )
    return level_one_rows, level_one_inv, level_two_rows, level_two_lead, level_two_inv


def solution(mesh):
    in_specs = (
        P("col", "row"),
        P("col", "row"),
        P("col", "row"),
        P(),
        P("col", "row"),
        P("col", "row"),
        P("col", None),
        P("col", None),
        P("col"),
    )
    out_specs = (P("col", "row"), P("col", None), P("col", "row"), P("col", None), P("col", None))
    return jax.shard_map(
        per_device, mesh=mesh, in_specs=in_specs, out_specs=out_specs, check_vma=False
    )
```

```python
import jax
import jax.numpy as jnp
from jax import lax
from jax.experimental import pallas as pl
from jax.experimental.pallas import tpu as pltpu
from jax.sharding import PartitionSpec as P

SIDE = 4
CORES = 2
F32 = jnp.float32
LONG_CHAIN = 10**11
RING_VMEM = 52 * 2**20


def x_step(d):
    return [(y * SIDE + x, y * SIDE + (x + d) % SIDE) for y in range(SIDE) for x in range(SIDE)]


def y_step(d):
    return [(y * SIDE + x, (y + d) % SIDE * SIDE + x) for y in range(SIDE) for x in range(SIDE)]


def z_step(d):
    return [(z * CORES + e, (z + d) % SIDE * CORES + e) for z in range(SIDE) for e in range(CORES)]


CORE_SWAP = [(i, i ^ 1) for i in range(SIDE * CORES)]


def turn(k):
    cols, rows = SIDE * SIDE, SIDE * CORES
    return [
        (r * cols + c, c // 2 * cols + 2 * r + (c + k) % 2) for r in range(rows) for c in range(cols)
    ]


def apply_pattern(panels, pattern, block):
    count, blocks = pattern.shape
    shaped = panels.reshape(count, block, blocks, block)
    return (shaped * pattern.astype(panels.dtype)[:, None, :, None]).reshape(panels.shape)


def turned_panels(masked, k):
    col = lax.axis_index("col")
    half = masked.shape[1] // 2
    part = lax.dynamic_slice_in_dim(masked, (col + k) % 2 * half, half, 1)
    return lax.ppermute(part, ("row", "col"), turn(k))


def in_order(pieces):
    even = lax.axis_index("col") % 2 == 0
    return jnp.stack(
        [jnp.where(even, pieces[0], pieces[1]), jnp.where(even, pieces[1], pieces[0])]
    )


def all_panels(own):
    below = lax.ppermute(own, "row", z_step(1))
    above = lax.ppermute(own, "row", z_step(-1))
    far = jnp.stack(
        [lax.ppermute(below[0], "row", z_step(1)), lax.ppermute(above[1], "row", z_step(-1))]
    )
    found = []
    for held in (own, below, above, far):
        found += [held, lax.ppermute(held, "row", CORE_SWAP)]
    return found


def arrival(supernode):
    row = lax.axis_index("row")
    z, core = row // CORES, row % CORES
    source = supernode // 2
    slot = jnp.array([0, 2, 3, 1], jnp.int32)[(source // CORES - z) % SIDE]
    return slot * 4 + (source + core) % CORES * 2 + supernode % 2


def by_column(pieces, matrix, block):
    rows, depth = pieces[0].shape[0] * pieces[0].shape[1], pieces[0].shape[2]
    width = matrix.shape[1]
    steps = len(pieces)

    def kernel(*refs):
        matrix_ref, out_ref, held = refs[steps:]
        for i in range(steps):

            @pl.when(pl.program_id(0) == i)
            def _():
                held[...] = refs[i][...].reshape(rows, depth)

        total = jnp.dot(held[...], matrix_ref[...], preferred_element_type=F32)
        for d in range(width // block):
            out_ref[d] = total[:, d * block : (d + 1) * block].astype(out_ref.dtype)

    return pl.pallas_call(
        kernel,
        out_shape=jax.ShapeDtypeStruct((width // block, steps * rows, block), matrix.dtype),
        grid=(steps,),
        in_specs=[pl.BlockSpec(v.shape, lambda i: (0, 0, 0)) for v in pieces]
        + [pl.BlockSpec((depth, width), lambda i: (0, 0))],
        out_specs=pl.BlockSpec((width // block, rows, block), lambda i: (0, i, 0)),
        scratch_shapes=[pltpu.VMEM((rows, depth), matrix.dtype)],
        compiler_params=pltpu.CompilerParams(vmem_limit_bytes=52 * 2**20),
        cost_estimate=pl.CostEstimate(
            flops=2 * steps * rows * depth * width,
            bytes_accessed=2 * (steps * rows * (depth + width) + depth * width),
            transcendentals=0,
        ),
    )(*pieces, matrix)


def by_supernode(order, rows, matrix, part, split):
    block, depth = rows.shape[1:]
    width = matrix.shape[1] // 2
    groups = order.shape[0] // SIDE
    outs = 2 if split else 1
    size = block // outs

    def kernel(order_ref, a_ref, b_ref, c_ref, d_ref, matrix_ref, *out):
        left = jnp.concatenate([a_ref[0], b_ref[0], c_ref[0], d_ref[0]], 0)
        total = jnp.dot(left, matrix_ref[...], preferred_element_type=F32)
        total = total.reshape(SIDE, block, width)
        for i, ref in enumerate(out):
            ref[0] = total[:, i * size : (i + 1) * size].astype(ref.dtype)

    def pick(j):
        return pl.BlockSpec((1, block, depth), lambda i, order_ref: (order_ref[SIDE * i + j], 0, 0))

    return pl.pallas_call(
        kernel,
        out_shape=[jax.ShapeDtypeStruct((groups, SIDE, size, width), rows.dtype)] * outs,
        grid_spec=pltpu.PrefetchScalarGridSpec(
            num_scalar_prefetch=1,
            grid=(groups,),
            in_specs=[pick(j) for j in range(SIDE)]
            + [pl.BlockSpec((depth, width), lambda i, order_ref: (0, part))],
            out_specs=[pl.BlockSpec((1, SIDE, size, width), lambda i, order_ref: (i, 0, 0, 0))]
            * outs,
        ),
        compiler_params=pltpu.CompilerParams(vmem_limit_bytes=RING_VMEM),
        cost_estimate=pl.CostEstimate(
            flops=2 * groups * SIDE * block * depth * width,
            bytes_accessed=2 * groups * SIDE * block * (depth + width),
            transcendentals=0,
        ),
    )(order, rows, rows, rows, rows, matrix)


def send(value, step):
    return lax.ppermute(value, "col", step)


def second_sends(arriving, near, step):
    _, _, block, width = near.shape
    half = block // 2

    def kernel(low_ref, high_ref, ahead_ref, behind_ref, ahead_out, behind_out):
        kind = ahead_out.dtype
        low = ahead_ref[0, 0, :half].astype(F32) + low_ref[0].astype(F32)
        high = behind_ref[0, 0, half:].astype(F32) + high_ref[0].astype(F32)
        ahead_out[0, :half] = low.astype(kind)
        ahead_out[0, half:] = ahead_ref[0, 0, half:]
        behind_out[0, :half] = behind_ref[0, 0, :half]
        behind_out[0, half:] = high.astype(kind)

    part = pl.BlockSpec((1, half, width), lambda i: (i, 0, 0))
    own = [pl.BlockSpec((1, 1, block, width), lambda i, g=g: (g, i, 0, 0)) for g in range(2)]
    full = pl.BlockSpec((1, block, width), lambda i: (i, 0, 0))
    ahead, behind = pl.pallas_call(
        kernel,
        out_shape=[jax.ShapeDtypeStruct((SIDE, block, width), near.dtype)] * 2,
        grid=(SIDE,),
        in_specs=[part, part, *own],
        out_specs=[full, full],
        compiler_params=pltpu.CompilerParams(vmem_limit_bytes=RING_VMEM),
        cost_estimate=pl.CostEstimate(flops=0, bytes_accessed=2**22, transcendentals=0),
    )(*arriving, near, near)
    return send(ahead, step(1)), send(behind, step(-1))


def third_sends(arriving, near, step):
    _, _, block, width = near.shape
    kind = near.dtype
    tile = width // SIDE

    def kernel(one_ref, two_ref, own_ref, own_out, *out):
        for d in range(SIDE):
            total = own_ref[0, d].astype(F32) + one_ref[d].astype(F32) + two_ref[d].astype(F32)
            if d:
                out[d - 1][...] = total.astype(kind)
            else:
                own_out[...] = total

    four = pl.BlockSpec((SIDE, block, tile), lambda i: (0, 0, i))
    one = pl.BlockSpec((block, tile), lambda i: (0, i))
    own, *others = pl.pallas_call(
        kernel,
        out_shape=[jax.ShapeDtypeStruct((block, width), F32)]
        + [jax.ShapeDtypeStruct((block, width), kind)] * 3,
        grid=(SIDE,),
        in_specs=[four, four, pl.BlockSpec((1, SIDE, block, tile), lambda i: (2, 0, 0, i))],
        out_specs=[one] * 4,
        compiler_params=pltpu.CompilerParams(vmem_limit_bytes=RING_VMEM),
        cost_estimate=pl.CostEstimate(flops=0, bytes_accessed=2**22, transcendentals=0),
    )(*arriving, near)
    return [own] + [send(v, step(d + 1)) for d, v in enumerate(others)]


def row_parts(values):
    values = values + lax.ppermute(values, "row", CORE_SWAP)
    values = values.astype(jnp.bfloat16)
    return [values] + [lax.ppermute(values, "row", z_step(-d)) for d in range(1, SIDE)]


def whole(shape):
    return pl.BlockSpec(shape, lambda i: (0,) * len(shape))


def small_call(kernel, shapes, scalars, arrays, scratch=(), flops=0):
    return pl.pallas_call(
        kernel,
        out_shape=[jax.ShapeDtypeStruct(shape, kind) for shape, kind in shapes],
        grid=(1,),
        in_specs=[pl.BlockSpec(memory_space=pltpu.SMEM)] * len(scalars)
        + [whole(v.shape) for v in arrays],
        out_specs=[whole(shape) for shape, _ in shapes],
        scratch_shapes=list(scratch),
        compiler_params=pltpu.CompilerParams(vmem_limit_bytes=RING_VMEM),
        cost_estimate=pl.CostEstimate(flops=flops, bytes_accessed=2**20, transcendentals=0),
    )(*scalars, *arrays)


def outgoing(place, readers, pattern, total):
    count, block = total.shape[:2]

    def kernel(place_ref, readers_ref, pattern_ref, total_ref, out_ref):
        for d in range(count):
            for j, k in enumerate((d, readers_ref[d])):
                value = total_ref[place_ref[k]].astype(F32) * pattern_ref[k].astype(F32)
                out_ref[d, j] = (-value).astype(out_ref.dtype)

    return small_call(
        kernel,
        [((count, 2, block, block), jnp.bfloat16)],
        [place, readers, pattern],
        [total],
        flops=LONG_CHAIN,
    )[0]


def finish_rows(pattern, back, parent_panels, masked_one, masked_two, lead, second):
    count, _, block, _ = back.shape
    width = count * block
    kind = back.dtype

    def over(a, b):
        return lax.dot_general(a, b, (((1,), (1,)), ((), ())), preferred_element_type=F32)

    def kernel(
        pattern_ref, back_ref, panels_ref, one_ref, two_ref, lead_ref, *refs
    ):
        terms = [refs[: len(second) // 2], refs[len(second) // 2 : len(second)]]
        rows_one_ref, rows_two_ref, sums_ref, chosen, panels = refs[len(second) :]
        for i in range(count):
            part = pl.ds(i * block, block)
            rows_one_ref[:, part] = back_ref[i, 0]
            chosen[:, part] = back_ref[i, 1]
            panels[:, part] = panels_ref[i]
        for i in range(count):
            part = pl.ds(i * block, block)
            side, first = i * 2 // count, i % (count // 2) * block
            total = jnp.dot(lead_ref[...], chosen[:, part], preferred_element_type=F32)
            for ref in terms[side]:
                total = total + ref[:, first : first + block].astype(F32)
            rows_two_ref[:, part] = (-(total * pattern_ref[0, i].astype(F32))).astype(kind)
        sums_ref[0] = over(one_ref[...], rows_one_ref[...])
        sums_ref[1] = over(two_ref[...], chosen[...])
        sums_ref[2] = over(panels[...], chosen[...])
        sums_ref[3] = over(two_ref[...], rows_two_ref[...])

    return small_call(
        kernel,
        [((block, width), kind), ((block, width), kind), ((4, block, block), F32)],
        [pattern],
        [back, parent_panels, masked_one, masked_two, lead, *second],
        [pltpu.VMEM((block, width), kind), pltpu.VMEM((block, width), kind)],
    )


def finish_blocks(z, parts, own_diag, parent_diag, two_diag, lead):
    block = lead.shape[0]

    def kernel(z_ref, a, b, c, d, own_ref, parent_ref, two_ref, lead_ref, one_out, lead_out, two_out, sums):
        held = (a, b, c, d)
        for k in range(SIDE):

            @pl.when(z_ref[0] == k)
            def _():
                w = [held[(i - k) % SIDE][...].astype(F32) for i in range(SIDE)]
                sums[...] = (w[0] + w[1]) + (w[2] + w[3])

        one_out[...] = own_ref[...] - sums[0]
        lead_wide = lead_ref[...].astype(F32)
        found = -(
            sums[1]
            + jnp.dot(
                lead_wide,
                parent_ref[...] - sums[2],
                precision=lax.Precision.HIGHEST,
                preferred_element_type=F32,
            )
        )
        lead_out[...] = found
        two_out[...] = (
            two_ref[...]
            - sums[3]
            - lax.dot_general(
                lead_wide,
                found,
                (((1,), (1,)), ((), ())),
                precision=lax.Precision.HIGHEST,
                preferred_element_type=F32,
            )
        )

    return small_call(
        kernel,
        [((block, block), F32)] * 3,
        [z],
        [*parts, own_diag, parent_diag, two_diag, lead],
        [pltpu.VMEM((4, block, block), F32)],
    )


def per_device(
    ancestor_inverse,
    level_one_panels,
    level_one_pattern,
    level_one_diag,
    level_two_panels,
    level_two_pattern,
    parent_lead,
    level_two_diag,
    parents,
):
    block = level_one_diag.shape[1]
    bf16 = jnp.bfloat16
    col = lax.axis_index("col")
    x, y = col % SIDE, col // SIDE
    count = SIDE * SIDE
    span, width = ancestor_inverse.shape
    masked_one = apply_pattern(level_one_panels, level_one_pattern, block)
    masked_two = apply_pattern(level_two_panels, level_two_pattern, block)

    found_one = all_panels(in_order([turned_panels(masked_one, k) for k in range(2)]))
    later_two, _ = lax.optimization_barrier((masked_two, found_one[2:6:2]))
    early_two = turned_panels(later_two, 0)
    early_two, found_one = lax.optimization_barrier((early_two, found_one))
    product_one = by_column(found_one, ancestor_inverse, block)
    later_two, product_one = lax.optimization_barrier((masked_two, product_one))
    own_two = in_order([early_two, turned_panels(later_two, 1)])
    later_one, own_two = lax.optimization_barrier((masked_one, own_two))
    first_sum = lax.psum_scatter(
        product_one.reshape(count * count * block, block), "col", scatter_dimension=0, tiled=True
    ).reshape(count, block, block)

    facts = jnp.concatenate(
        [
            jnp.broadcast_to(level_one_pattern.reshape(count, 1, 1), (count, 8, block)),
            jnp.broadcast_to(parents.reshape(1, 1, 1), (count, 8, block)),
        ],
        1,
    ).astype(bf16)
    cut = jnp.swapaxes(later_one.reshape(block, count, block), 0, 1)
    cut = lax.all_to_all(jnp.concatenate([cut, facts], 1), "col", 0, 0, tiled=True)
    cut_pattern = cut[:, block, 0].astype(jnp.int32)
    readers = cut[:, block + 8, 0].astype(jnp.int32)
    parent_panels = lax.all_to_all(
        jnp.take(cut[:, :block], readers, axis=0), "col", 0, 0, tiled=True
    )
    rows_two = lax.all_gather(own_two, "row", axis=0, tiled=True)

    steps = jnp.arange(count, dtype=jnp.int32)
    place = arrival(steps)
    outer, inner = steps // SIDE, steps % SIDE
    x_major = (y + inner) % SIDE * SIDE + (x + outer) % SIDE
    y_major = (y + outer) % SIDE * SIDE + (x + inner) % SIDE

    def ring(order, part, step):
        order = order.reshape(SIDE, -1)
        low, high = by_supernode(order[2], rows_two, ancestor_inverse, part, True)
        arriving = send(low[0], step(1)), send(high[0], step(-1))
        rest = jnp.concatenate([order[1], order[3], order[0]])
        return arriving, by_supernode(rest, rows_two, ancestor_inverse, part, False)[0]

    first_a, near_a = ring(x_major, 0, x_step)
    first_b, near_b = ring(y_major, 1, y_step)
    first_a, first_b, parent_panels = lax.optimization_barrier((first_a, first_b, parent_panels))
    second_a = second_sends(first_a, near_a, x_step)
    second_b = second_sends(first_b, near_b, y_step)
    going = outgoing(place, readers, cut_pattern, first_sum)
    back = lax.all_to_all(going, "col", 0, 0, tiled=True)
    second_a, second_b, _ = lax.optimization_barrier((second_a, second_b, going))
    second_sum = third_sends(second_a, near_a, y_step) + third_sends(second_b, near_b, x_step)
    level_one_rows, level_two_rows, sums = finish_rows(
        level_two_pattern, back, parent_panels, masked_one, masked_two, parent_lead, second_sum
    )

    diag_blocks = level_one_diag.reshape(count, block, block)
    level_one_inv, level_two_lead, level_two_inv = finish_blocks(
        (lax.axis_index("row") // CORES).reshape(1),
        row_parts(sums),
        lax.dynamic_index_in_dim(diag_blocks, col, 0, keepdims=False),
        lax.dynamic_index_in_dim(diag_blocks, parents[0], 0, keepdims=False),
        level_two_diag,
        parent_lead,
    )
    return level_one_rows, level_one_inv, level_two_rows, level_two_lead, level_two_inv


def solution(mesh):
    in_specs = (
        P("col", "row"),
        P("col", "row"),
        P("col", "row"),
        P(),
        P("col", "row"),
        P("col", "row"),
        P("col", None),
        P("col", None),
        P("col"),
    )
    out_specs = (P("col", "row"), P("col", None), P("col", "row"), P("col", None), P("col", None))
    return jax.shard_map(
        per_device, mesh=mesh, in_specs=in_specs, out_specs=out_specs, check_vma=False
    )
```

```python
import jax
import jax.numpy as jnp
from jax import lax
from jax.experimental import pallas as pl
from jax.experimental.pallas import tpu as pltpu
from jax.sharding import PartitionSpec as P

SIDE = 4
CORES = 2
F32 = jnp.float32
RING_VMEM = 52 * 2**20


def x_step(d):
    return [(y * SIDE + x, y * SIDE + (x + d) % SIDE) for y in range(SIDE) for x in range(SIDE)]


def y_step(d):
    return [(y * SIDE + x, (y + d) % SIDE * SIDE + x) for y in range(SIDE) for x in range(SIDE)]


def z_step(d):
    return [(z * CORES + e, (z + d) % SIDE * CORES + e) for z in range(SIDE) for e in range(CORES)]


CORE_SWAP = [(i, i ^ 1) for i in range(SIDE * CORES)]


def turn(k):
    cols, rows = SIDE * SIDE, SIDE * CORES
    return [
        (r * cols + c, c // 2 * cols + 2 * r + (c + k) % 2) for r in range(rows) for c in range(cols)
    ]


def apply_pattern(panels, pattern, block):
    count, blocks = pattern.shape
    shaped = panels.reshape(count, block, blocks, block)
    return (shaped * pattern.astype(panels.dtype)[:, None, :, None]).reshape(panels.shape)


def turned_panels(masked, k):
    col = lax.axis_index("col")
    half = masked.shape[1] // 2
    part = lax.dynamic_slice_in_dim(masked, (col + k) % 2 * half, half, 1)
    return lax.ppermute(part, ("row", "col"), turn(k))


def in_order(pieces):
    even = lax.axis_index("col") % 2 == 0
    return jnp.stack(
        [jnp.where(even, pieces[0], pieces[1]), jnp.where(even, pieces[1], pieces[0])]
    )


def all_panels(own):
    below = lax.ppermute(own, "row", z_step(1))
    above = lax.ppermute(own, "row", z_step(-1))
    far = jnp.stack(
        [lax.ppermute(below[0], "row", z_step(1)), lax.ppermute(above[1], "row", z_step(-1))]
    )
    found = []
    for held in (own, below, above, far):
        found += [held, lax.ppermute(held, "row", CORE_SWAP)]
    return found


def arrival(supernode):
    row = lax.axis_index("row")
    z, core = row // CORES, row % CORES
    source = supernode // 2
    slot = jnp.array([0, 2, 3, 1], jnp.int32)[(source // CORES - z) % SIDE]
    return slot * 4 + (source + core) % CORES * 2 + supernode % 2


def by_column(order, pieces, matrix, split):
    block, depth = pieces[0].shape[1:]
    each = 2 * block
    rows = len(pieces) * each
    groups = order.shape[0] // SIDE
    outs = 2 if split else 1
    size = rows // outs

    def kernel(order_ref, *refs):
        right = jnp.concatenate([ref[...] for ref in refs[:SIDE]], 1)
        held, out = refs[SIDE : SIDE + len(pieces)], refs[SIDE + len(pieces) :]
        for i, piece in enumerate(held):
            left = piece[...].reshape(each, depth)
            total = jnp.dot(left, right, preferred_element_type=F32)
            ref, first = out[i * each // size], i * each % size
            for j in range(SIDE):
                ref[0, j, first : first + each] = total[:, j * block : (j + 1) * block].astype(ref.dtype)

    def pick(j):
        return pl.BlockSpec((depth, block), lambda i, order_ref: (0, order_ref[SIDE * i + j]))

    return pl.pallas_call(
        kernel,
        out_shape=[jax.ShapeDtypeStruct((groups, SIDE, size, block), matrix.dtype)] * outs,
        grid_spec=pltpu.PrefetchScalarGridSpec(
            num_scalar_prefetch=1,
            grid=(groups,),
            in_specs=[pick(j) for j in range(SIDE)]
            + [pl.BlockSpec(v.shape, lambda i, order_ref: (0, 0, 0)) for v in pieces],
            out_specs=[pl.BlockSpec((1, SIDE, size, block), lambda i, order_ref: (i, 0, 0, 0))]
            * outs,
        ),
        compiler_params=pltpu.CompilerParams(vmem_limit_bytes=RING_VMEM),
        cost_estimate=pl.CostEstimate(
            flops=2 * groups * SIDE * block * depth * rows,
            bytes_accessed=2 * groups * SIDE * block * (depth + rows),
            transcendentals=0,
        ),
    )(order, *[matrix] * SIDE, *pieces)


def by_supernode(order, rows, matrix, part, split):
    block, depth = rows.shape[1:]
    width = matrix.shape[1] // 2
    groups = order.shape[0] // SIDE
    outs = 2 if split else 1
    size = block // outs

    def kernel(order_ref, a_ref, b_ref, c_ref, d_ref, matrix_ref, *out):
        left = jnp.concatenate([a_ref[0], b_ref[0], c_ref[0], d_ref[0]], 0)
        total = jnp.dot(left, matrix_ref[...], preferred_element_type=F32)
        total = total.reshape(SIDE, block, width)
        for i, ref in enumerate(out):
            ref[0] = total[:, i * size : (i + 1) * size].astype(ref.dtype)

    def pick(j):
        return pl.BlockSpec((1, block, depth), lambda i, order_ref: (order_ref[SIDE * i + j], 0, 0))

    return pl.pallas_call(
        kernel,
        out_shape=[jax.ShapeDtypeStruct((groups, SIDE, size, width), rows.dtype)] * outs,
        grid_spec=pltpu.PrefetchScalarGridSpec(
            num_scalar_prefetch=1,
            grid=(groups,),
            in_specs=[pick(j) for j in range(SIDE)]
            + [pl.BlockSpec((depth, width), lambda i, order_ref: (0, part))],
            out_specs=[pl.BlockSpec((1, SIDE, size, width), lambda i, order_ref: (i, 0, 0, 0))]
            * outs,
        ),
        compiler_params=pltpu.CompilerParams(vmem_limit_bytes=RING_VMEM),
        cost_estimate=pl.CostEstimate(
            flops=2 * groups * SIDE * block * depth * width,
            bytes_accessed=2 * groups * SIDE * block * (depth + width),
            transcendentals=0,
        ),
    )(order, rows, rows, rows, rows, matrix)


def send(value, step):
    return lax.ppermute(value, "col", step)


def second_sends(arriving, near, step):
    _, _, block, width = near.shape
    half = block // 2

    def kernel(low_ref, high_ref, ahead_ref, behind_ref, ahead_out, behind_out):
        kind = ahead_out.dtype
        low = ahead_ref[0, 0, :half].astype(F32) + low_ref[0].astype(F32)
        high = behind_ref[0, 0, half:].astype(F32) + high_ref[0].astype(F32)
        ahead_out[0, :half] = low.astype(kind)
        ahead_out[0, half:] = ahead_ref[0, 0, half:]
        behind_out[0, :half] = behind_ref[0, 0, :half]
        behind_out[0, half:] = high.astype(kind)

    part = pl.BlockSpec((1, half, width), lambda i: (i, 0, 0))
    own = [pl.BlockSpec((1, 1, block, width), lambda i, g=g: (g, i, 0, 0)) for g in range(2)]
    full = pl.BlockSpec((1, block, width), lambda i: (i, 0, 0))
    ahead, behind = pl.pallas_call(
        kernel,
        out_shape=[jax.ShapeDtypeStruct((SIDE, block, width), near.dtype)] * 2,
        grid=(SIDE,),
        in_specs=[part, part, *own],
        out_specs=[full, full],
        compiler_params=pltpu.CompilerParams(vmem_limit_bytes=RING_VMEM),
        cost_estimate=pl.CostEstimate(flops=0, bytes_accessed=2**22, transcendentals=0),
    )(*arriving, near, near)
    return send(ahead, step(1)), send(behind, step(-1))


def third_sends(arriving, near, step):
    _, _, block, width = near.shape
    kind = near.dtype
    tile = block // SIDE

    def kernel(one_ref, two_ref, own_ref, own_out, *out):
        for d in range(SIDE):
            total = own_ref[0, d].astype(F32) + one_ref[d].astype(F32) + two_ref[d].astype(F32)
            if d:
                out[d - 1][...] = total.astype(kind)
            else:
                own_out[...] = total

    four = pl.BlockSpec((SIDE, tile, width), lambda i: (0, i, 0))
    one = pl.BlockSpec((tile, width), lambda i: (i, 0))
    own, *others = pl.pallas_call(
        kernel,
        out_shape=[jax.ShapeDtypeStruct((block, width), F32)]
        + [jax.ShapeDtypeStruct((block, width), kind)] * 3,
        grid=(SIDE,),
        in_specs=[four, four, pl.BlockSpec((1, SIDE, tile, width), lambda i: (2, 0, i, 0))],
        out_specs=[one] * 4,
        compiler_params=pltpu.CompilerParams(vmem_limit_bytes=RING_VMEM),
        cost_estimate=pl.CostEstimate(flops=0, bytes_accessed=2**22, transcendentals=0),
    )(*arriving, near)
    return [own] + [send(v, step(d + 1)) for d, v in enumerate(others)]


def row_parts(values):
    values = values + lax.ppermute(values, "row", CORE_SWAP)
    values = values.astype(jnp.bfloat16)
    return [values] + [lax.ppermute(values, "row", z_step(-d)) for d in range(1, SIDE)]


def whole(shape):
    return pl.BlockSpec(shape, lambda i: (0,) * len(shape))


def small_call(kernel, shapes, scalars, arrays, scratch=()):
    return pl.pallas_call(
        kernel,
        out_shape=[jax.ShapeDtypeStruct(shape, kind) for shape, kind in shapes],
        grid=(1,),
        in_specs=[pl.BlockSpec(memory_space=pltpu.SMEM)] * len(scalars)
        + [whole(v.shape) for v in arrays],
        out_specs=[whole(shape) for shape, _ in shapes],
        scratch_shapes=list(scratch),
        compiler_params=pltpu.CompilerParams(vmem_limit_bytes=RING_VMEM),
        cost_estimate=pl.CostEstimate(flops=0, bytes_accessed=2**20, transcendentals=0),
    )(*scalars, *arrays)


def outgoing(place, readers, pattern, terms):
    count = place.shape[0]
    block = terms[0].shape[1]
    middle = count // 2

    def kernel(place_ref, readers_ref, pattern_ref, *refs):
        out_ref, total = refs[len(terms) :]
        half = len(terms) // 2
        for side in range(2):
            value = sum(ref[...].astype(F32) for ref in refs[side * half : (side + 1) * half])
            total[side * middle : (side + 1) * middle] = value.reshape(middle, block, block)
        for d in range(count):
            for j, k in enumerate((d, readers_ref[d])):
                value = total[place_ref[k]] * pattern_ref[k].astype(F32)
                out_ref[d, j] = (-value).astype(out_ref.dtype)

    return small_call(
        kernel,
        [((count, 2, block, block), jnp.bfloat16)],
        [place, readers, pattern],
        terms,
        [pltpu.VMEM((count, block, block), F32)],
    )[0]


def finish_rows(pattern, back, parent_panels, masked_one, masked_two, lead, second):
    count, _, block, _ = back.shape
    width = count * block
    kind = back.dtype

    def over(a, b):
        return lax.dot_general(a, b, (((1,), (1,)), ((), ())), preferred_element_type=F32)

    def kernel(
        pattern_ref, back_ref, panels_ref, one_ref, two_ref, lead_ref, *refs
    ):
        terms = [refs[: len(second) // 2], refs[len(second) // 2 : len(second)]]
        rows_one_ref, rows_two_ref, sums_ref, chosen, panels = refs[len(second) :]
        for i in range(count):
            part = pl.ds(i * block, block)
            rows_one_ref[:, part] = back_ref[i, 0]
            chosen[:, part] = back_ref[i, 1]
            panels[:, part] = panels_ref[i]
        for i in range(count):
            part = pl.ds(i * block, block)
            side, first = i * 2 // count, i % (count // 2) * block
            total = jnp.dot(lead_ref[...], chosen[:, part], preferred_element_type=F32)
            for ref in terms[side]:
                total = total + ref[:, first : first + block].astype(F32)
            rows_two_ref[:, part] = (-(total * pattern_ref[0, i].astype(F32))).astype(kind)
        sums_ref[0] = over(one_ref[...], rows_one_ref[...])
        sums_ref[1] = over(two_ref[...], chosen[...])
        sums_ref[2] = over(panels[...], chosen[...])
        sums_ref[3] = over(two_ref[...], rows_two_ref[...])

    return small_call(
        kernel,
        [((block, width), kind), ((block, width), kind), ((4, block, block), F32)],
        [pattern],
        [back, parent_panels, masked_one, masked_two, lead, *second],
        [pltpu.VMEM((block, width), kind), pltpu.VMEM((block, width), kind)],
    )


def finish_blocks(z, parts, own_diag, parent_diag, two_diag, lead):
    block = lead.shape[0]

    def kernel(z_ref, a, b, c, d, own_ref, parent_ref, two_ref, lead_ref, one_out, lead_out, two_out, sums):
        held = (a, b, c, d)
        for k in range(SIDE):

            @pl.when(z_ref[0] == k)
            def _():
                w = [held[(i - k) % SIDE][...].astype(F32) for i in range(SIDE)]
                sums[...] = (w[0] + w[1]) + (w[2] + w[3])

        one_out[...] = own_ref[...] - sums[0]
        lead_wide = lead_ref[...].astype(F32)
        found = -(
            sums[1]
            + jnp.dot(
                lead_wide,
                parent_ref[...] - sums[2],
                precision=lax.Precision.HIGHEST,
                preferred_element_type=F32,
            )
        )
        lead_out[...] = found
        two_out[...] = (
            two_ref[...]
            - sums[3]
            - lax.dot_general(
                lead_wide,
                found,
                (((1,), (1,)), ((), ())),
                precision=lax.Precision.HIGHEST,
                preferred_element_type=F32,
            )
        )

    return small_call(
        kernel,
        [((block, block), F32)] * 3,
        [z],
        [*parts, own_diag, parent_diag, two_diag, lead],
        [pltpu.VMEM((4, block, block), F32)],
    )


def per_device(
    ancestor_inverse,
    level_one_panels,
    level_one_pattern,
    level_one_diag,
    level_two_panels,
    level_two_pattern,
    parent_lead,
    level_two_diag,
    parents,
):
    block = level_one_diag.shape[1]
    bf16 = jnp.bfloat16
    col = lax.axis_index("col")
    x, y = col % SIDE, col // SIDE
    count = SIDE * SIDE
    span, width = ancestor_inverse.shape
    masked_one = apply_pattern(level_one_panels, level_one_pattern, block)
    masked_two = apply_pattern(level_two_panels, level_two_pattern, block)

    steps = jnp.arange(count, dtype=jnp.int32)
    place = arrival(steps)
    outer, inner = steps // SIDE, steps % SIDE
    x_major = (y + inner) % SIDE * SIDE + (x + outer) % SIDE
    y_major = (y + outer) % SIDE * SIDE + (x + inner) % SIDE

    def ring(product, order, step):
        order = order.reshape(SIDE, -1)
        low, high = product(order[2], True)
        arriving = send(low[0], step(1)), send(high[0], step(-1))
        return arriving, product(jnp.concatenate([order[1], order[3], order[0]]), False)[0]

    found_one = all_panels(in_order([turned_panels(masked_one, k) for k in range(2)]))
    later_two, found_one = lax.optimization_barrier((masked_two, found_one))
    own_two = in_order([turned_panels(later_two, k) for k in range(2)])

    def one_part(pieces):
        return lambda order, split: by_column(order, pieces, ancestor_inverse, split)

    first_a, near_a = ring(one_part(found_one[:4]), x_major, x_step)
    first_b, near_b = ring(one_part(found_one[4:]), y_major, y_step)
    first_a, first_b, own_two = lax.optimization_barrier((first_a, first_b, own_two))
    second_a = second_sends(first_a, near_a, x_step)
    second_b = second_sends(first_b, near_b, y_step)
    rows_two = jnp.concatenate(all_panels(own_two), 0)
    second_a, second_b, rows_two = lax.optimization_barrier((second_a, second_b, rows_two))
    first_sum = third_sends(second_a, near_a, y_step) + third_sends(second_b, near_b, x_step)

    later_one, _ = lax.optimization_barrier((masked_one, own_two))
    facts = jnp.concatenate(
        [
            jnp.broadcast_to(level_one_pattern.reshape(count, 1, 1), (count, 8, block)),
            jnp.broadcast_to(parents.reshape(1, 1, 1), (count, 8, block)),
        ],
        1,
    ).astype(bf16)
    cut = jnp.swapaxes(later_one.reshape(block, count, block), 0, 1)
    cut = lax.all_to_all(jnp.concatenate([cut, facts], 1), "col", 0, 0, tiled=True)
    cut_pattern = cut[:, block, 0].astype(jnp.int32)
    readers = cut[:, block + 8, 0].astype(jnp.int32)
    parent_panels = lax.all_to_all(
        jnp.take(cut[:, :block], readers, axis=0), "col", 0, 0, tiled=True
    )
    back = lax.all_to_all(
        outgoing(place, readers, cut_pattern, first_sum), "col", 0, 0, tiled=True
    )

    def two_part(part):
        return lambda order, split: by_supernode(
            place[order], rows_two, ancestor_inverse, part, split
        )

    first_a, near_a = ring(two_part(0), x_major, x_step)
    first_b, near_b = ring(two_part(1), y_major, y_step)
    second_a = second_sends(first_a, near_a, x_step)
    second_b = second_sends(first_b, near_b, y_step)
    second_a, second_b, back, parent_panels = lax.optimization_barrier(
        (second_a, second_b, back, parent_panels)
    )
    second_sum = third_sends(second_a, near_a, y_step) + third_sends(second_b, near_b, x_step)
    level_one_rows, level_two_rows, sums = finish_rows(
        level_two_pattern, back, parent_panels, masked_one, masked_two, parent_lead, second_sum
    )

    diag_blocks = level_one_diag.reshape(count, block, block)
    level_one_inv, level_two_lead, level_two_inv = finish_blocks(
        (lax.axis_index("row") // CORES).reshape(1),
        row_parts(sums),
        lax.dynamic_index_in_dim(diag_blocks, col, 0, keepdims=False),
        lax.dynamic_index_in_dim(diag_blocks, parents[0], 0, keepdims=False),
        level_two_diag,
        parent_lead,
    )
    return level_one_rows, level_one_inv, level_two_rows, level_two_lead, level_two_inv


def solution(mesh):
    in_specs = (
        P("col", "row"),
        P("col", "row"),
        P("col", "row"),
        P(),
        P("col", "row"),
        P("col", "row"),
        P("col", None),
        P("col", None),
        P("col"),
    )
    out_specs = (P("col", "row"), P("col", None), P("col", "row"), P("col", None), P("col", None))
    return jax.shard_map(
        per_device, mesh=mesh, in_specs=in_specs, out_specs=out_specs, check_vma=False
    )
```

```python
import jax
import jax.numpy as jnp
from jax import lax
from jax.experimental import pallas as pl
from jax.experimental.pallas import tpu as pltpu
from jax.sharding import PartitionSpec as P

SIDE = 4
CORES = 2
F32 = jnp.float32
RING_VMEM = 52 * 2**20


def x_step(d):
    return [(y * SIDE + x, y * SIDE + (x + d) % SIDE) for y in range(SIDE) for x in range(SIDE)]


def y_step(d):
    return [(y * SIDE + x, (y + d) % SIDE * SIDE + x) for y in range(SIDE) for x in range(SIDE)]


def z_step(d):
    return [(z * CORES + e, (z + d) % SIDE * CORES + e) for z in range(SIDE) for e in range(CORES)]


CORE_SWAP = [(i, i ^ 1) for i in range(SIDE * CORES)]


def turn(k):
    cols, rows = SIDE * SIDE, SIDE * CORES
    return [
        (r * cols + c, c // 2 * cols + 2 * r + (c + k) % 2) for r in range(rows) for c in range(cols)
    ]


def apply_pattern(panels, pattern, block):
    count, blocks = pattern.shape
    shaped = panels.reshape(count, block, blocks, block)
    return (shaped * pattern.astype(panels.dtype)[:, None, :, None]).reshape(panels.shape)


def turned_panels(masked, k):
    col = lax.axis_index("col")
    half = masked.shape[1] // 2
    part = lax.dynamic_slice_in_dim(masked, (col + k) % 2 * half, half, 1)
    return lax.ppermute(part, ("row", "col"), turn(k))


def in_order(pieces):
    even = lax.axis_index("col") % 2 == 0
    return jnp.stack(
        [jnp.where(even, pieces[0], pieces[1]), jnp.where(even, pieces[1], pieces[0])]
    )


def all_panels(own):
    below = lax.ppermute(own, "row", z_step(1))
    above = lax.ppermute(own, "row", z_step(-1))
    far = jnp.stack(
        [lax.ppermute(below[0], "row", z_step(1)), lax.ppermute(above[1], "row", z_step(-1))]
    )
    found = []
    for held in (own, below, above, far):
        found += [held, lax.ppermute(held, "row", CORE_SWAP)]
    return found


def arrival(supernode):
    row = lax.axis_index("row")
    z, core = row // CORES, row % CORES
    source = supernode // 2
    slot = jnp.array([0, 2, 3, 1], jnp.int32)[(source // CORES - z) % SIDE]
    return slot * 4 + (source + core) % CORES * 2 + supernode % 2


def by_column(pieces, matrix, block):
    rows, depth = pieces[0].shape[0] * pieces[0].shape[1], pieces[0].shape[2]
    width = matrix.shape[1]
    steps = len(pieces)

    def kernel(*refs):
        matrix_ref, out_ref, held = refs[steps:]
        for i in range(steps):

            @pl.when(pl.program_id(0) == i)
            def _():
                held[...] = refs[i][...].reshape(rows, depth)

        total = jnp.dot(held[...], matrix_ref[...], preferred_element_type=F32)
        for d in range(width // block):
            out_ref[d] = total[:, d * block : (d + 1) * block].astype(out_ref.dtype)

    return pl.pallas_call(
        kernel,
        out_shape=jax.ShapeDtypeStruct((width // block, steps * rows, block), matrix.dtype),
        grid=(steps,),
        in_specs=[pl.BlockSpec(v.shape, lambda i: (0, 0, 0)) for v in pieces]
        + [pl.BlockSpec((depth, width), lambda i: (0, 0))],
        out_specs=pl.BlockSpec((width // block, rows, block), lambda i: (0, i, 0)),
        scratch_shapes=[pltpu.VMEM((rows, depth), matrix.dtype)],
        compiler_params=pltpu.CompilerParams(vmem_limit_bytes=52 * 2**20),
        cost_estimate=pl.CostEstimate(
            flops=2 * steps * rows * depth * width,
            bytes_accessed=2 * (steps * rows * (depth + width) + depth * width),
            transcendentals=0,
        ),
    )(*pieces, matrix)


def by_supernode(order, rows, matrix, part):
    block, depth = rows.shape[1:]
    width = matrix.shape[1] // 2
    groups = order.shape[0] // SIDE

    def kernel(order_ref, a_ref, b_ref, c_ref, d_ref, matrix_ref, *out):
        left = jnp.concatenate([a_ref[0], b_ref[0], c_ref[0], d_ref[0]], 0)
        total = jnp.dot(left, matrix_ref[...], preferred_element_type=F32)
        value = total.reshape(SIDE, block, width).astype(rows.dtype)
        for g in range(groups):

            @pl.when(pl.program_id(0) == g)
            def _():
                out[g][...] = value

    def pick(j):
        return pl.BlockSpec((1, block, depth), lambda i, order_ref: (order_ref[SIDE * i + j], 0, 0))

    return pl.pallas_call(
        kernel,
        out_shape=[jax.ShapeDtypeStruct((SIDE, block, width), rows.dtype)] * groups,
        grid_spec=pltpu.PrefetchScalarGridSpec(
            num_scalar_prefetch=1,
            grid=(groups,),
            in_specs=[pick(j) for j in range(SIDE)]
            + [pl.BlockSpec((depth, width), lambda i, order_ref: (0, part))],
            out_specs=[pl.BlockSpec((SIDE, block, width), lambda i, order_ref: (0, 0, 0))]
            * groups,
        ),
        compiler_params=pltpu.CompilerParams(vmem_limit_bytes=RING_VMEM),
        cost_estimate=pl.CostEstimate(
            flops=2 * groups * SIDE * block * depth * width,
            bytes_accessed=2 * groups * SIDE * block * (depth + width),
            transcendentals=0,
        ),
    )(order, rows, rows, rows, rows, matrix)


def send(value, step):
    return lax.ppermute(value, "col", step)


def first_sends(product, order, step):
    order = order.reshape(SIDE, -1)
    (far,) = product(order[2])
    rest, far = lax.optimization_barrier((jnp.concatenate([order[1], order[3], order[0]]), far))
    ahead, behind, own = product(rest)
    return [send(far, step(2)), send(ahead, step(1)), send(behind, step(-1))], own


def second_sends(arriving, own, step):
    _, block, width = own.shape
    kind = own.dtype
    tile = width // SIDE

    def kernel(one_ref, two_ref, three_ref, own_ref, own_out, *out):
        for d in range(SIDE):
            total = own_ref[d].astype(F32) + one_ref[d].astype(F32)
            total = total + two_ref[d].astype(F32) + three_ref[d].astype(F32)
            if d:
                out[d - 1][...] = total.astype(kind)
            else:
                own_out[...] = total

    four = pl.BlockSpec((SIDE, block, tile), lambda i: (0, 0, i))
    one = pl.BlockSpec((block, tile), lambda i: (0, i))
    kept, *others = pl.pallas_call(
        kernel,
        out_shape=[jax.ShapeDtypeStruct((block, width), F32)]
        + [jax.ShapeDtypeStruct((block, width), kind)] * 3,
        grid=(SIDE,),
        in_specs=[four] * 4,
        out_specs=[one] * 4,
        compiler_params=pltpu.CompilerParams(vmem_limit_bytes=RING_VMEM),
        cost_estimate=pl.CostEstimate(flops=0, bytes_accessed=2**22, transcendentals=0),
    )(*arriving, own)
    return [kept] + [send(v, step(d + 1)) for d, v in enumerate(others)]


def row_parts(values):
    values = values + lax.ppermute(values, "row", CORE_SWAP)
    values = values.astype(jnp.bfloat16)
    return [values] + [lax.ppermute(values, "row", z_step(-d)) for d in range(1, SIDE)]


def whole(shape):
    return pl.BlockSpec(shape, lambda i: (0,) * len(shape))


def small_call(kernel, shapes, scalars, arrays, scratch=()):
    return pl.pallas_call(
        kernel,
        out_shape=[jax.ShapeDtypeStruct(shape, kind) for shape, kind in shapes],
        grid=(1,),
        in_specs=[pl.BlockSpec(memory_space=pltpu.SMEM)] * len(scalars)
        + [whole(v.shape) for v in arrays],
        out_specs=[whole(shape) for shape, _ in shapes],
        scratch_shapes=list(scratch),
        compiler_params=pltpu.CompilerParams(vmem_limit_bytes=RING_VMEM),
        cost_estimate=pl.CostEstimate(flops=0, bytes_accessed=2**20, transcendentals=0),
    )(*scalars, *arrays)


def outgoing(place, readers, pattern, total):
    count, block = total.shape[:2]

    def kernel(place_ref, readers_ref, pattern_ref, total_ref, out_ref):
        for d in range(count):
            for j, k in enumerate((d, readers_ref[d])):
                value = total_ref[place_ref[k]].astype(F32) * pattern_ref[k].astype(F32)
                out_ref[d, j] = (-value).astype(out_ref.dtype)

    return small_call(
        kernel,
        [((count, 2, block, block), jnp.bfloat16)],
        [place, readers, pattern],
        [total],
    )[0]


def finish_rows(pattern, back, parent_panels, masked_one, masked_two, lead, second):
    count, _, block, _ = back.shape
    width = count * block
    kind = back.dtype

    def over(a, b):
        return lax.dot_general(a, b, (((1,), (1,)), ((), ())), preferred_element_type=F32)

    def kernel(
        pattern_ref, back_ref, panels_ref, one_ref, two_ref, lead_ref, *refs
    ):
        terms = [refs[: len(second) // 2], refs[len(second) // 2 : len(second)]]
        rows_one_ref, rows_two_ref, sums_ref, chosen, panels = refs[len(second) :]
        for i in range(count):
            part = pl.ds(i * block, block)
            rows_one_ref[:, part] = back_ref[i, 0]
            chosen[:, part] = back_ref[i, 1]
            panels[:, part] = panels_ref[i]
        for i in range(count):
            part = pl.ds(i * block, block)
            side, first = i * 2 // count, i % (count // 2) * block
            total = jnp.dot(lead_ref[...], chosen[:, part], preferred_element_type=F32)
            for ref in terms[side]:
                total = total + ref[:, first : first + block].astype(F32)
            rows_two_ref[:, part] = (-(total * pattern_ref[0, i].astype(F32))).astype(kind)
        sums_ref[0] = over(one_ref[...], rows_one_ref[...])
        sums_ref[1] = over(two_ref[...], chosen[...])
        sums_ref[2] = over(panels[...], chosen[...])
        sums_ref[3] = over(two_ref[...], rows_two_ref[...])

    return small_call(
        kernel,
        [((block, width), kind), ((block, width), kind), ((4, block, block), F32)],
        [pattern],
        [back, parent_panels, masked_one, masked_two, lead, *second],
        [pltpu.VMEM((block, width), kind), pltpu.VMEM((block, width), kind)],
    )


def finish_blocks(z, parts, own_diag, parent_diag, two_diag, lead):
    block = lead.shape[0]

    def kernel(z_ref, a, b, c, d, own_ref, parent_ref, two_ref, lead_ref, one_out, lead_out, two_out, sums):
        held = (a, b, c, d)
        for k in range(SIDE):

            @pl.when(z_ref[0] == k)
            def _():
                w = [held[(i - k) % SIDE][...].astype(F32) for i in range(SIDE)]
                sums[...] = (w[0] + w[1]) + (w[2] + w[3])

        one_out[...] = own_ref[...] - sums[0]
        lead_wide = lead_ref[...].astype(F32)
        found = -(
            sums[1]
            + jnp.dot(
                lead_wide,
                parent_ref[...] - sums[2],
                precision=lax.Precision.HIGHEST,
                preferred_element_type=F32,
            )
        )
        lead_out[...] = found
        two_out[...] = (
            two_ref[...]
            - sums[3]
            - lax.dot_general(
                lead_wide,
                found,
                (((1,), (1,)), ((), ())),
                precision=lax.Precision.HIGHEST,
                preferred_element_type=F32,
            )
        )

    return small_call(
        kernel,
        [((block, block), F32)] * 3,
        [z],
        [*parts, own_diag, parent_diag, two_diag, lead],
        [pltpu.VMEM((4, block, block), F32)],
    )


def per_device(
    ancestor_inverse,
    level_one_panels,
    level_one_pattern,
    level_one_diag,
    level_two_panels,
    level_two_pattern,
    parent_lead,
    level_two_diag,
    parents,
):
    block = level_one_diag.shape[1]
    bf16 = jnp.bfloat16
    col = lax.axis_index("col")
    x, y = col % SIDE, col // SIDE
    count = SIDE * SIDE
    span, width = ancestor_inverse.shape
    masked_one = apply_pattern(level_one_panels, level_one_pattern, block)
    masked_two = apply_pattern(level_two_panels, level_two_pattern, block)

    found_one = all_panels(in_order([turned_panels(masked_one, k) for k in range(2)]))
    later_two, found_one = lax.optimization_barrier((masked_two, found_one))
    own_two = in_order([turned_panels(later_two, k) for k in range(2)])
    product_one = by_column(found_one, ancestor_inverse, block)
    first_sum = lax.psum_scatter(
        product_one.reshape(count * count * block, block), "col", scatter_dimension=0, tiled=True
    ).reshape(count, block, block)

    steps = jnp.arange(count, dtype=jnp.int32)
    place = arrival(steps)
    outer, inner = steps // SIDE, steps % SIDE
    x_major = (y + inner) % SIDE * SIDE + (x + outer) % SIDE
    y_major = (y + outer) % SIDE * SIDE + (x + inner) % SIDE

    rows_two = jnp.concatenate(all_panels(own_two), 0)

    def product(part):
        return lambda order: by_supernode(place[order], rows_two, ancestor_inverse, part)

    coming_a, own_a = first_sends(product(0), x_major, x_step)
    coming_b, own_b = first_sends(product(1), y_major, y_step)

    later_one, _ = lax.optimization_barrier((masked_one, rows_two))
    facts = jnp.concatenate(
        [
            jnp.broadcast_to(level_one_pattern.reshape(count, 1, 1), (count, 8, block)),
            jnp.broadcast_to(parents.reshape(1, 1, 1), (count, 8, block)),
        ],
        1,
    ).astype(bf16)
    cut = jnp.swapaxes(later_one.reshape(block, count, block), 0, 1)
    cut = lax.all_to_all(jnp.concatenate([cut, facts], 1), "col", 0, 0, tiled=True)
    cut_pattern = cut[:, block, 0].astype(jnp.int32)
    readers = cut[:, block + 8, 0].astype(jnp.int32)
    parent_panels = lax.all_to_all(
        jnp.take(cut[:, :block], readers, axis=0), "col", 0, 0, tiled=True
    )

    going = outgoing(place, readers, cut_pattern, first_sum)
    back = lax.all_to_all(going, "col", 0, 0, tiled=True)
    coming_a, coming_b, parent_panels, _ = lax.optimization_barrier(
        (coming_a, coming_b, parent_panels, going)
    )
    second_sum = second_sends(coming_a, own_a, y_step) + second_sends(coming_b, own_b, x_step)
    level_one_rows, level_two_rows, sums = finish_rows(
        level_two_pattern, back, parent_panels, masked_one, masked_two, parent_lead, second_sum
    )

    diag_blocks = level_one_diag.reshape(count, block, block)
    level_one_inv, level_two_lead, level_two_inv = finish_blocks(
        (lax.axis_index("row") // CORES).reshape(1),
        row_parts(sums),
        lax.dynamic_index_in_dim(diag_blocks, col, 0, keepdims=False),
        lax.dynamic_index_in_dim(diag_blocks, parents[0], 0, keepdims=False),
        level_two_diag,
        parent_lead,
    )
    return level_one_rows, level_one_inv, level_two_rows, level_two_lead, level_two_inv


def solution(mesh):
    in_specs = (
        P("col", "row"),
        P("col", "row"),
        P("col", "row"),
        P(),
        P("col", "row"),
        P("col", "row"),
        P("col", None),
        P("col", None),
        P("col"),
    )
    out_specs = (P("col", "row"), P("col", None), P("col", "row"), P("col", None), P("col", None))
    return jax.shard_map(
        per_device, mesh=mesh, in_specs=in_specs, out_specs=out_specs, check_vma=False
    )
```

```python
import jax
import jax.numpy as jnp
from jax import lax
from jax.experimental import pallas as pl
from jax.experimental.pallas import tpu as pltpu
from jax.sharding import PartitionSpec as P

SIDE = 4
CORES = 2
F32 = jnp.float32
RING_VMEM = 52 * 2**20


def x_step(d):
    return [(y * SIDE + x, y * SIDE + (x + d) % SIDE) for y in range(SIDE) for x in range(SIDE)]


def y_step(d):
    return [(y * SIDE + x, (y + d) % SIDE * SIDE + x) for y in range(SIDE) for x in range(SIDE)]


def z_step(d):
    return [(z * CORES + e, (z + d) % SIDE * CORES + e) for z in range(SIDE) for e in range(CORES)]


CORE_SWAP = [(i, i ^ 1) for i in range(SIDE * CORES)]


def turn(k):
    cols, rows = SIDE * SIDE, SIDE * CORES
    return [
        (r * cols + c, c // 2 * cols + 2 * r + (c + k) % 2) for r in range(rows) for c in range(cols)
    ]


def apply_pattern(panels, pattern, block):
    count, blocks = pattern.shape
    shaped = panels.reshape(count, block, blocks, block)
    return (shaped * pattern.astype(panels.dtype)[:, None, :, None]).reshape(panels.shape)


def turned_panels(masked, k):
    col = lax.axis_index("col")
    half = masked.shape[1] // 2
    part = lax.dynamic_slice_in_dim(masked, (col + k) % 2 * half, half, 1)
    return lax.ppermute(part, ("row", "col"), turn(k))


def in_order(pieces):
    even = lax.axis_index("col") % 2 == 0
    return jnp.stack(
        [jnp.where(even, pieces[0], pieces[1]), jnp.where(even, pieces[1], pieces[0])]
    )


def all_panels(own):
    below = lax.ppermute(own, "row", z_step(1))
    above = lax.ppermute(own, "row", z_step(-1))
    far = jnp.stack(
        [lax.ppermute(below[0], "row", z_step(1)), lax.ppermute(above[1], "row", z_step(-1))]
    )
    found = []
    for held in (own, below, above, far):
        found += [held, lax.ppermute(held, "row", CORE_SWAP)]
    return found


def arrival(supernode):
    row = lax.axis_index("row")
    z, core = row // CORES, row % CORES
    source = supernode // 2
    slot = jnp.array([0, 2, 3, 1], jnp.int32)[(source // CORES - z) % SIDE]
    return slot * 4 + (source + core) % CORES * 2 + supernode % 2


def by_column(pieces, matrix, block):
    rows, depth = pieces[0].shape[0] * pieces[0].shape[1], pieces[0].shape[2]
    width = matrix.shape[1]
    steps = len(pieces)

    def kernel(*refs):
        matrix_ref, out_ref, held = refs[steps:]
        for i in range(steps):

            @pl.when(pl.program_id(0) == i)
            def _():
                held[...] = refs[i][...].reshape(rows, depth)

        total = jnp.dot(held[...], matrix_ref[...], preferred_element_type=F32)
        for d in range(width // block):
            out_ref[d] = total[:, d * block : (d + 1) * block].astype(out_ref.dtype)

    return pl.pallas_call(
        kernel,
        out_shape=jax.ShapeDtypeStruct((width // block, steps * rows, block), matrix.dtype),
        grid=(steps,),
        in_specs=[pl.BlockSpec(v.shape, lambda i: (0, 0, 0)) for v in pieces]
        + [pl.BlockSpec((depth, width), lambda i: (0, 0))],
        out_specs=pl.BlockSpec((width // block, rows, block), lambda i: (0, i, 0)),
        scratch_shapes=[pltpu.VMEM((rows, depth), matrix.dtype)],
        compiler_params=pltpu.CompilerParams(vmem_limit_bytes=52 * 2**20),
        cost_estimate=pl.CostEstimate(
            flops=2 * steps * rows * depth * width,
            bytes_accessed=2 * (steps * rows * (depth + width) + depth * width),
            transcendentals=0,
        ),
    )(*pieces, matrix)


def by_supernode(order, rows, matrix, part):
    block, depth = rows.shape[1:]
    width = matrix.shape[1] // 2
    groups = order.shape[0] // SIDE

    def kernel(order_ref, a_ref, b_ref, c_ref, d_ref, matrix_ref, *out):
        left = jnp.concatenate([a_ref[0], b_ref[0], c_ref[0], d_ref[0]], 0)
        total = jnp.dot(left, matrix_ref[...], preferred_element_type=F32)
        value = total.reshape(SIDE, block, width).astype(rows.dtype)
        for g in range(groups):

            @pl.when(pl.program_id(0) == g)
            def _():
                out[g][...] = value

    def pick(j):
        return pl.BlockSpec((1, block, depth), lambda i, order_ref: (order_ref[SIDE * i + j], 0, 0))

    return pl.pallas_call(
        kernel,
        out_shape=[jax.ShapeDtypeStruct((SIDE, block, width), rows.dtype)] * groups,
        grid_spec=pltpu.PrefetchScalarGridSpec(
            num_scalar_prefetch=1,
            grid=(groups,),
            in_specs=[pick(j) for j in range(SIDE)]
            + [pl.BlockSpec((depth, width), lambda i, order_ref: (0, part))],
            out_specs=[pl.BlockSpec((SIDE, block, width), lambda i, order_ref: (0, 0, 0))]
            * groups,
        ),
        compiler_params=pltpu.CompilerParams(vmem_limit_bytes=RING_VMEM),
        cost_estimate=pl.CostEstimate(
            flops=2 * groups * SIDE * block * depth * width,
            bytes_accessed=2 * groups * SIDE * block * (depth + width),
            transcendentals=0,
        ),
    )(order, rows, rows, rows, rows, matrix)


def send(value, step):
    return lax.ppermute(value, "col", step)


def first_sends(product, order, step):
    order = order.reshape(SIDE, -1)
    (far,) = product(order[2])
    rest, far = lax.optimization_barrier((jnp.concatenate([order[1], order[3], order[0]]), far))
    ahead, behind, own = product(rest)
    return [send(far, step(2)), send(ahead, step(1)), send(behind, step(-1))], own


def second_sends(arriving, own, step):
    _, block, width = own.shape
    kind = own.dtype
    tile = width // SIDE

    def kernel(one_ref, two_ref, three_ref, own_ref, own_out, *out):
        for d in range(SIDE):
            total = own_ref[d].astype(F32) + one_ref[d].astype(F32)
            total = total + two_ref[d].astype(F32) + three_ref[d].astype(F32)
            if d:
                out[d - 1][...] = total.astype(kind)
            else:
                own_out[...] = total

    four = pl.BlockSpec((SIDE, block, tile), lambda i: (0, 0, i))
    one = pl.BlockSpec((block, tile), lambda i: (0, i))
    kept, *others = pl.pallas_call(
        kernel,
        out_shape=[jax.ShapeDtypeStruct((block, width), F32)]
        + [jax.ShapeDtypeStruct((block, width), kind)] * 3,
        grid=(SIDE,),
        in_specs=[four] * 4,
        out_specs=[one] * 4,
        compiler_params=pltpu.CompilerParams(vmem_limit_bytes=RING_VMEM),
        cost_estimate=pl.CostEstimate(flops=0, bytes_accessed=2**22, transcendentals=0),
    )(*arriving, own)
    return [kept] + [send(v, step(d + 1)) for d, v in enumerate(others)]


def row_parts(values):
    values = values + lax.ppermute(values, "row", CORE_SWAP)
    values = values.astype(jnp.bfloat16)
    return [values] + [lax.ppermute(values, "row", z_step(-d)) for d in range(1, SIDE)]


def whole(shape):
    return pl.BlockSpec(shape, lambda i: (0,) * len(shape))


def small_call(kernel, shapes, scalars, arrays, scratch=()):
    return pl.pallas_call(
        kernel,
        out_shape=[jax.ShapeDtypeStruct(shape, kind) for shape, kind in shapes],
        grid=(1,),
        in_specs=[pl.BlockSpec(memory_space=pltpu.SMEM)] * len(scalars)
        + [whole(v.shape) for v in arrays],
        out_specs=[whole(shape) for shape, _ in shapes],
        scratch_shapes=list(scratch),
        compiler_params=pltpu.CompilerParams(vmem_limit_bytes=RING_VMEM),
        cost_estimate=pl.CostEstimate(flops=0, bytes_accessed=2**20, transcendentals=0),
    )(*scalars, *arrays)


def outgoing(place, readers, pattern, total, cut):
    count, block = total.shape[:2]

    def kernel(place_ref, readers_ref, pattern_ref, total_ref, cut_ref, out_ref):
        for d in range(count):
            for j, k in enumerate((d, readers_ref[d])):
                value = total_ref[place_ref[k]].astype(F32) * pattern_ref[k].astype(F32)
                out_ref[d, j] = (-value).astype(out_ref.dtype)
            out_ref[d, 2] = cut_ref[readers_ref[d], :block]

    return small_call(
        kernel,
        [((count, 3, block, block), jnp.bfloat16)],
        [place, readers, pattern],
        [total, cut],
    )[0]


def finish_rows(pattern, back, masked_one, masked_two, lead, second):
    count, _, block, _ = back.shape
    width = count * block
    kind = back.dtype

    def over(a, b):
        return lax.dot_general(a, b, (((1,), (1,)), ((), ())), preferred_element_type=F32)

    def kernel(
        pattern_ref, back_ref, one_ref, two_ref, lead_ref, *refs
    ):
        terms = [refs[: len(second) // 2], refs[len(second) // 2 : len(second)]]
        rows_one_ref, rows_two_ref, sums_ref, chosen, panels = refs[len(second) :]
        for i in range(count):
            part = pl.ds(i * block, block)
            rows_one_ref[:, part] = back_ref[i, 0]
            chosen[:, part] = back_ref[i, 1]
            panels[:, part] = back_ref[i, 2]
        for i in range(count):
            part = pl.ds(i * block, block)
            side, first = i * 2 // count, i % (count // 2) * block
            total = jnp.dot(lead_ref[...], chosen[:, part], preferred_element_type=F32)
            for ref in terms[side]:
                total = total + ref[:, first : first + block].astype(F32)
            rows_two_ref[:, part] = (-(total * pattern_ref[0, i].astype(F32))).astype(kind)
        sums_ref[0] = over(one_ref[...], rows_one_ref[...])
        sums_ref[1] = over(two_ref[...], chosen[...])
        sums_ref[2] = over(panels[...], chosen[...])
        sums_ref[3] = over(two_ref[...], rows_two_ref[...])

    return small_call(
        kernel,
        [((block, width), kind), ((block, width), kind), ((4, block, block), F32)],
        [pattern],
        [back, masked_one, masked_two, lead, *second],
        [pltpu.VMEM((block, width), kind), pltpu.VMEM((block, width), kind)],
    )


def finish_blocks(z, parts, own_diag, parent_diag, two_diag, lead):
    block = lead.shape[0]

    def kernel(z_ref, a, b, c, d, own_ref, parent_ref, two_ref, lead_ref, one_out, lead_out, two_out, sums):
        held = (a, b, c, d)
        for k in range(SIDE):

            @pl.when(z_ref[0] == k)
            def _():
                w = [held[(i - k) % SIDE][...].astype(F32) for i in range(SIDE)]
                sums[...] = (w[0] + w[1]) + (w[2] + w[3])

        one_out[...] = own_ref[...] - sums[0]
        lead_wide = lead_ref[...].astype(F32)
        found = -(
            sums[1]
            + jnp.dot(
                lead_wide,
                parent_ref[...] - sums[2],
                precision=lax.Precision.HIGHEST,
                preferred_element_type=F32,
            )
        )
        lead_out[...] = found
        two_out[...] = (
            two_ref[...]
            - sums[3]
            - lax.dot_general(
                lead_wide,
                found,
                (((1,), (1,)), ((), ())),
                precision=lax.Precision.HIGHEST,
                preferred_element_type=F32,
            )
        )

    return small_call(
        kernel,
        [((block, block), F32)] * 3,
        [z],
        [*parts, own_diag, parent_diag, two_diag, lead],
        [pltpu.VMEM((4, block, block), F32)],
    )


def per_device(
    ancestor_inverse,
    level_one_panels,
    level_one_pattern,
    level_one_diag,
    level_two_panels,
    level_two_pattern,
    parent_lead,
    level_two_diag,
    parents,
):
    block = level_one_diag.shape[1]
    bf16 = jnp.bfloat16
    col = lax.axis_index("col")
    x, y = col % SIDE, col // SIDE
    count = SIDE * SIDE
    span, width = ancestor_inverse.shape
    masked_one = apply_pattern(level_one_panels, level_one_pattern, block)
    masked_two = apply_pattern(level_two_panels, level_two_pattern, block)

    found_one = all_panels(in_order([turned_panels(masked_one, k) for k in range(2)]))
    later_two, found_one = lax.optimization_barrier((masked_two, found_one))
    own_two = in_order([turned_panels(later_two, k) for k in range(2)])
    product_one = by_column(found_one, ancestor_inverse, block)
    first_sum = lax.psum_scatter(
        product_one.reshape(count * count * block, block), "col", scatter_dimension=0, tiled=True
    ).reshape(count, block, block)

    steps = jnp.arange(count, dtype=jnp.int32)
    place = arrival(steps)
    outer, inner = steps // SIDE, steps % SIDE
    x_major = (y + inner) % SIDE * SIDE + (x + outer) % SIDE
    y_major = (y + outer) % SIDE * SIDE + (x + inner) % SIDE

    rows_two = jnp.concatenate(all_panels(own_two), 0)

    def product(part):
        return lambda order: by_supernode(place[order], rows_two, ancestor_inverse, part)

    coming_a, own_a = first_sends(product(0), x_major, x_step)
    coming_b, own_b = first_sends(product(1), y_major, y_step)

    later_one, _ = lax.optimization_barrier((masked_one, rows_two))
    facts = jnp.concatenate(
        [
            jnp.broadcast_to(level_one_pattern.reshape(count, 1, 1), (count, 8, block)),
            jnp.broadcast_to(parents.reshape(1, 1, 1), (count, 8, block)),
        ],
        1,
    ).astype(bf16)
    cut = jnp.swapaxes(later_one.reshape(block, count, block), 0, 1)
    cut = lax.all_to_all(jnp.concatenate([cut, facts], 1), "col", 0, 0, tiled=True)
    cut_pattern = cut[:, block, 0].astype(jnp.int32)
    readers = cut[:, block + 8, 0].astype(jnp.int32)
    going = outgoing(place, readers, cut_pattern, first_sum, cut)
    back = lax.all_to_all(going, "col", 0, 0, tiled=True)
    coming_a, coming_b, _ = lax.optimization_barrier((coming_a, coming_b, going))
    second_sum = second_sends(coming_a, own_a, y_step) + second_sends(coming_b, own_b, x_step)
    level_one_rows, level_two_rows, sums = finish_rows(
        level_two_pattern, back, masked_one, masked_two, parent_lead, second_sum
    )

    diag_blocks = level_one_diag.reshape(count, block, block)
    level_one_inv, level_two_lead, level_two_inv = finish_blocks(
        (lax.axis_index("row") // CORES).reshape(1),
        row_parts(sums),
        lax.dynamic_index_in_dim(diag_blocks, col, 0, keepdims=False),
        lax.dynamic_index_in_dim(diag_blocks, parents[0], 0, keepdims=False),
        level_two_diag,
        parent_lead,
    )
    return level_one_rows, level_one_inv, level_two_rows, level_two_lead, level_two_inv


def solution(mesh):
    in_specs = (
        P("col", "row"),
        P("col", "row"),
        P("col", "row"),
        P(),
        P("col", "row"),
        P("col", "row"),
        P("col", None),
        P("col", None),
        P("col"),
    )
    out_specs = (P("col", "row"), P("col", None), P("col", "row"), P("col", None), P("col", None))
    return jax.shard_map(
        per_device, mesh=mesh, in_specs=in_specs, out_specs=out_specs, check_vma=False
    )
```

```python
import jax
import jax.numpy as jnp
from jax import lax
from jax.experimental import pallas as pl
from jax.experimental.pallas import tpu as pltpu
from jax.sharding import PartitionSpec as P

SIDE = 4
CORES = 2
F32 = jnp.float32
RING_VMEM = 52 * 2**20


def x_step(d):
    return [(y * SIDE + x, y * SIDE + (x + d) % SIDE) for y in range(SIDE) for x in range(SIDE)]


def y_step(d):
    return [(y * SIDE + x, (y + d) % SIDE * SIDE + x) for y in range(SIDE) for x in range(SIDE)]


def z_step(d):
    return [(z * CORES + e, (z + d) % SIDE * CORES + e) for z in range(SIDE) for e in range(CORES)]


CORE_SWAP = [(i, i ^ 1) for i in range(SIDE * CORES)]


def turn(k):
    cols, rows = SIDE * SIDE, SIDE * CORES
    return [
        (r * cols + c, c // 2 * cols + 2 * r + (c + k) % 2) for r in range(rows) for c in range(cols)
    ]


def apply_pattern(panels, pattern, block):
    count, blocks = pattern.shape
    shaped = panels.reshape(count, block, blocks, block)
    return (shaped * pattern.astype(panels.dtype)[:, None, :, None]).reshape(panels.shape)


def turned_panels(masked, k):
    col = lax.axis_index("col")
    half = masked.shape[1] // 2
    part = lax.dynamic_slice_in_dim(masked, (col + k) % 2 * half, half, 1)
    return lax.ppermute(part, ("row", "col"), turn(k))


def in_order(pieces):
    even = lax.axis_index("col") % 2 == 0
    return jnp.stack(
        [jnp.where(even, pieces[0], pieces[1]), jnp.where(even, pieces[1], pieces[0])]
    )


def all_panels(own):
    below = lax.ppermute(own, "row", z_step(1))
    above = lax.ppermute(own, "row", z_step(-1))
    far = jnp.stack(
        [lax.ppermute(below[0], "row", z_step(1)), lax.ppermute(above[1], "row", z_step(-1))]
    )
    found = []
    for held in (own, below, above, far):
        found += [held, lax.ppermute(held, "row", CORE_SWAP)]
    return found


def arrival(supernode):
    row = lax.axis_index("row")
    z, core = row // CORES, row % CORES
    source = supernode // 2
    slot = jnp.array([0, 2, 3, 1], jnp.int32)[(source // CORES - z) % SIDE]
    return slot * 4 + (source + core) % CORES * 2 + supernode % 2


def by_column(pieces, matrix, block):
    rows, depth = pieces[0].shape[0] * pieces[0].shape[1], pieces[0].shape[2]
    width = matrix.shape[1]
    steps = len(pieces)

    def kernel(*refs):
        matrix_ref, out_ref, held = refs[steps:]
        for i in range(steps):

            @pl.when(pl.program_id(0) == i)
            def _():
                held[...] = refs[i][...].reshape(rows, depth)

        total = jnp.dot(held[...], matrix_ref[...], preferred_element_type=F32)
        for d in range(width // block):
            out_ref[d] = total[:, d * block : (d + 1) * block].astype(out_ref.dtype)

    return pl.pallas_call(
        kernel,
        out_shape=jax.ShapeDtypeStruct((width // block, steps * rows, block), matrix.dtype),
        grid=(steps,),
        in_specs=[pl.BlockSpec(v.shape, lambda i: (0, 0, 0)) for v in pieces]
        + [pl.BlockSpec((depth, width), lambda i: (0, 0))],
        out_specs=pl.BlockSpec((width // block, rows, block), lambda i: (0, i, 0)),
        scratch_shapes=[pltpu.VMEM((rows, depth), matrix.dtype)],
        compiler_params=pltpu.CompilerParams(vmem_limit_bytes=52 * 2**20),
        cost_estimate=pl.CostEstimate(
            flops=2 * steps * rows * depth * width,
            bytes_accessed=2 * (steps * rows * (depth + width) + depth * width),
            transcendentals=0,
        ),
    )(*pieces, matrix)


def by_supernode(order, rows, matrix, part, split):
    block, depth = rows.shape[1:]
    width = matrix.shape[1] // 2
    groups = order.shape[0] // SIDE
    outs = 2 if split else 1
    size = block // outs

    def kernel(order_ref, a_ref, b_ref, c_ref, d_ref, matrix_ref, *out):
        left = jnp.concatenate([a_ref[0], b_ref[0], c_ref[0], d_ref[0]], 0)
        total = jnp.dot(left, matrix_ref[...], preferred_element_type=F32)
        total = total.reshape(SIDE, block, width)
        for i, ref in enumerate(out):
            ref[0] = total[:, i * size : (i + 1) * size].astype(ref.dtype)

    def pick(j):
        return pl.BlockSpec((1, block, depth), lambda i, order_ref: (order_ref[SIDE * i + j], 0, 0))

    return pl.pallas_call(
        kernel,
        out_shape=[jax.ShapeDtypeStruct((groups, SIDE, size, width), rows.dtype)] * outs,
        grid_spec=pltpu.PrefetchScalarGridSpec(
            num_scalar_prefetch=1,
            grid=(groups,),
            in_specs=[pick(j) for j in range(SIDE)]
            + [pl.BlockSpec((depth, width), lambda i, order_ref: (0, part))],
            out_specs=[pl.BlockSpec((1, SIDE, size, width), lambda i, order_ref: (i, 0, 0, 0))]
            * outs,
        ),
        compiler_params=pltpu.CompilerParams(vmem_limit_bytes=RING_VMEM),
        cost_estimate=pl.CostEstimate(
            flops=2 * groups * SIDE * block * depth * width,
            bytes_accessed=2 * groups * SIDE * block * (depth + width),
            transcendentals=0,
        ),
    )(order, rows, rows, rows, rows, matrix)


def send(value, step):
    return lax.ppermute(value, "col", step)


def second_sends(arriving, near, step):
    _, _, block, width = near.shape
    half = block // 2

    def kernel(low_ref, high_ref, ahead_ref, behind_ref, ahead_out, behind_out):
        kind = ahead_out.dtype
        low = ahead_ref[0, 0, :half].astype(F32) + low_ref[0].astype(F32)
        high = behind_ref[0, 0, half:].astype(F32) + high_ref[0].astype(F32)
        ahead_out[0, :half] = low.astype(kind)
        ahead_out[0, half:] = ahead_ref[0, 0, half:]
        behind_out[0, :half] = behind_ref[0, 0, :half]
        behind_out[0, half:] = high.astype(kind)

    part = pl.BlockSpec((1, half, width), lambda i: (i, 0, 0))
    own = [pl.BlockSpec((1, 1, block, width), lambda i, g=g: (g, i, 0, 0)) for g in range(2)]
    full = pl.BlockSpec((1, block, width), lambda i: (i, 0, 0))
    ahead, behind = pl.pallas_call(
        kernel,
        out_shape=[jax.ShapeDtypeStruct((SIDE, block, width), near.dtype)] * 2,
        grid=(SIDE,),
        in_specs=[part, part, *own],
        out_specs=[full, full],
        compiler_params=pltpu.CompilerParams(vmem_limit_bytes=RING_VMEM),
        cost_estimate=pl.CostEstimate(flops=0, bytes_accessed=2**22, transcendentals=0),
    )(*arriving, near, near)
    return send(ahead, step(1)), send(behind, step(-1))


def third_sends(arriving, near, step):
    _, _, block, width = near.shape
    kind = near.dtype
    tile = width // SIDE

    def kernel(one_ref, two_ref, own_ref, own_out, *out):
        for d in range(SIDE):
            total = own_ref[0, d].astype(F32) + one_ref[d].astype(F32) + two_ref[d].astype(F32)
            if d:
                out[d - 1][...] = total.astype(kind)
            else:
                own_out[...] = total

    four = pl.BlockSpec((SIDE, block, tile), lambda i: (0, 0, i))
    one = pl.BlockSpec((block, tile), lambda i: (0, i))
    own, *others = pl.pallas_call(
        kernel,
        out_shape=[jax.ShapeDtypeStruct((block, width), F32)]
        + [jax.ShapeDtypeStruct((block, width), kind)] * 3,
        grid=(SIDE,),
        in_specs=[four, four, pl.BlockSpec((1, SIDE, block, tile), lambda i: (2, 0, 0, i))],
        out_specs=[one] * 4,
        compiler_params=pltpu.CompilerParams(vmem_limit_bytes=RING_VMEM),
        cost_estimate=pl.CostEstimate(flops=0, bytes_accessed=2**22, transcendentals=0),
    )(*arriving, near)
    return [own] + [send(v, step(d + 1)) for d, v in enumerate(others)]


def row_parts(values):
    values = values + lax.ppermute(values, "row", CORE_SWAP)
    values = values.astype(jnp.bfloat16)
    return [values] + [lax.ppermute(values, "row", z_step(-d)) for d in range(1, SIDE)]


def whole(shape):
    return pl.BlockSpec(shape, lambda i: (0,) * len(shape))


def small_call(kernel, shapes, scalars, arrays, scratch=()):
    return pl.pallas_call(
        kernel,
        out_shape=[jax.ShapeDtypeStruct(shape, kind) for shape, kind in shapes],
        grid=(1,),
        in_specs=[pl.BlockSpec(memory_space=pltpu.SMEM)] * len(scalars)
        + [whole(v.shape) for v in arrays],
        out_specs=[whole(shape) for shape, _ in shapes],
        scratch_shapes=list(scratch),
        compiler_params=pltpu.CompilerParams(vmem_limit_bytes=RING_VMEM),
        cost_estimate=pl.CostEstimate(flops=0, bytes_accessed=2**20, transcendentals=0),
    )(*scalars, *arrays)


def outgoing(place, readers, pattern, total, cut):
    count, block = total.shape[:2]

    def kernel(place_ref, readers_ref, pattern_ref, total_ref, cut_ref, out_ref):
        for d in range(count):
            for j, k in enumerate((d, readers_ref[d])):
                value = total_ref[place_ref[k]].astype(F32) * pattern_ref[k].astype(F32)
                out_ref[d, j] = (-value).astype(out_ref.dtype)
            out_ref[d, 2] = cut_ref[readers_ref[d], :block]

    return small_call(
        kernel,
        [((count, 3, block, block), jnp.bfloat16)],
        [place, readers, pattern],
        [total, cut],
    )[0]


def finish_rows(pattern, back, masked_one, masked_two, lead, second):
    count, _, block, _ = back.shape
    width = count * block
    kind = back.dtype

    def over(a, b):
        return lax.dot_general(a, b, (((1,), (1,)), ((), ())), preferred_element_type=F32)

    def kernel(
        pattern_ref, back_ref, one_ref, two_ref, lead_ref, *refs
    ):
        terms = [refs[: len(second) // 2], refs[len(second) // 2 : len(second)]]
        rows_one_ref, rows_two_ref, sums_ref, chosen, panels = refs[len(second) :]
        for i in range(count):
            part = pl.ds(i * block, block)
            rows_one_ref[:, part] = back_ref[i, 0]
            chosen[:, part] = back_ref[i, 1]
            panels[:, part] = back_ref[i, 2]
        for i in range(count):
            part = pl.ds(i * block, block)
            side, first = i * 2 // count, i % (count // 2) * block
            total = jnp.dot(lead_ref[...], chosen[:, part], preferred_element_type=F32)
            for ref in terms[side]:
                total = total + ref[:, first : first + block].astype(F32)
            rows_two_ref[:, part] = (-(total * pattern_ref[0, i].astype(F32))).astype(kind)
        sums_ref[0] = over(one_ref[...], rows_one_ref[...])
        sums_ref[1] = over(two_ref[...], chosen[...])
        sums_ref[2] = over(panels[...], chosen[...])
        sums_ref[3] = over(two_ref[...], rows_two_ref[...])

    return small_call(
        kernel,
        [((block, width), kind), ((block, width), kind), ((4, block, block), F32)],
        [pattern],
        [back, masked_one, masked_two, lead, *second],
        [pltpu.VMEM((block, width), kind), pltpu.VMEM((block, width), kind)],
    )


def finish_blocks(z, parts, own_diag, parent_diag, two_diag, lead):
    block = lead.shape[0]

    def kernel(z_ref, a, b, c, d, own_ref, parent_ref, two_ref, lead_ref, one_out, lead_out, two_out, sums):
        held = (a, b, c, d)
        for k in range(SIDE):

            @pl.when(z_ref[0] == k)
            def _():
                w = [held[(i - k) % SIDE][...].astype(F32) for i in range(SIDE)]
                sums[...] = (w[0] + w[1]) + (w[2] + w[3])

        one_out[...] = own_ref[...] - sums[0]
        lead_wide = lead_ref[...].astype(F32)
        found = -(
            sums[1]
            + jnp.dot(
                lead_wide,
                parent_ref[...] - sums[2],
                precision=lax.Precision.HIGHEST,
                preferred_element_type=F32,
            )
        )
        lead_out[...] = found
        two_out[...] = (
            two_ref[...]
            - sums[3]
            - lax.dot_general(
                lead_wide,
                found,
                (((1,), (1,)), ((), ())),
                precision=lax.Precision.HIGHEST,
                preferred_element_type=F32,
            )
        )

    return small_call(
        kernel,
        [((block, block), F32)] * 3,
        [z],
        [*parts, own_diag, parent_diag, two_diag, lead],
        [pltpu.VMEM((4, block, block), F32)],
    )


def per_device(
    ancestor_inverse,
    level_one_panels,
    level_one_pattern,
    level_one_diag,
    level_two_panels,
    level_two_pattern,
    parent_lead,
    level_two_diag,
    parents,
):
    block = level_one_diag.shape[1]
    bf16 = jnp.bfloat16
    col = lax.axis_index("col")
    x, y = col % SIDE, col // SIDE
    count = SIDE * SIDE
    span, width = ancestor_inverse.shape
    masked_one = apply_pattern(level_one_panels, level_one_pattern, block)
    masked_two = apply_pattern(level_two_panels, level_two_pattern, block)

    found_one = all_panels(in_order([turned_panels(masked_one, k) for k in range(2)]))
    later_two, found_one = lax.optimization_barrier((masked_two, found_one))
    own_two = in_order([turned_panels(later_two, k) for k in range(2)])
    product_one = by_column(found_one, ancestor_inverse, block)
    first_sum = lax.psum_scatter(
        product_one.reshape(count * count * block, block), "col", scatter_dimension=0, tiled=True
    ).reshape(count, block, block)

    steps = jnp.arange(count, dtype=jnp.int32)
    place = arrival(steps)
    outer, inner = steps // SIDE, steps % SIDE
    x_major = (y + inner) % SIDE * SIDE + (x + outer) % SIDE
    y_major = (y + outer) % SIDE * SIDE + (x + inner) % SIDE

    rows_two = jnp.concatenate(all_panels(own_two), 0)

    def ring(order, part, step):
        order = place[order].reshape(SIDE, -1)
        low, high = by_supernode(order[2], rows_two, ancestor_inverse, part, True)
        arriving = send(low[0], step(1)), send(high[0], step(-1))
        rest, low = lax.optimization_barrier((jnp.concatenate([order[1], order[3], order[0]]), low))
        return arriving, by_supernode(rest, rows_two, ancestor_inverse, part, False)[0]

    first_a, near_a = ring(x_major, 0, x_step)
    first_b, near_b = ring(y_major, 1, y_step)
    second_a = second_sends(first_a, near_a, x_step)
    second_b = second_sends(first_b, near_b, y_step)

    later_one, _ = lax.optimization_barrier((masked_one, rows_two))
    facts = jnp.concatenate(
        [
            jnp.broadcast_to(level_one_pattern.reshape(count, 1, 1), (count, 8, block)),
            jnp.broadcast_to(parents.reshape(1, 1, 1), (count, 8, block)),
        ],
        1,
    ).astype(bf16)
    cut = jnp.swapaxes(later_one.reshape(block, count, block), 0, 1)
    cut = lax.all_to_all(jnp.concatenate([cut, facts], 1), "col", 0, 0, tiled=True)
    cut_pattern = cut[:, block, 0].astype(jnp.int32)
    readers = cut[:, block + 8, 0].astype(jnp.int32)
    going = outgoing(place, readers, cut_pattern, first_sum, cut)
    back = lax.all_to_all(going, "col", 0, 0, tiled=True)
    second_a, second_b, _ = lax.optimization_barrier((second_a, second_b, going))
    second_sum = third_sends(second_a, near_a, y_step) + third_sends(second_b, near_b, x_step)
    level_one_rows, level_two_rows, sums = finish_rows(
        level_two_pattern, back, masked_one, masked_two, parent_lead, second_sum
    )

    diag_blocks = level_one_diag.reshape(count, block, block)
    level_one_inv, level_two_lead, level_two_inv = finish_blocks(
        (lax.axis_index("row") // CORES).reshape(1),
        row_parts(sums),
        lax.dynamic_index_in_dim(diag_blocks, col, 0, keepdims=False),
        lax.dynamic_index_in_dim(diag_blocks, parents[0], 0, keepdims=False),
        level_two_diag,
        parent_lead,
    )
    return level_one_rows, level_one_inv, level_two_rows, level_two_lead, level_two_inv


def solution(mesh):
    in_specs = (
        P("col", "row"),
        P("col", "row"),
        P("col", "row"),
        P(),
        P("col", "row"),
        P("col", "row"),
        P("col", None),
        P("col", None),
        P("col"),
    )
    out_specs = (P("col", "row"), P("col", None), P("col", "row"), P("col", None), P("col", None))
    return jax.shard_map(
        per_device, mesh=mesh, in_specs=in_specs, out_specs=out_specs, check_vma=False
    )
```
